32 devices in a mesh: pos: 8 (over z, x), pix: 4 (over y, core).
Axes of the slice: x: 2, y: 2, z: 4, core: 2. Of those that a mesh axis runs over, the one named last changes fastest.
Arguments:
- probes: float32 [4096, 32768], P('pos', 'pix'), may hold values from -1000 to 1000, as said below
- sketch: float32 [32768, 48], P('pix'), may hold values from -0.03125 to 0.03125
Outputs:
- projection: float32 [48, 32768], P(None, 'pix')
The draws below stay inside these ranges and needn't reach their ends.
Inputs may be any that keep to these rules, and one draw needn't show every extreme that they name: `probes`: real values of varying scale per position and per column.
All inputs are finite; a program needn't handle non-finite values.
Results may differ from the reference program's by a relative error of at most 0.000075.
Values sent between devices are 32-bit elements; how exact they have to be, the bound alone decides.
No kernel may reach another device: no remote copies, remote signals or barrier semaphores. Data moves between devices by JAX's collectives and lax.ppermute only.
A program may use at most 64 MiB of HBM per device.

```python
import math
import jax
import jax.numpy as jnp
from jax import lax

RANK = 48
COLS = 32768
POSITIONS = 4096


def draw_probes(key, part):
    key = jax.random.fold_in(key, 7)
    first, second, third = jax.random.split(key, 3)
    ramp = jnp.arange(POSITIONS, dtype=jnp.float32)[:, None] / float(POSITIONS - 1)
    base = jnp.clip(jax.random.normal(first, (POSITIONS, COLS), jnp.float32), -6.0, 6.0)
    scales = jnp.exp(jax.random.uniform(second, (POSITIONS, 1), jnp.float32, 0.0, math.log(10.0)))
    scales = scales * (1.0 + 2.0 * ramp)
    widths = jnp.exp(jax.random.uniform(third, (1, COLS), jnp.float32, 0.0, math.log(3.0)))
    return (base * scales * widths).astype(jnp.float32)


def shard_levels(key, dims, pieces, smallest, largest):
    level, own = 1.0, jax.random.fold_in(key, 6)
    for dim, blocks in pieces:
        steps = jnp.exp(jax.random.uniform(jax.random.fold_in(own, dim), (blocks,), jnp.float32, smallest / len(pieces), largest / len(pieces)))
        level = level * jnp.repeat(steps, dims[dim] // blocks).reshape([-1 if axis == dim else 1 for axis in range(len(dims))])
    return level


def gaussian(stream_key, extent, deviation, limit, shards=(), held_as=jnp.bfloat16):
    drawn = deviation * jax.random.normal(stream_key, extent, jnp.float32)
    if shards:
        drawn = drawn * shard_levels(stream_key, extent, shards, -0.22, 0.18)
    return jnp.clip(drawn, -limit, limit).astype(held_as)


def setup_inputs(seed: int = 0) -> dict:
    key_list = jax.random.split(jax.random.key(seed), 3)
    return {
        "probes": draw_probes(jax.random.fold_in(key_list[2], 71), 0),
        "sketch": gaussian(key_list[1], (COLS, RANK), COLS ** -0.5, 0.03125, ((0, 4),), jnp.float32),
    }


def reference(probes, sketch):
    tall = jnp.dot(probes.astype(jnp.float32), sketch.astype(jnp.float32), precision=lax.Precision.HIGHEST, preferred_element_type=jnp.float32)
    gram = jnp.dot(tall.T.astype(jnp.float32), tall.astype(jnp.float32), precision=lax.Precision.HIGHEST, preferred_element_type=jnp.float32)
    lower = jnp.linalg.cholesky(gram)
    basis = lax.linalg.triangular_solve(lower, tall.T, left_side=True, lower=True).T
    return jnp.dot(basis.T.astype(jnp.float32), probes.astype(jnp.float32), precision=lax.Precision.HIGHEST, preferred_element_type=jnp.float32)
```

```python
import functools

import jax
import jax.numpy as jnp
from jax import lax
from jax.experimental import pallas as pl
from jax.experimental.pallas import tpu as pltpu
from jax.sharding import PartitionSpec as P

F32 = jnp.float32
BF16 = jnp.bfloat16
VMEM_LIMIT = 40 * 1024 * 1024
LAST = (((1,), (1,)), ((), ()))
PLAIN = (((1,), (0,)), ((), ()))


def split(x):
    head = x.astype(BF16)
    return head, (x - head.astype(F32)).astype(BF16)


def dot(a, b, dims):
    return lax.dot_general(a, b, dims, preferred_element_type=F32)


def tall_kernel(x_ref, s_ref, out_ref, acc_ref):
    step = pl.program_id(0)
    rank = s_ref.shape[0]

    @pl.when(step == 0)
    def _():
        acc_ref[...] = jnp.zeros_like(acc_ref)

    s_both = jnp.concatenate(split(s_ref[...]), axis=0)
    x_head, x_rest = split(x_ref[...])
    acc_ref[...] += dot(x_head, s_both, LAST) + dot(x_rest, s_both, LAST)

    @pl.when(step == pl.num_programs(0) - 1)
    def _():
        acc = acc_ref[...].T
        out_ref[...] = acc[:rank] + acc[rank:]


def tall_partial(probes, sketch_t):
    rows, cols = probes.shape
    rank = sketch_t.shape[0]
    width = min(1024, cols)
    return pl.pallas_call(
        tall_kernel,
        grid=(cols // width,),
        in_specs=[
            pl.BlockSpec((rows, width), lambda i: (0, i)),
            pl.BlockSpec((rank, width), lambda i: (0, i)),
        ],
        out_specs=pl.BlockSpec((rank, rows), lambda i: (0, 0)),
        out_shape=jax.ShapeDtypeStruct((rank, rows), F32),
        scratch_shapes=[pltpu.VMEM((rows, 2 * rank), F32)],
        compiler_params=pltpu.CompilerParams(vmem_limit_bytes=VMEM_LIMIT),
        cost_estimate=pl.CostEstimate(
            flops=4 * rows * cols * rank * 2, bytes_accessed=4 * rows * cols, transcendentals=0
        ),
        name="tall_partial",
    )(probes, sketch_t)


def prepare_kernel(*refs):
    parts, (both_ref, gram_ref) = refs[:-2], refs[-2:]
    tall = parts[0][...]
    for part in parts[1:]:
        tall = tall + part[...]
    rank = tall.shape[0]
    head, rest = split(tall)
    tail = (tall - head.astype(F32) - rest.astype(F32)).astype(BF16)
    both_ref[...] = jnp.concatenate([head, rest], axis=0)
    three = jnp.concatenate([head, rest, tail], axis=0)
    g = dot(three, three, LAST)
    r = rank
    big = g[:r, :r]
    cross = g[:r, r : 2 * r] + g[r : 2 * r, :r]
    small = g[:r, 2 * r :] + g[2 * r :, :r] + g[r : 2 * r, r : 2 * r]
    gram_ref[...] = big + (cross + small)


def prepare(parts):
    rank, rows = parts[0].shape
    whole = pl.BlockSpec(memory_space=pltpu.VMEM)
    return pl.pallas_call(
        prepare_kernel,
        in_specs=[whole] * len(parts),
        out_specs=[whole, whole],
        out_shape=[
            jax.ShapeDtypeStruct((2 * rank, rows), BF16),
            jax.ShapeDtypeStruct((rank, rank), F32),
        ],
        compiler_params=pltpu.CompilerParams(vmem_limit_bytes=VMEM_LIMIT),
        cost_estimate=pl.CostEstimate(
            flops=rows * rank * rank * 18, bytes_accessed=24 * rank * rows, transcendentals=0
        ),
        name="prepare",
    )(*parts)


def block_kernel(which_ref, both_ref, x_ref, out_ref):
    rank = out_ref.shape[0]
    both = both_ref[...]
    x_head, x_rest = split(x_ref[...])
    first = dot(both, x_head, PLAIN)
    second = dot(both[:rank], x_rest, PLAIN)
    out_ref[...] = first[:rank] + (first[rank:] + second)


def block_product(which, both, probes, blocks):
    rows, cols = probes.shape
    rank = both.shape[0] // 2
    width = cols // blocks
    sub = min(512, width)
    steps = width // sub
    return pl.pallas_call(
        block_kernel,
        grid_spec=pltpu.PrefetchScalarGridSpec(
            num_scalar_prefetch=1,
            grid=(steps,),
            in_specs=[
                pl.BlockSpec((2 * rank, rows), lambda i, w: (0, 0)),
                pl.BlockSpec((rows, sub), lambda i, w: (0, w[0] * steps + i)),
            ],
            out_specs=pl.BlockSpec((rank, sub), lambda i, w: (0, i)),
        ),
        out_shape=jax.ShapeDtypeStruct((rank, width), F32),
        compiler_params=pltpu.CompilerParams(vmem_limit_bytes=VMEM_LIMIT),
        cost_estimate=pl.CostEstimate(
            flops=6 * rows * width * rank, bytes_accessed=4 * rows * width, transcendentals=0
        ),
        name="block_product",
    )(which, both, probes)


def place_kernel(count, where_ref, *refs):
    parts, (out_ref, sems) = refs[:count], refs[count:]
    width = parts[0].shape[1]
    copies = []
    for r in range(count):
        start = pl.multiple_of(where_ref[r] * width, width)
        copies.append(
            pltpu.make_async_copy(parts[r], out_ref.at[:, pl.ds(start, width)], sems.at[r])
        )
    for copy in copies:
        copy.start()
    for copy in copies:
        copy.wait()


def place(where, parts):
    rank, width = parts[0].shape
    count = len(parts)
    anywhere = pl.BlockSpec(memory_space=pl.ANY)
    return pl.pallas_call(
        functools.partial(place_kernel, count),
        in_specs=[pl.BlockSpec(memory_space=pltpu.SMEM)] + [anywhere] * count,
        out_specs=anywhere,
        out_shape=jax.ShapeDtypeStruct((rank, width * count), F32),
        scratch_shapes=[pltpu.SemaphoreType.DMA((count,))],
        cost_estimate=pl.CostEstimate(
            flops=0, bytes_accessed=8 * rank * width * count, transcendentals=0
        ),
        name="place",
    )(where, *parts)


def body(n_pos, n_pix, probes, sketch):
    def swap(value, axis, size, bit):
        return lax.ppermute(value, axis, [(i, i ^ bit) for i in range(size)])

    me = lax.axis_index("pos").astype(jnp.int32)
    rank = sketch.shape[1]

    own = tall_partial(probes, sketch.T)
    parts = [own] + [swap(own, "pix", n_pix, r) for r in range(1, n_pix)]
    both, gram_part = prepare(parts)

    grams = [gram_part] + [swap(gram_part, "pos", n_pos, r) for r in range(1, n_pos)]

    def product(r):
        return block_product((me ^ r)[None], both, probes, n_pos)

    even = list(range(0, n_pos, 2))
    received = {}
    for s in even[::-1]:
        received[s] = swap(product(s ^ 1), "pos", n_pos, 1)
    pairs = {s: product(s) + received[s] for s in even[::-1]}

    arrived = [swap(pairs[s], "pos", n_pos, s) for s in even[1:][::-1]]

    gram = functools.reduce(jnp.add, grams)
    lower = jnp.linalg.cholesky(gram)
    inverse = lax.linalg.triangular_solve(
        lower, jnp.eye(rank, dtype=F32), left_side=True, lower=True
    )

    mine = functools.reduce(jnp.add, arrived, pairs[0])
    final = jnp.dot(inverse, mine, precision=lax.Precision.HIGHEST, preferred_element_type=F32)

    pieces = {0: final}
    for s in even[1:]:
        pieces[s] = swap(final, "pos", n_pos, s)
    for s in even:
        pieces[s ^ 1] = swap(pieces[s], "pos", n_pos, 1)

    where = me ^ jnp.arange(n_pos, dtype=jnp.int32)
    return place(where, [pieces[r] for r in range(n_pos)])


def solution(mesh):
    in_specs = (P("pos", "pix"), P("pix", None))
    out_specs = P(None, "pix")
    run = functools.partial(body, mesh.shape["pos"], mesh.shape["pix"])
    return jax.shard_map(run, mesh=mesh, in_specs=in_specs, out_specs=out_specs, check_vma=False)
```

```python
import functools

import jax
import jax.numpy as jnp
from jax import lax
from jax.experimental import pallas as pl
from jax.experimental.pallas import tpu as pltpu
from jax.sharding import PartitionSpec as P

F32 = jnp.float32
BF16 = jnp.bfloat16
VMEM_LIMIT = 40 * 1024 * 1024
LANES = 128
CHUNKS = 4
LAST = (((1,), (1,)), ((), ()))
PLAIN = (((1,), (0,)), ((), ()))
ANYWHERE = pl.BlockSpec(memory_space=pl.ANY)
PARAMS = pltpu.CompilerParams(vmem_limit_bytes=VMEM_LIMIT)


def split(x):
    head = x.astype(BF16)
    return head, (x - head.astype(F32)).astype(BF16)


def dot(a, b, dims):
    return lax.dot_general(a, b, dims, preferred_element_type=F32)


def tall_kernel(x_ref, s_ref, out_ref, acc_ref):
    step = pl.program_id(0)
    rank = s_ref.shape[0]

    @pl.when(step == 0)
    def _():
        acc_ref[...] = jnp.zeros_like(acc_ref)

    s_head, s_rest = split(s_ref[...])
    s_both = jnp.concatenate([s_head, s_rest], axis=0)
    x_head, x_rest = split(x_ref[...])
    both = dot(s_both, x_head, LAST)
    acc_ref[...] += both[:rank] + (both[rank:] + dot(s_head, x_rest, LAST))

    @pl.when(step == pl.num_programs(0) - 1)
    def _():
        out_ref[...] = acc_ref[...]


def tall_partial(probes, sketch_t):
    rows, cols = probes.shape
    rank = sketch_t.shape[0]
    width = min(1024, cols)
    return pl.pallas_call(
        tall_kernel,
        grid=(cols // width,),
        in_specs=[
            pl.BlockSpec((rows, width), lambda i: (0, i)),
            pl.BlockSpec((rank, width), lambda i: (0, i)),
        ],
        out_specs=pl.BlockSpec((rank, rows), lambda i: (0, 0)),
        out_shape=jax.ShapeDtypeStruct((rank, rows), F32),
        scratch_shapes=[pltpu.VMEM((rank, rows), F32)],
        compiler_params=PARAMS,
        cost_estimate=pl.CostEstimate(
            flops=6 * rows * cols * rank, bytes_accessed=4 * rows * cols, transcendentals=0
        ),
        name="tall_partial",
    )(probes, sketch_t)


def prepare_kernel(first_ref, second_ref, both_ref, gram_ref):
    tall = first_ref[...] + second_ref[...]
    rank = tall.shape[0]
    head, rest = split(tall)
    tail = (tall - head.astype(F32) - rest.astype(F32)).astype(BF16)
    both_ref[...] = jnp.concatenate([head, rest], axis=0)
    three = jnp.concatenate([head, rest, tail], axis=0)
    g = dot(three, three, LAST)
    r = rank
    big = g[:r, :r]
    cross = g[:r, r : 2 * r] + g[r : 2 * r, :r]
    small = g[:r, 2 * r :] + g[2 * r :, :r] + g[r : 2 * r, r : 2 * r]
    gram = big + (cross + small)
    gram_ref[...] = jnp.concatenate([gram, jnp.zeros((r, LANES - r), F32)], axis=1)


def prepare(first, second):
    rank, rows = first.shape
    whole = pl.BlockSpec(memory_space=pltpu.VMEM)
    return pl.pallas_call(
        prepare_kernel,
        in_specs=[whole, whole],
        out_specs=[whole, whole],
        out_shape=[
            jax.ShapeDtypeStruct((2 * rank, rows), BF16),
            jax.ShapeDtypeStruct((rank, LANES), F32),
        ],
        compiler_params=PARAMS,
        cost_estimate=pl.CostEstimate(
            flops=rows * rank * rank * 18, bytes_accessed=24 * rank * rows, transcendentals=0
        ),
        name="prepare",
    )(first, second)


def block_kernel(has_gram, which_ref, both_ref, x_ref, *refs):
    out_ref = refs[-1]
    step = pl.program_id(0)
    rank = out_ref.shape[0]
    sub = x_ref.shape[1]
    both = both_ref[...]
    x_head, x_rest = split(x_ref[...])
    first = dot(both, x_head, PLAIN)
    second = dot(both[:rank], x_rest, PLAIN)
    where = pl.ds(pl.multiple_of(step * sub, sub), sub)
    out_ref[:, where] = first[:rank] + (first[rank:] + second)
    if has_gram:

        @pl.when(step == 0)
        def _():
            out_ref[:, out_ref.shape[1] - LANES :] = refs[0][...]


def block_product(which, both, probes, width, gram=None, after=None):
    rows = probes.shape[0]
    rank = both.shape[0] // 2
    sub = min(512, width)
    steps = width // sub
    in_specs = [
        pl.BlockSpec((2 * rank, rows), lambda i, w: (0, 0)),
        pl.BlockSpec((rows, sub), lambda i, w: (0, w[0] * steps + i)),
    ]
    args = [both, probes]
    out_width = width
    if gram is not None:
        in_specs.append(pl.BlockSpec((rank, LANES), lambda i, w: (0, 0)))
        args.append(gram)
        out_width += LANES
    if after is not None:
        in_specs.append(ANYWHERE)
        args.append(after)
    return pl.pallas_call(
        functools.partial(block_kernel, gram is not None),
        grid_spec=pltpu.PrefetchScalarGridSpec(
            num_scalar_prefetch=1,
            grid=(steps,),
            in_specs=in_specs,
            out_specs=pl.BlockSpec((rank, out_width), lambda i, w: (0, 0)),
        ),
        out_shape=jax.ShapeDtypeStruct((rank, out_width), F32),
        compiler_params=PARAMS,
        cost_estimate=pl.CostEstimate(
            flops=6 * rows * width * rank, bytes_accessed=4 * rows * width, transcendentals=0
        ),
        name="block_product",
    )(which, *args)


def inverse_kernel(gram_ref, out_ref):
    rank = out_ref.shape[0]
    rows = lax.broadcasted_iota(jnp.int32, (rank, LANES), 0)
    cols = lax.broadcasted_iota(jnp.int32, (rank, LANES), 1)
    work = jnp.where(cols < rank, gram_ref[...], (cols == rows + rank).astype(F32))
    for k in range(rank):
        pivot = work[k : k + 1, :]
        scale = 1.0 / jnp.sqrt(work[k : k + 1, k : k + 1])
        row = pivot * scale
        column = jnp.where(rows[:, :1] > k, work[:, k : k + 1] * scale, 0.0)
        work = jnp.where(rows == k, row, work - column * row)
    out_ref[...] = work[:, rank : 2 * rank]


def inverse_factor(chunk):
    rank, width = chunk.shape
    last = width // LANES - 1
    return pl.pallas_call(
        inverse_kernel,
        grid=(1,),
        in_specs=[pl.BlockSpec((rank, LANES), lambda i: (0, last))],
        out_specs=pl.BlockSpec((rank, rank), lambda i: (0, 0)),
        out_shape=jax.ShapeDtypeStruct((rank, rank), F32),
        compiler_params=PARAMS,
        cost_estimate=pl.CostEstimate(
            flops=20_000_000, bytes_accessed=8 * rank * LANES, transcendentals=rank
        ),
        name="inverse_factor",
    )(chunk)


def finish_kernel(count, where_ref, inverse_ref, *refs):
    parts, out_ref = refs[:count], refs[-1]
    step = pl.program_id(0)
    rank, width = out_ref.shape
    head, rest = split(inverse_ref[...])
    both = jnp.concatenate([head, rest], axis=0)
    for k in range(count):

        @pl.when(step == k)
        def _():
            p_head, p_rest = split(parts[k][:, :width])
            first = dot(both, p_head, PLAIN)
            out_ref[...] = first[:rank] + (first[rank:] + dot(head, p_rest, PLAIN))


def finish(where, inverse, parts, width, total, before=None):
    rank = inverse.shape[0]
    count = len(parts)
    in_specs = [pl.BlockSpec((rank, rank), lambda i, w: (0, 0))]
    in_specs += [pl.BlockSpec(part.shape, lambda i, w: (0, 0)) for part in parts]
    args = [inverse, *parts]
    aliases = {}
    if before is not None:
        in_specs.append(ANYWHERE)
        args.append(before)
        aliases = {len(args): 0}
    return pl.pallas_call(
        functools.partial(finish_kernel, count),
        grid_spec=pltpu.PrefetchScalarGridSpec(
            num_scalar_prefetch=1,
            grid=(count,),
            in_specs=in_specs,
            out_specs=pl.BlockSpec((rank, width), lambda i, w: (0, w[i])),
        ),
        out_shape=jax.ShapeDtypeStruct((rank, total), F32),
        input_output_aliases=aliases,
        compiler_params=PARAMS,
        cost_estimate=pl.CostEstimate(
            flops=6 * rank * rank * width * count,
            bytes_accessed=8 * rank * width * count,
            transcendentals=0,
        ),
        name="finish",
    )(where, *args)


def body(n_pos, n_pix, probes, sketch):
    def swap(value, axis, size, bit):
        return lax.ppermute(value, axis, [(i, i ^ bit) for i in range(size)])

    me = lax.axis_index("pos").astype(jnp.int32)
    side, outer = me % 2, me // 2
    n_outer = n_pos // 2
    cols = probes.shape[1]
    width = cols // 2 // CHUNKS

    def send_outer(value, pairs):
        return lax.ppermute(
            value, "pos", [(2 * a + s, 2 * b + s) for a, b in pairs for s in range(2)]
        )

    def outer_sum(value):
        if n_outer != 4:
            bit = 2
            while bit < n_pos:
                value = value + swap(value, "pos", n_pos, bit)
                bit *= 2
            return value
        value = value + send_outer(value, [(0, 1), (3, 2)])
        value = value + send_outer(value, [(1, 2), (2, 1)])
        back = send_outer(value, [(1, 0), (2, 3)])
        inner = (outer == 1) | (outer == 2)
        return jnp.where(inner, value, back)

    tall = tall_partial(probes, sketch.T)
    bit = 1
    while 2 * bit < n_pix:
        tall = tall + swap(tall, "pix", n_pix, bit)
        bit *= 2
    both, gram = prepare(tall, swap(tall, "pix", n_pix, bit))

    def product(half, i, after):
        which = (half * CHUNKS + i)[None]
        return block_product(which, both, probes, width, gram if i == 0 else None, after)

    received, sums = [], []
    for i in range(CHUNKS):
        away = product(1 - side, i, received[i - 2] if i >= 2 else None)
        received.append(swap(away, "pos", n_pos, 1))
    for i in range(CHUNKS):
        sums.append(outer_sum(product(side, i, None) + received[i]))

    inverse = inverse_factor(sums[0])
    sums[0] = sums[0][:, :width]
    others = [swap(part, "pos", n_pos, 1) for part in sums]

    slots = jnp.stack([side * CHUNKS, (1 - side) * CHUNKS])
    early = [i for i in range(CHUNKS - 1) for _ in range(2)]
    where = jnp.stack([slots[k % 2] + i for k, i in enumerate(early)])
    parts = [part for i in range(CHUNKS - 1) for part in (sums[i], others[i])]
    out = finish(where, inverse, parts, width, cols)
    return finish(slots + (CHUNKS - 1), inverse, [sums[-1], others[-1]], width, cols, out)


def solution(mesh):
    in_specs = (P("pos", "pix"), P("pix", None))
    out_specs = P(None, "pix")
    run = functools.partial(body, mesh.shape["pos"], mesh.shape["pix"])
    return jax.shard_map(run, mesh=mesh, in_specs=in_specs, out_specs=out_specs, check_vma=False)
```

```python
import functools

import jax
import jax.numpy as jnp
from jax import lax
from jax.experimental import pallas as pl
from jax.experimental.pallas import tpu as pltpu
from jax.sharding import PartitionSpec as P

F32 = jnp.float32
BF16 = jnp.bfloat16
VMEM_LIMIT = 40 * 1024 * 1024
LANES = 128
CHUNKS = 1
STREAMS = 4
PANEL = 4
LAST = (((1,), (1,)), ((), ()))
PLAIN = (((1,), (0,)), ((), ()))
ANYWHERE = pl.BlockSpec(memory_space=pl.ANY)
PARAMS = pltpu.CompilerParams(vmem_limit_bytes=VMEM_LIMIT)


def split(x):
    head = x.astype(BF16)
    return head, (x - head.astype(F32)).astype(BF16)


def dot(a, b, dims):
    return lax.dot_general(a, b, dims, preferred_element_type=F32)


def row_blocks(rows):
    return STREAMS if rows % (16 * STREAMS) == 0 else 1


def tall_kernel(s_ref, *refs):
    x_refs, (out_ref, acc_ref) = refs[:-2], refs[-2:]
    step = pl.program_id(0)
    rank = s_ref.shape[0]

    @pl.when(step == 0)
    def _():
        acc_ref[...] = jnp.zeros_like(acc_ref)

    s_head, s_rest = split(s_ref[...])
    s_both = jnp.concatenate([s_head, s_rest], axis=0)
    x_head, x_rest = split(jnp.concatenate([ref[...] for ref in x_refs], axis=0))
    both = dot(s_both, x_head, LAST)
    acc_ref[...] += both[:rank] + (both[rank:] + dot(s_head, x_rest, LAST))

    @pl.when(step == pl.num_programs(0) - 1)
    def _():
        out_ref[...] = acc_ref[...]


def tall_partial(probes, sketch_t):
    rows, cols = probes.shape
    rank = sketch_t.shape[0]
    width = min(1024, cols)
    streams = row_blocks(rows)
    sketch_t = pltpu.with_memory_space_constraint(sketch_t, pltpu.MemorySpace.HBM)
    x_specs = [
        pl.BlockSpec((rows // streams, width), lambda i, q=q: (q, i)) for q in range(streams)
    ]
    return pl.pallas_call(
        tall_kernel,
        grid=(cols // width,),
        in_specs=[pl.BlockSpec((rank, width), lambda i: (0, i)), *x_specs],
        out_specs=pl.BlockSpec((rank, rows), lambda i: (0, 0)),
        out_shape=jax.ShapeDtypeStruct((rank, rows), F32),
        scratch_shapes=[pltpu.VMEM((rank, rows), F32)],
        compiler_params=PARAMS,
        cost_estimate=pl.CostEstimate(
            flops=6 * rows * cols * rank, bytes_accessed=4 * rows * cols, transcendentals=0
        ),
        name="tall_partial",
    )(sketch_t, *[probes] * streams)


def prepare_kernel(first_ref, second_ref, both_ref, gram_ref):
    tall = first_ref[...] + second_ref[...]
    rank = tall.shape[0]
    head, rest = split(tall)
    tail = (tall - head.astype(F32) - rest.astype(F32)).astype(BF16)
    both_ref[...] = jnp.concatenate([head, rest], axis=0)
    three = jnp.concatenate([head, rest, tail], axis=0)
    g = dot(three, three, LAST)
    r = rank
    big = g[:r, :r]
    cross = g[:r, r : 2 * r] + g[r : 2 * r, :r]
    small = g[:r, 2 * r :] + g[2 * r :, :r] + g[r : 2 * r, r : 2 * r]
    gram = big + (cross + small)
    gram_ref[...] = jnp.concatenate([gram, jnp.zeros((r, LANES - r), F32)], axis=1)


def prepare(first, second):
    rank, rows = first.shape
    whole = pl.BlockSpec(memory_space=pltpu.VMEM)
    return pl.pallas_call(
        prepare_kernel,
        in_specs=[whole, whole],
        out_specs=[whole, whole],
        out_shape=[
            jax.ShapeDtypeStruct((2 * rank, rows), BF16),
            jax.ShapeDtypeStruct((rank, LANES), F32),
        ],
        compiler_params=PARAMS,
        cost_estimate=pl.CostEstimate(
            flops=rows * rank * rank * 18, bytes_accessed=24 * rank * rows, transcendentals=0
        ),
        name="prepare",
    )(first, second)


def product_kernel(streams, plan, grams, which_ref, both_ref, gram_ref, *refs):
    count = 1 + max(out for out, _ in plan)
    x_refs, outs = refs[:streams], refs[len(refs) - count :]
    step = pl.program_id(0)
    rank = outs[0].shape[0]
    sub = x_refs[0].shape[1]
    both = both_ref[...]
    x_head, x_rest = split(jnp.concatenate([ref[...] for ref in x_refs], axis=0))
    first = dot(both, x_head, PLAIN)
    second = dot(both[:rank], x_rest, PLAIN)
    result = first[:rank] + (first[rank:] + second)
    for k, (out, offset) in enumerate(plan):

        @pl.when(step == k)
        def _():
            outs[out][:, offset : offset + sub] = result

    @pl.when(step == 0)
    def _():
        for out, offset in grams:
            outs[out][:, offset : offset + LANES] = gram_ref[...]


def products(both, gram, probes, sub, outputs, after=()):
    rows = probes.shape[0]
    rank = both.shape[0] // 2
    streams = row_blocks(rows)
    plan, grams, widths, which = [], [], [], []
    for out, (blocks, with_gram) in enumerate(outputs):
        extra = LANES if with_gram else 0
        for j, block in enumerate(blocks):
            plan.append((out, j * sub + (extra if j else 0)))
            which.append(block)
        if with_gram:
            grams.append((out, sub))
        widths.append(len(blocks) * sub + extra)
    x_specs = [
        pl.BlockSpec((rows // streams, sub), lambda i, w, q=q: (q, w[i])) for q in range(streams)
    ]
    return pl.pallas_call(
        functools.partial(product_kernel, streams, plan, grams),
        grid_spec=pltpu.PrefetchScalarGridSpec(
            num_scalar_prefetch=1,
            grid=(len(plan),),
            in_specs=[
                pl.BlockSpec((2 * rank, rows), lambda i, w: (0, 0)),
                pl.BlockSpec((rank, LANES), lambda i, w: (0, 0)),
                *x_specs,
                *[ANYWHERE] * len(after),
            ],
            out_specs=[pl.BlockSpec((rank, width), lambda i, w: (0, 0)) for width in widths],
        ),
        out_shape=[jax.ShapeDtypeStruct((rank, width), F32) for width in widths],
        compiler_params=PARAMS,
        cost_estimate=pl.CostEstimate(
            flops=6 * rows * rank * sub * len(plan),
            bytes_accessed=4 * rows * sub * len(plan),
            transcendentals=0,
        ),
        name="products",
    )(jnp.stack(which), both, gram, *[probes] * streams, *after)


def inverse_kernel(gram_ref, out_ref):
    rank = out_ref.shape[0]
    rows = lax.broadcasted_iota(jnp.int32, (rank, LANES), 0)
    cols = lax.broadcasted_iota(jnp.int32, (rank, LANES), 1)
    work = jnp.where(cols < rank, gram_ref[...], (cols == rows + rank).astype(F32))
    scale = jnp.ones((rank, LANES), F32)
    for start in range(0, rank, PANEL):
        panel = [
            jnp.broadcast_to(work[:, k : k + 1], (rank, LANES))
            for k in range(start, start + PANEL)
        ]
        for j in range(PANEL):
            k = start + j
            over = 1.0 / panel[j][k : k + 1, :]
            scale = jnp.where(rows == k, over, scale)
            factor = jnp.where(rows > k, panel[j] * over, 0.0)
            work = work - factor * work[k : k + 1, :]
            for later in range(j + 1, PANEL):
                panel[later] = panel[later] - factor * panel[later][k : k + 1, :]
    out_ref[...] = (work * jnp.sqrt(scale))[:, rank : 2 * rank]


def inverse_factor(chunk, start):
    rank = chunk.shape[0]
    return pl.pallas_call(
        inverse_kernel,
        grid=(1,),
        in_specs=[pl.BlockSpec((rank, LANES), lambda i: (0, start // LANES))],
        out_specs=pl.BlockSpec((rank, rank), lambda i: (0, 0)),
        out_shape=jax.ShapeDtypeStruct((rank, rank), F32),
        compiler_params=PARAMS,
        cost_estimate=pl.CostEstimate(
            flops=20_000_000, bytes_accessed=8 * rank * LANES, transcendentals=rank
        ),
        name="inverse_factor",
    )(chunk)


def finish_kernel(plan, where_ref, inverse_ref, *refs):
    out_ref = refs[-1]
    step = pl.program_id(0)
    rank, width = out_ref.shape
    head, rest = split(inverse_ref[...])
    both = jnp.concatenate([head, rest], axis=0)
    for k, (source, offset) in enumerate(plan):

        @pl.when(step == k)
        def _():
            p_head, p_rest = split(refs[source][:, offset : offset + width])
            first = dot(both, p_head, PLAIN)
            out_ref[...] = first[:rank] + (first[rank:] + dot(head, p_rest, PLAIN))


def finish(inverse, sources, pieces, width, total, before=None):
    rank = inverse.shape[0]
    count = len(pieces)
    in_specs = [pl.BlockSpec((rank, rank), lambda i, w: (0, 0))]
    in_specs += [pl.BlockSpec(source.shape, lambda i, w: (0, 0)) for source in sources]
    args = [inverse, *sources]
    aliases = {}
    if before is not None:
        in_specs.append(ANYWHERE)
        args.append(before)
        aliases = {len(args): 0}
    return pl.pallas_call(
        functools.partial(finish_kernel, [piece[1:] for piece in pieces]),
        grid_spec=pltpu.PrefetchScalarGridSpec(
            num_scalar_prefetch=1,
            grid=(count,),
            in_specs=in_specs,
            out_specs=pl.BlockSpec((rank, width), lambda i, w: (0, w[i])),
        ),
        out_shape=jax.ShapeDtypeStruct((rank, total), F32),
        input_output_aliases=aliases,
        compiler_params=PARAMS,
        cost_estimate=pl.CostEstimate(
            flops=6 * rank * rank * width * count,
            bytes_accessed=8 * rank * width * count,
            transcendentals=0,
        ),
        name="finish",
    )(jnp.stack([piece[0] for piece in pieces]), *args)


def body(n_pos, n_pix, probes, sketch):
    def swap(value, axis, size, bit):
        return lax.ppermute(value, axis, [(i, i ^ bit) for i in range(size)])

    def over(value, bit):
        return swap(value, "pos", n_pos, bit)

    me = lax.axis_index("pos").astype(jnp.int32)
    near, far = me & 1, (me >> 1) & 1
    cols = probes.shape[1]
    width = cols // (8 * CHUNKS)

    tall = tall_partial(probes, sketch.T)
    bit = 1
    while 2 * bit < n_pix:
        tall = tall + swap(tall, "pix", n_pix, bit)
        bit *= 2
    both, gram = prepare(tall, swap(tall, "pix", n_pix, bit))

    def block_a(c, p, q):
        return 8 * c + 2 * (near ^ p) + (far ^ q)

    def block_b(c, p, q):
        return 8 * c + 4 + 2 * (far ^ p) + (near ^ q)

    def outputs(c, p):
        return [
            ([block_a(c, p, 1), block_a(c, p, 0)], c == 0),
            ([block_b(c, p, 1), block_b(c, p, 0)], False),
        ]

    first = products(both, gram, probes, width, outputs(0, 1))
    plan = [(c, p) for c in range(CHUNKS) for p in (1, 0) if (c, p) != (0, 1)]
    rest = products(
        both, gram, probes, width, [out for c, p in plan for out in outputs(c, p)], (first[0],)
    )
    made = {(0, 1): first}
    made.update({key: rest[2 * k : 2 * k + 2] for k, key in enumerate(plan)})

    inverse, out = None, None
    for c in range(CHUNKS):
        g = LANES if c == 0 else 0
        away_a, away_b = made[c, 1]
        own_a, own_b = made[c, 0]
        sum_a = own_a + over(away_a, 1)
        sum_b = own_b + over(away_b, 2)
        got_a = over(sum_a[:, : width + g], 2)
        got_b = over(sum_b[:, :width], 1)
        whole = jnp.concatenate(
            [
                sum_a[:, width + g :] + got_a[:, :width],
                sum_a[:, width : width + g] + got_a[:, width:],
                sum_b[:, width:] + got_b,
            ],
            axis=1,
        )
        bit = 4
        while bit < n_pos:
            whole = whole + over(whole, bit)
            bit *= 2
        if c == 0:
            inverse = inverse_factor(whole, width)
        mine_a, mine_b = whole[:, :width], whole[:, width + g :]
        next_a = over(mine_a, 2)
        next_b = over(mine_b, 1)
        last_a = over(jnp.concatenate([mine_a, next_a], axis=1), 1)
        last_b = over(jnp.concatenate([mine_b, next_b], axis=1), 2)
        out = finish(
            inverse,
            [whole, next_a, next_b],
            [
                (block_a(c, 0, 0), 0, 0),
                (block_b(c, 0, 0), 0, width + g),
                (block_a(c, 0, 1), 1, 0),
                (block_b(c, 0, 1), 2, 0),
            ],
            width,
            cols,
            out,
        )
        out = finish(
            inverse,
            [last_a, last_b],
            [
                (block_a(c, 1, 0), 0, 0),
                (block_a(c, 1, 1), 0, width),
                (block_b(c, 1, 0), 1, 0),
                (block_b(c, 1, 1), 1, width),
            ],
            width,
            cols,
            out,
        )
    return out


def solution(mesh):
    in_specs = (P("pos", "pix"), P("pix", None))
    out_specs = P(None, "pix")
    run = functools.partial(body, mesh.shape["pos"], mesh.shape["pix"])
    return jax.shard_map(run, mesh=mesh, in_specs=in_specs, out_specs=out_specs, check_vma=False)
```

```python
import functools

import jax
import jax.numpy as jnp
from jax import lax
from jax.experimental import pallas as pl
from jax.experimental.pallas import tpu as pltpu
from jax.sharding import PartitionSpec as P

F32 = jnp.float32
BF16 = jnp.bfloat16
VMEM_LIMIT = 30 * 1024 * 1024
LANES = 128
CHUNKS = 1
PANEL = 4
LAST = (((1,), (1,)), ((), ()))
PLAIN = (((1,), (0,)), ((), ()))
ANYWHERE = pl.BlockSpec(memory_space=pl.ANY)
WHOLE = pl.BlockSpec(memory_space=pltpu.VMEM)
PARAMS = pltpu.CompilerParams(vmem_limit_bytes=VMEM_LIMIT)


def split(x):
    head = x.astype(BF16)
    return head, (x - head.astype(F32)).astype(BF16)


def dot(a, b, dims):
    return lax.dot_general(a, b, dims, preferred_element_type=F32)


def tall_kernel(x_hbm, s_hbm, out_ref, head_ref, rest_ref, x_buf, s_buf, x_sems, s_sems):
    blocks, rows, width = x_buf.shape
    rank = s_hbm.shape[0]

    def copies(k):
        where = pl.ds(k * width, width)
        return (
            pltpu.make_async_copy(s_hbm.at[:, where], s_buf.at[k], s_sems.at[k]),
            pltpu.make_async_copy(x_hbm.at[:, where], x_buf.at[k], x_sems.at[k]),
        )

    for k in range(blocks):
        for copy in copies(k):
            copy.start()
    for k in range(blocks):
        for copy in copies(k):
            copy.wait()
        s_head, s_rest = split(s_buf[k])
        s_both = jnp.concatenate([s_head, s_rest], axis=0)
        x_head, x_rest = split(x_buf[k])
        head_ref[k] = x_head
        rest_ref[k] = x_rest
        both = dot(s_both, x_head, LAST)
        part = both[:rank] + (both[rank:] + dot(s_head, x_rest, LAST))
        if k == 0:
            out_ref[...] = part
        else:
            out_ref[...] += part


def tall_partial(probes, sketch_t, width):
    rows, cols = probes.shape
    rank = sketch_t.shape[0]
    blocks = cols // width
    hbm = pltpu.MemorySpace.HBM
    return pl.pallas_call(
        tall_kernel,
        in_specs=[pl.BlockSpec(memory_space=hbm)] * 2,
        out_specs=[WHOLE] * 3,
        out_shape=[
            jax.ShapeDtypeStruct((rank, rows), F32),
            pltpu.VMEM((blocks, rows, width), BF16),
            pltpu.VMEM((blocks, rows, width), BF16),
        ],
        scratch_shapes=[
            pltpu.VMEM((blocks, rows, width), F32),
            pltpu.VMEM((blocks, rank, width), F32),
            pltpu.SemaphoreType.DMA((blocks,)),
            pltpu.SemaphoreType.DMA((blocks,)),
        ],
        compiler_params=PARAMS,
        cost_estimate=pl.CostEstimate(
            flops=6 * rows * cols * rank, bytes_accessed=4 * rows * cols, transcendentals=0
        ),
        name="tall_partial",
    )(
        pltpu.with_memory_space_constraint(probes, hbm),
        pltpu.with_memory_space_constraint(sketch_t, hbm),
    )


def prepare_kernel(first_ref, second_ref, both_ref, gram_ref):
    tall = first_ref[...] + second_ref[...]
    rank = tall.shape[0]
    head, rest = split(tall)
    tail = (tall - head.astype(F32) - rest.astype(F32)).astype(BF16)
    both_ref[...] = jnp.concatenate([head, rest], axis=0)
    three = jnp.concatenate([head, rest, tail], axis=0)
    g = dot(three, three, LAST)
    r = rank
    big = g[:r, :r]
    cross = g[:r, r : 2 * r] + g[r : 2 * r, :r]
    small = g[:r, 2 * r :] + g[2 * r :, :r] + g[r : 2 * r, r : 2 * r]
    gram = big + (cross + small)
    gram_ref[...] = jnp.concatenate([gram, jnp.zeros((r, LANES - r), F32)], axis=1)


def prepare(first, second):
    rank, rows = first.shape
    return pl.pallas_call(
        prepare_kernel,
        in_specs=[WHOLE, WHOLE],
        out_specs=[WHOLE, WHOLE],
        out_shape=[
            jax.ShapeDtypeStruct((2 * rank, rows), BF16),
            jax.ShapeDtypeStruct((rank, LANES), F32),
        ],
        compiler_params=PARAMS,
        cost_estimate=pl.CostEstimate(
            flops=rows * rank * rank * 18, bytes_accessed=24 * rank * rows, transcendentals=0
        ),
        name="prepare",
    )(first, second)


def product_kernel(plan, grams, which_ref, both_ref, gram_ref, head_ref, rest_ref, *refs):
    count = 1 + max(out for out, _ in plan)
    outs = refs[len(refs) - count :]
    rank = gram_ref.shape[0]
    sub = head_ref.shape[2]
    both = both_ref[...]
    for k, (out, offset) in enumerate(plan):
        block = which_ref[k]
        first = dot(both, head_ref[block], PLAIN)
        second = dot(both[:rank], rest_ref[block], PLAIN)
        outs[out][:, offset : offset + sub] = first[:rank] + (first[rank:] + second)
    for out, offset in grams:
        outs[out][:, offset : offset + LANES] = gram_ref[...]


def products(both, gram, head, rest, outputs, after=()):
    _, rows, sub = head.shape
    rank = both.shape[0] // 2
    plan, grams, widths, which = [], [], [], []
    for out, (blocks, with_gram) in enumerate(outputs):
        extra = LANES if with_gram else 0
        for j, block in enumerate(blocks):
            plan.append((out, j * sub + (extra if j else 0)))
            which.append(block)
        if with_gram:
            grams.append((out, sub))
        widths.append(len(blocks) * sub + extra)
    vmem = pltpu.MemorySpace.VMEM
    return pl.pallas_call(
        functools.partial(product_kernel, plan, grams),
        in_specs=[
            pl.BlockSpec(memory_space=pltpu.SMEM),
            *[WHOLE] * 4,
            *[ANYWHERE] * len(after),
        ],
        out_specs=[WHOLE] * len(widths),
        out_shape=[jax.ShapeDtypeStruct((rank, width), F32) for width in widths],
        compiler_params=PARAMS,
        cost_estimate=pl.CostEstimate(
            flops=6 * rows * rank * sub * len(plan),
            bytes_accessed=4 * rank * sub * len(plan),
            transcendentals=0,
        ),
        name="products",
    )(
        jnp.stack(which),
        both,
        gram,
        pltpu.with_memory_space_constraint(head, vmem),
        pltpu.with_memory_space_constraint(rest, vmem),
        *after,
    )


def inverse_kernel(gram_ref, out_ref):
    rank = out_ref.shape[0]
    rows = lax.broadcasted_iota(jnp.int32, (rank, LANES), 0)
    cols = lax.broadcasted_iota(jnp.int32, (rank, LANES), 1)
    work = jnp.where(cols < rank, gram_ref[...], (cols == rows + rank).astype(F32))
    scale = jnp.ones((rank, LANES), F32)
    for start in range(0, rank, PANEL):
        panel = [
            jnp.broadcast_to(work[:, k : k + 1], (rank, LANES))
            for k in range(start, start + PANEL)
        ]
        for j in range(PANEL):
            k = start + j
            over = 1.0 / panel[j][k : k + 1, :]
            scale = jnp.where(rows == k, over, scale)
            factor = jnp.where(rows > k, panel[j] * over, 0.0)
            work = work - factor * work[k : k + 1, :]
            for later in range(j + 1, PANEL):
                panel[later] = panel[later] - factor * panel[later][k : k + 1, :]
    out_ref[...] = (work * jnp.sqrt(scale))[:, rank : 2 * rank]


def inverse_factor(chunk, start):
    rank = chunk.shape[0]
    return pl.pallas_call(
        inverse_kernel,
        grid=(1,),
        in_specs=[pl.BlockSpec((rank, LANES), lambda i: (0, start // LANES))],
        out_specs=pl.BlockSpec((rank, rank), lambda i: (0, 0)),
        out_shape=jax.ShapeDtypeStruct((rank, rank), F32),
        compiler_params=PARAMS,
        cost_estimate=pl.CostEstimate(
            flops=20_000_000, bytes_accessed=8 * rank * LANES, transcendentals=rank
        ),
        name="inverse_factor",
    )(chunk)


def finish_kernel(plan, where_ref, inverse_ref, *refs):
    out_ref = refs[-1]
    step = pl.program_id(0)
    rank, width = out_ref.shape
    head, rest = split(inverse_ref[...])
    both = jnp.concatenate([head, rest], axis=0)
    for k, (source, offset) in enumerate(plan):

        @pl.when(step == k)
        def _():
            p_head, p_rest = split(refs[source][:, offset : offset + width])
            first = dot(both, p_head, PLAIN)
            out_ref[...] = first[:rank] + (first[rank:] + dot(head, p_rest, PLAIN))


def finish(inverse, sources, pieces, width, total, before=None):
    rank = inverse.shape[0]
    count = len(pieces)
    in_specs = [pl.BlockSpec((rank, rank), lambda i, w: (0, 0))]
    in_specs += [pl.BlockSpec(source.shape, lambda i, w: (0, 0)) for source in sources]
    args = [inverse, *sources]
    aliases = {}
    if before is not None:
        in_specs.append(ANYWHERE)
        args.append(before)
        aliases = {len(args): 0}
    return pl.pallas_call(
        functools.partial(finish_kernel, [piece[1:] for piece in pieces]),
        grid_spec=pltpu.PrefetchScalarGridSpec(
            num_scalar_prefetch=1,
            grid=(count,),
            in_specs=in_specs,
            out_specs=pl.BlockSpec((rank, width), lambda i, w: (0, w[i])),
        ),
        out_shape=jax.ShapeDtypeStruct((rank, total), F32),
        input_output_aliases=aliases,
        compiler_params=PARAMS,
        cost_estimate=pl.CostEstimate(
            flops=6 * rank * rank * width * count,
            bytes_accessed=8 * rank * width * count,
            transcendentals=0,
        ),
        name="finish",
    )(jnp.stack([piece[0] for piece in pieces]), *args)


def body(n_pos, n_pix, probes, sketch):
    def swap(value, axis, size, bit):
        return lax.ppermute(value, axis, [(i, i ^ bit) for i in range(size)])

    def over(value, bit):
        return swap(value, "pos", n_pos, bit)

    me = lax.axis_index("pos").astype(jnp.int32)
    near, far = me & 1, (me >> 1) & 1
    cols = probes.shape[1]
    width = cols // (8 * CHUNKS)

    tall, head, rest = tall_partial(probes, sketch.T, width)
    bit = 1
    while 2 * bit < n_pix:
        tall = tall + swap(tall, "pix", n_pix, bit)
        bit *= 2
    both, gram = prepare(tall, swap(tall, "pix", n_pix, bit))

    def block_a(c, p, q):
        return 8 * c + 2 * (near ^ p) + (far ^ q)

    def block_b(c, p, q):
        return 8 * c + 4 + 2 * (far ^ p) + (near ^ q)

    def outputs(c, p):
        return [
            ([block_a(c, p, 1), block_a(c, p, 0)], c == 0),
            ([block_b(c, p, 1), block_b(c, p, 0)], False),
        ]

    first = products(both, gram, head, rest, outputs(0, 1))
    plan = [(c, p) for c in range(CHUNKS) for p in (1, 0) if (c, p) != (0, 1)]
    others = products(
        both, gram, head, rest, [out for c, p in plan for out in outputs(c, p)], (first[0],)
    )
    made = {(0, 1): first}
    made.update({key: others[2 * k : 2 * k + 2] for k, key in enumerate(plan)})

    inverse, out = None, None
    for c in range(CHUNKS):
        g = LANES if c == 0 else 0
        away_a, away_b = made[c, 1]
        own_a, own_b = made[c, 0]
        sum_a = own_a + over(away_a, 1)
        sum_b = own_b + over(away_b, 2)
        got_a = over(sum_a[:, : width + g], 2)
        got_b = over(sum_b[:, :width], 1)
        whole = jnp.concatenate(
            [
                sum_a[:, width + g :] + got_a[:, :width],
                sum_a[:, width : width + g] + got_a[:, width:],
                sum_b[:, width:] + got_b,
            ],
            axis=1,
        )
        bit = 4
        while bit < n_pos:
            whole = whole + over(whole, bit)
            bit *= 2
        if c == 0:
            inverse = inverse_factor(whole, width)
        mine_a, mine_b = whole[:, :width], whole[:, width + g :]
        next_a = over(mine_a, 2)
        next_b = over(mine_b, 1)
        last_a = over(jnp.concatenate([mine_a, next_a], axis=1), 1)
        last_b = over(jnp.concatenate([mine_b, next_b], axis=1), 2)
        out = finish(
            inverse,
            [whole, next_a, next_b],
            [
                (block_a(c, 0, 0), 0, 0),
                (block_b(c, 0, 0), 0, width + g),
                (block_a(c, 0, 1), 1, 0),
                (block_b(c, 0, 1), 2, 0),
            ],
            width,
            cols,
            out,
        )
        out = finish(
            inverse,
            [last_a, last_b],
            [
                (block_a(c, 1, 0), 0, 0),
                (block_a(c, 1, 1), 0, width),
                (block_b(c, 1, 0), 1, 0),
                (block_b(c, 1, 1), 1, width),
            ],
            width,
            cols,
            out,
        )
    return out


def solution(mesh):
    in_specs = (P("pos", "pix"), P("pix", None))
    out_specs = P(None, "pix")
    run = functools.partial(body, mesh.shape["pos"], mesh.shape["pix"])
    return jax.shard_map(run, mesh=mesh, in_specs=in_specs, out_specs=out_specs, check_vma=False)
```

```python
import functools

import jax
import jax.numpy as jnp
from jax import lax
from jax.experimental import pallas as pl
from jax.experimental.pallas import tpu as pltpu
from jax.sharding import PartitionSpec as P

F32 = jnp.float32
BF16 = jnp.bfloat16
VMEM_LIMIT = 24 * 1024 * 1024
LANES = 128
CHUNKS = 1
PANEL = 4
LAST = (((1,), (1,)), ((), ()))
PLAIN = (((1,), (0,)), ((), ()))
ANYWHERE = pl.BlockSpec(memory_space=pl.ANY)
WHOLE = pl.BlockSpec(memory_space=pltpu.VMEM)
PARAMS = pltpu.CompilerParams(vmem_limit_bytes=VMEM_LIMIT)
SMALL = pltpu.CompilerParams(vmem_limit_bytes=VMEM_LIMIT // 4)


def split(x):
    head = x.astype(BF16)
    return head, (x - head.astype(F32)).astype(BF16)


def dot(a, b, dims):
    return lax.dot_general(a, b, dims, preferred_element_type=F32)


def tall_kernel(x_hbm, s_hbm, out_ref, head_ref, rest_ref, x_buf, s_buf, x_sems, s_sems):
    blocks, rows, width = x_buf.shape
    rank = s_hbm.shape[0]

    def copies(k):
        where = pl.ds(k * width, width)
        return (
            pltpu.make_async_copy(s_hbm.at[:, where], s_buf.at[k], s_sems.at[k]),
            pltpu.make_async_copy(x_hbm.at[:, where], x_buf.at[k], x_sems.at[k]),
        )

    for k in range(blocks):
        for copy in copies(k):
            copy.start()
    for k in range(blocks):
        for copy in copies(k):
            copy.wait()
        s_head, s_rest = split(s_buf[k])
        s_both = jnp.concatenate([s_head, s_rest], axis=0)
        x_head, x_rest = split(x_buf[k])
        head_ref[k] = x_head
        rest_ref[k] = x_rest
        both = dot(s_both, x_head, LAST)
        part = both[:rank] + (both[rank:] + dot(s_head, x_rest, LAST))
        if k == 0:
            out_ref[...] = part
        else:
            out_ref[...] += part


def tall_partial(probes, sketch_t, width):
    rows, cols = probes.shape
    rank = sketch_t.shape[0]
    blocks = cols // width
    hbm = pltpu.MemorySpace.HBM
    return pl.pallas_call(
        tall_kernel,
        in_specs=[pl.BlockSpec(memory_space=hbm)] * 2,
        out_specs=[WHOLE] * 3,
        out_shape=[
            jax.ShapeDtypeStruct((rank, rows), F32),
            pltpu.VMEM((blocks, rows, width), BF16),
            pltpu.VMEM((blocks, rows, width), BF16),
        ],
        scratch_shapes=[
            pltpu.VMEM((blocks, rows, width), F32),
            pltpu.VMEM((blocks, rank, width), F32),
            pltpu.SemaphoreType.DMA((blocks,)),
            pltpu.SemaphoreType.DMA((blocks,)),
        ],
        compiler_params=PARAMS,
        cost_estimate=pl.CostEstimate(
            flops=6 * rows * cols * rank, bytes_accessed=4 * rows * cols, transcendentals=0
        ),
        name="tall_partial",
    )(
        pltpu.with_memory_space_constraint(probes, hbm),
        pltpu.with_memory_space_constraint(sketch_t, hbm),
    )


def prepare_kernel(first_ref, second_ref, both_ref, gram_ref):
    tall = first_ref[...] + second_ref[...]
    rank = tall.shape[0]
    head, rest = split(tall)
    tail = (tall - head.astype(F32) - rest.astype(F32)).astype(BF16)
    both_ref[...] = jnp.concatenate([head, rest], axis=0)
    three = jnp.concatenate([head, rest, tail], axis=0)
    g = dot(three, three, LAST)
    r = rank
    big = g[:r, :r]
    cross = g[:r, r : 2 * r] + g[r : 2 * r, :r]
    small = g[:r, 2 * r :] + g[2 * r :, :r] + g[r : 2 * r, r : 2 * r]
    gram = big + (cross + small)
    gram_ref[...] = jnp.concatenate([gram, jnp.zeros((r, LANES - r), F32)], axis=1)


def prepare(first, second):
    rank, rows = first.shape
    return pl.pallas_call(
        prepare_kernel,
        in_specs=[WHOLE, WHOLE],
        out_specs=[WHOLE, WHOLE],
        out_shape=[
            jax.ShapeDtypeStruct((2 * rank, rows), BF16),
            jax.ShapeDtypeStruct((rank, LANES), F32),
        ],
        compiler_params=SMALL,
        cost_estimate=pl.CostEstimate(
            flops=rows * rank * rank * 18, bytes_accessed=24 * rank * rows, transcendentals=0
        ),
        name="prepare",
    )(first, second)


def product_kernel(plan, grams, which_ref, both_ref, gram_ref, head_ref, rest_ref, *refs):
    count = 1 + max(out for out, _ in plan)
    outs = refs[len(refs) - count :]
    rank = gram_ref.shape[0]
    sub = head_ref.shape[2]
    both = both_ref[...]
    for k, (out, offset) in enumerate(plan):
        block = which_ref[k]
        first = dot(both, head_ref[block], PLAIN)
        second = dot(both[:rank], rest_ref[block], PLAIN)
        outs[out][:, offset : offset + sub] = first[:rank] + (first[rank:] + second)
    for out, offset in grams:
        outs[out][:, offset : offset + LANES] = gram_ref[...]


def products(both, gram, head, rest, outputs, after=()):
    _, rows, sub = head.shape
    rank = both.shape[0] // 2
    plan, grams, widths, which = [], [], [], []
    for out, (blocks, with_gram) in enumerate(outputs):
        extra = LANES if with_gram else 0
        for j, block in enumerate(blocks):
            plan.append((out, j * sub + (extra if j else 0)))
            which.append(block)
        if with_gram:
            grams.append((out, sub))
        widths.append(len(blocks) * sub + extra)
    return pl.pallas_call(
        functools.partial(product_kernel, plan, grams),
        in_specs=[
            pl.BlockSpec(memory_space=pltpu.SMEM),
            *[WHOLE] * 4,
            *[ANYWHERE] * len(after),
        ],
        out_specs=[WHOLE] * len(widths),
        out_shape=[jax.ShapeDtypeStruct((rank, width), F32) for width in widths],
        compiler_params=PARAMS,
        cost_estimate=pl.CostEstimate(
            flops=6 * rows * rank * sub * len(plan),
            bytes_accessed=4 * rank * sub * len(plan),
            transcendentals=0,
        ),
        name="products",
    )(
        jnp.stack(which),
        both,
        gram,
        head,
        rest,
        *after,
    )


def inverse_kernel(gram_ref, out_ref):
    rank = out_ref.shape[0]
    rows = lax.broadcasted_iota(jnp.int32, (rank, LANES), 0)
    cols = lax.broadcasted_iota(jnp.int32, (rank, LANES), 1)
    work = jnp.where(cols < rank, gram_ref[...], (cols == rows + rank).astype(F32))
    scale = jnp.ones((rank, LANES), F32)
    for start in range(0, rank, PANEL):
        panel = [
            jnp.broadcast_to(work[:, k : k + 1], (rank, LANES))
            for k in range(start, start + PANEL)
        ]
        for j in range(PANEL):
            k = start + j
            over = 1.0 / panel[j][k : k + 1, :]
            scale = jnp.where(rows == k, over, scale)
            factor = jnp.where(rows > k, panel[j] * over, 0.0)
            work = work - factor * work[k : k + 1, :]
            for later in range(j + 1, PANEL):
                panel[later] = panel[later] - factor * panel[later][k : k + 1, :]
    out_ref[...] = (work * jnp.sqrt(scale))[:, rank : 2 * rank]


def inverse_factor(chunk, start):
    rank = chunk.shape[0]
    return pl.pallas_call(
        inverse_kernel,
        grid=(1,),
        in_specs=[pl.BlockSpec((rank, LANES), lambda i: (0, start // LANES))],
        out_specs=pl.BlockSpec((rank, rank), lambda i: (0, 0)),
        out_shape=jax.ShapeDtypeStruct((rank, rank), F32),
        compiler_params=SMALL,
        cost_estimate=pl.CostEstimate(
            flops=20_000_000, bytes_accessed=8 * rank * LANES, transcendentals=rank
        ),
        name="inverse_factor",
    )(chunk)


def finish_kernel(plan, where_ref, inverse_ref, *refs):
    out_ref = refs[-1]
    step = pl.program_id(0)
    rank, width = out_ref.shape
    head, rest = split(inverse_ref[...])
    both = jnp.concatenate([head, rest], axis=0)
    for k, (source, offset) in enumerate(plan):

        @pl.when(step == k)
        def _():
            p_head, p_rest = split(refs[source][:, offset : offset + width])
            first = dot(both, p_head, PLAIN)
            out_ref[...] = first[:rank] + (first[rank:] + dot(head, p_rest, PLAIN))


def finish(inverse, sources, pieces, width, total, before=None):
    rank = inverse.shape[0]
    count = len(pieces)
    in_specs = [pl.BlockSpec((rank, rank), lambda i, w: (0, 0))]
    in_specs += [pl.BlockSpec(source.shape, lambda i, w: (0, 0)) for source in sources]
    args = [inverse, *sources]
    aliases = {}
    if before is not None:
        in_specs.append(ANYWHERE)
        args.append(before)
        aliases = {len(args): 0}
    return pl.pallas_call(
        functools.partial(finish_kernel, [piece[1:] for piece in pieces]),
        grid_spec=pltpu.PrefetchScalarGridSpec(
            num_scalar_prefetch=1,
            grid=(count,),
            in_specs=in_specs,
            out_specs=pl.BlockSpec((rank, width), lambda i, w: (0, w[i])),
        ),
        out_shape=jax.ShapeDtypeStruct((rank, total), F32),
        input_output_aliases=aliases,
        compiler_params=SMALL,
        cost_estimate=pl.CostEstimate(
            flops=6 * rank * rank * width * count,
            bytes_accessed=8 * rank * width * count,
            transcendentals=0,
        ),
        name="finish",
    )(jnp.stack([piece[0] for piece in pieces]), *args)


def body(n_pos, n_pix, probes, sketch):
    def swap(value, axis, size, bit):
        return lax.ppermute(value, axis, [(i, i ^ bit) for i in range(size)])

    def over(value, bit):
        return swap(value, "pos", n_pos, bit)

    me = lax.axis_index("pos").astype(jnp.int32)
    near, far = me & 1, (me >> 1) & 1
    cols = probes.shape[1]
    width = cols // (8 * CHUNKS)

    tall, head, rest = tall_partial(probes, sketch.T, width)
    bit = 1
    while 2 * bit < n_pix:
        tall = tall + swap(tall, "pix", n_pix, bit)
        bit *= 2
    both, gram = prepare(tall, swap(tall, "pix", n_pix, bit))

    def block_a(c, p, q):
        return 8 * c + 2 * (near ^ p) + (far ^ q)

    def block_b(c, p, q):
        return 8 * c + 4 + 2 * (far ^ p) + (near ^ q)

    def outputs(c, p):
        return [
            ([block_a(c, p, 1), block_a(c, p, 0)], c == 0),
            ([block_b(c, p, 1), block_b(c, p, 0)], False),
        ]

    first = products(both, gram, head, rest, outputs(0, 1))
    plan = [(c, p) for c in range(CHUNKS) for p in (1, 0) if (c, p) != (0, 1)]
    others = products(
        both, gram, head, rest, [out for c, p in plan for out in outputs(c, p)], (first[0],)
    )
    made = {(0, 1): first}
    made.update({key: others[2 * k : 2 * k + 2] for k, key in enumerate(plan)})

    inverse, out = None, None
    for c in range(CHUNKS):
        g = LANES if c == 0 else 0
        away_a, away_b = made[c, 1]
        own_a, own_b = made[c, 0]
        sum_a = own_a + over(away_a, 1)
        sum_b = own_b + over(away_b, 2)
        got_a = over(sum_a[:, : width + g], 2)
        got_b = over(sum_b[:, :width], 1)
        whole = jnp.concatenate(
            [
                sum_a[:, width + g :] + got_a[:, :width],
                sum_a[:, width : width + g] + got_a[:, width:],
                sum_b[:, width:] + got_b,
            ],
            axis=1,
        )
        bit = 4
        while bit < n_pos:
            whole = whole + over(whole, bit)
            bit *= 2
        if c == 0:
            inverse = inverse_factor(whole, width)
        mine_a, mine_b = whole[:, :width], whole[:, width + g :]
        next_a = over(mine_a, 2)
        next_b = over(mine_b, 1)
        last_a = over(jnp.concatenate([mine_a, next_a], axis=1), 1)
        last_b = over(jnp.concatenate([mine_b, next_b], axis=1), 2)
        out = finish(
            inverse,
            [whole, next_a, next_b],
            [
                (block_a(c, 0, 0), 0, 0),
                (block_b(c, 0, 0), 0, width + g),
                (block_a(c, 0, 1), 1, 0),
                (block_b(c, 0, 1), 2, 0),
            ],
            width,
            cols,
            out,
        )
        out = finish(
            inverse,
            [last_a, last_b],
            [
                (block_a(c, 1, 0), 0, 0),
                (block_a(c, 1, 1), 0, width),
                (block_b(c, 1, 0), 1, 0),
                (block_b(c, 1, 1), 1, width),
            ],
            width,
            cols,
            out,
        )
    return out


def solution(mesh):
    in_specs = (P("pos", "pix"), P("pix", None))
    out_specs = P(None, "pix")
    run = functools.partial(body, mesh.shape["pos"], mesh.shape["pix"])
    return jax.shard_map(run, mesh=mesh, in_specs=in_specs, out_specs=out_specs, check_vma=False)
```

```python
import functools

import jax
import jax.numpy as jnp
from jax import lax
from jax.experimental import pallas as pl
from jax.experimental.pallas import tpu as pltpu
from jax.sharding import PartitionSpec as P

F32 = jnp.float32
BF16 = jnp.bfloat16
VMEM_LIMIT = 40 * 1024 * 1024
LANES = 128
CHUNKS = 1
AHEAD = 6
UNIT = 512
PANEL = 4
LAST = (((1,), (1,)), ((), ()))
PLAIN = (((1,), (0,)), ((), ()))
ANYWHERE = pl.BlockSpec(memory_space=pl.ANY)
HBM = pl.BlockSpec(memory_space=pltpu.MemorySpace.HBM)
WHOLE = pl.BlockSpec(memory_space=pltpu.VMEM)
TABLE = pl.BlockSpec(memory_space=pltpu.SMEM)
PARAMS = pltpu.CompilerParams(vmem_limit_bytes=VMEM_LIMIT)


def split(x):
    head = x.astype(BF16)
    return head, (x - head.astype(F32)).astype(BF16)


def dot(a, b, dims):
    return lax.dot_general(a, b, dims, preferred_element_type=F32)


def in_hbm(x):
    return pltpu.with_memory_space_constraint(x, pltpu.MemorySpace.HBM)


def stream(copies, use):
    for copy in copies[:AHEAD]:
        copy.start()
    for k, copy in enumerate(copies):
        copy.wait()
        if k + AHEAD < len(copies):
            copies[k + AHEAD].start()
        use(k)


def tall_kernel(x_hbm, s_hbm, out_ref, x_buf, s_buf, x_sems, s_sem):
    blocks, _, unit = x_buf.shape
    rank = s_hbm.shape[0]
    copies = [
        pltpu.make_async_copy(x_hbm.at[:, pl.ds(k * unit, unit)], x_buf.at[k], x_sems.at[k])
        for k in range(blocks)
    ]
    sketch = pltpu.make_async_copy(s_hbm, s_buf, s_sem)
    sketch.start()

    def use(k):
        if k == 0:
            sketch.wait()
        s_head, s_rest = split(s_buf[:, k * unit : (k + 1) * unit])
        s_both = jnp.concatenate([s_head, s_rest], axis=0)
        x_head, x_rest = split(x_buf[k])
        both = dot(s_both, x_head, LAST)
        part = both[:rank] + (both[rank:] + dot(s_head, x_rest, LAST))
        if k == 0:
            out_ref[...] = part
        else:
            out_ref[...] += part

    stream(copies, use)


def tall_partial(probes, sketch_t):
    rows, cols = probes.shape
    rank = sketch_t.shape[0]
    unit = min(UNIT, cols)
    blocks = cols // unit
    return pl.pallas_call(
        tall_kernel,
        in_specs=[HBM, HBM],
        out_specs=WHOLE,
        out_shape=jax.ShapeDtypeStruct((rank, rows), F32),
        scratch_shapes=[
            pltpu.VMEM((blocks, rows, unit), F32),
            pltpu.VMEM((rank, cols), F32),
            pltpu.SemaphoreType.DMA((blocks,)),
            pltpu.SemaphoreType.DMA,
        ],
        compiler_params=PARAMS,
        cost_estimate=pl.CostEstimate(
            flops=6 * rows * cols * rank, bytes_accessed=4 * rows * cols, transcendentals=0
        ),
        name="tall_partial",
    )(in_hbm(probes), in_hbm(sketch_t))


def multiply_blocks(both_ref, which_ref, x_hbm, x_buf, sems, plan, outs):
    rank = outs[0].shape[0]
    unit = x_buf.shape[2]
    copies = [
        pltpu.make_async_copy(
            x_hbm.at[:, pl.ds(pl.multiple_of(which_ref[k] * unit, unit), unit)],
            x_buf.at[k],
            sems.at[k],
        )
        for k in range(len(plan))
    ]

    def use(k):
        both = both_ref[...]
        x_head, x_rest = split(x_buf[k])
        first = dot(both, x_head, PLAIN)
        second = dot(both[:rank], x_rest, PLAIN)
        out, offset = plan[k]
        outs[out][:, offset : offset + unit] = first[:rank] + (first[rank:] + second)

    return copies, use


def first_kernel(plan, grams, which_ref, one_ref, two_ref, x_hbm, both_ref, gram_ref, *refs):
    outs, (x_buf, sems) = refs[:-2], refs[-2:]
    copies, use = multiply_blocks(both_ref, which_ref, x_hbm, x_buf, sems, plan, outs)

    def use_first(k):
        if k == 0:
            tall = one_ref[...] + two_ref[...]
            head, rest = split(tall)
            both_ref[...] = jnp.concatenate([head, rest], axis=0)
        use(k)

    stream(copies, use_first)
    tall = one_ref[...] + two_ref[...]
    r = tall.shape[0]
    head, rest = split(tall)
    tail = (tall - head.astype(F32) - rest.astype(F32)).astype(BF16)
    three = jnp.concatenate([head, rest, tail], axis=0)
    g = dot(three, three, LAST)
    cross = g[:r, r : 2 * r] + g[r : 2 * r, :r]
    small = g[:r, 2 * r :] + g[2 * r :, :r] + g[r : 2 * r, r : 2 * r]
    gram = g[:r, :r] + (cross + small)
    gram_ref[...] = jnp.concatenate([gram, jnp.zeros((r, LANES - r), F32)], axis=1)
    for out, offset in grams:
        outs[out][:, offset : offset + LANES] = gram_ref[...]


def rest_kernel(plan, grams, which_ref, both_ref, gram_ref, x_hbm, after_ref, *refs):
    outs, (x_buf, sems) = refs[:-2], refs[-2:]
    copies, use = multiply_blocks(both_ref, which_ref, x_hbm, x_buf, sems, plan, outs)
    stream(copies, use)
    for out, offset in grams:
        outs[out][:, offset : offset + LANES] = gram_ref[...]


def layout(outputs, sub):
    unit = min(UNIT, sub)
    plan, grams, widths, which = [], [], [], []
    for out, (blocks, with_gram) in enumerate(outputs):
        extra = LANES if with_gram else 0
        for j, block in enumerate(blocks):
            for part in range(sub // unit):
                plan.append((out, j * sub + part * unit + (extra if j else 0)))
                which.append(block * (sub // unit) + part)
        if with_gram:
            grams.append((out, sub))
        widths.append(len(blocks) * sub + extra)
    return unit, plan, grams, widths, jnp.stack(which)


def products(kernel, inputs, in_specs, made, probes, outputs, sub, name):
    rows = probes.shape[0]
    rank = inputs[1].shape[0]
    unit, plan, grams, widths, which = layout(outputs, sub)
    shapes = [*made, *[jax.ShapeDtypeStruct((rank, width), F32) for width in widths]]
    return pl.pallas_call(
        functools.partial(kernel, plan, grams),
        in_specs=[TABLE, *in_specs],
        out_specs=[WHOLE] * len(shapes),
        out_shape=shapes,
        scratch_shapes=[
            pltpu.VMEM((len(plan), rows, unit), F32),
            pltpu.SemaphoreType.DMA((len(plan),)),
        ],
        compiler_params=PARAMS,
        cost_estimate=pl.CostEstimate(
            flops=6 * rows * rank * unit * len(plan),
            bytes_accessed=4 * rows * unit * len(plan),
            transcendentals=0,
        ),
        name=name,
    )(which, *inputs)


def first_products(one, two, probes, outputs, sub):
    rank, rows = one.shape
    made = [
        jax.ShapeDtypeStruct((2 * rank, rows), BF16),
        jax.ShapeDtypeStruct((rank, LANES), F32),
    ]
    both, gram, *outs = products(
        first_kernel,
        [one, two, in_hbm(probes)],
        [WHOLE, WHOLE, HBM],
        made,
        probes,
        outputs,
        sub,
        "first_products",
    )
    return both, gram, outs


def rest_products(both, gram, probes, outputs, sub, after):
    return products(
        rest_kernel,
        [both, gram, in_hbm(probes), after],
        [WHOLE, WHOLE, HBM, ANYWHERE],
        [],
        probes,
        outputs,
        sub,
        "rest_products",
    )


def inverse_kernel(gram_ref, out_ref):
    rank = out_ref.shape[0]
    rows = lax.broadcasted_iota(jnp.int32, (rank, LANES), 0)
    cols = lax.broadcasted_iota(jnp.int32, (rank, LANES), 1)
    work = jnp.where(cols < rank, gram_ref[...], (cols == rows + rank).astype(F32))
    scale = jnp.ones((rank, LANES), F32)
    for start in range(0, rank, PANEL):
        panel = [
            jnp.broadcast_to(work[:, k : k + 1], (rank, LANES))
            for k in range(start, start + PANEL)
        ]
        for j in range(PANEL):
            k = start + j
            over = 1.0 / panel[j][k : k + 1, :]
            scale = jnp.where(rows == k, over, scale)
            factor = jnp.where(rows > k, panel[j] * over, 0.0)
            work = work - factor * work[k : k + 1, :]
            for later in range(j + 1, PANEL):
                panel[later] = panel[later] - factor * panel[later][k : k + 1, :]
    out_ref[...] = (work * jnp.sqrt(scale))[:, rank : 2 * rank]


def inverse_factor(chunk, start):
    rank = chunk.shape[0]
    return pl.pallas_call(
        inverse_kernel,
        grid=(1,),
        in_specs=[pl.BlockSpec((rank, LANES), lambda i: (0, start // LANES))],
        out_specs=pl.BlockSpec((rank, rank), lambda i: (0, 0)),
        out_shape=jax.ShapeDtypeStruct((rank, rank), F32),
        compiler_params=PARAMS,
        cost_estimate=pl.CostEstimate(
            flops=20_000_000, bytes_accessed=8 * rank * LANES, transcendentals=rank
        ),
        name="inverse_factor",
    )(chunk)


def finish_kernel(plan, where_ref, inverse_ref, *refs):
    out_hbm, buf, sems = refs[-3:]
    _, rank, width = buf.shape
    head, rest = split(inverse_ref[...])
    both = jnp.concatenate([head, rest], axis=0)
    copies = []
    for k, (source, offset) in enumerate(plan):
        p_head, p_rest = split(refs[source][:, offset : offset + width])
        first = dot(both, p_head, PLAIN)
        buf[k] = first[:rank] + (first[rank:] + dot(head, p_rest, PLAIN))
        where = pl.ds(pl.multiple_of(where_ref[k] * width, width), width)
        copies.append(pltpu.make_async_copy(buf.at[k], out_hbm.at[:, where], sems.at[k]))
        copies[k].start()
    for copy in copies:
        copy.wait()


def finish(inverse, sources, pieces, width, total, before=None):
    rank = inverse.shape[0]
    count = len(pieces)
    in_specs = [TABLE, WHOLE, *[WHOLE] * len(sources)]
    args = [jnp.stack([piece[0] for piece in pieces]), inverse, *sources]
    aliases = {}
    if before is not None:
        in_specs.append(HBM)
        args.append(before)
        aliases = {len(args) - 1: 0}
    return pl.pallas_call(
        functools.partial(finish_kernel, [piece[1:] for piece in pieces]),
        in_specs=in_specs,
        out_specs=HBM,
        out_shape=jax.ShapeDtypeStruct((rank, total), F32),
        scratch_shapes=[
            pltpu.VMEM((count, rank, width), F32),
            pltpu.SemaphoreType.DMA((count,)),
        ],
        input_output_aliases=aliases,
        compiler_params=PARAMS,
        cost_estimate=pl.CostEstimate(
            flops=6 * rank * rank * width * count,
            bytes_accessed=8 * rank * width * count,
            transcendentals=0,
        ),
        name="finish",
    )(*args)


def body(n_pos, n_pix, probes, sketch):
    def swap(value, axis, size, bit):
        return lax.ppermute(value, axis, [(i, i ^ bit) for i in range(size)])

    def over(value, bit):
        return swap(value, "pos", n_pos, bit)

    me = lax.axis_index("pos").astype(jnp.int32)
    near, far = me & 1, (me >> 1) & 1
    cols = probes.shape[1]
    width = cols // (8 * CHUNKS)

    tall = tall_partial(probes, sketch.T)
    bit = 1
    while 2 * bit < n_pix:
        tall = tall + swap(tall, "pix", n_pix, bit)
        bit *= 2
    other = swap(tall, "pix", n_pix, bit)

    def block_a(c, p, q):
        return 8 * c + 2 * (near ^ p) + (far ^ q)

    def block_b(c, p, q):
        return 8 * c + 4 + 2 * (far ^ p) + (near ^ q)

    def outputs(c, p):
        return [
            ([block_a(c, p, 1), block_a(c, p, 0)], c == 0),
            ([block_b(c, p, 1), block_b(c, p, 0)], False),
        ]

    both, gram, first = first_products(tall, other, probes, outputs(0, 1), width)
    plan = [(c, p) for c in range(CHUNKS) for p in (1, 0) if (c, p) != (0, 1)]
    rest = rest_products(
        both, gram, probes, [out for c, p in plan for out in outputs(c, p)], width, first[0]
    )
    made = {(0, 1): first}
    made.update({key: rest[2 * k : 2 * k + 2] for k, key in enumerate(plan)})

    inverse, out = None, None
    for c in range(CHUNKS):
        g = LANES if c == 0 else 0
        away_a, away_b = made[c, 1]
        own_a, own_b = made[c, 0]
        sum_a = own_a + over(away_a, 1)
        sum_b = own_b + over(away_b, 2)
        got_a = over(sum_a[:, : width + g], 2)
        got_b = over(sum_b[:, :width], 1)
        whole = jnp.concatenate(
            [
                sum_a[:, width + g :] + got_a[:, :width],
                sum_a[:, width : width + g] + got_a[:, width:],
                sum_b[:, width:] + got_b,
            ],
            axis=1,
        )
        bit = 4
        while bit < n_pos:
            whole = whole + over(whole, bit)
            bit *= 2
        if c == 0:
            inverse = inverse_factor(whole, width)
        mine_a, mine_b = whole[:, :width], whole[:, width + g :]
        next_a = over(mine_a, 2)
        next_b = over(mine_b, 1)
        last_a = over(jnp.concatenate([mine_a, next_a], axis=1), 1)
        last_b = over(jnp.concatenate([mine_b, next_b], axis=1), 2)
        out = finish(
            inverse,
            [whole, next_a, next_b],
            [
                (block_a(c, 0, 0), 0, 0),
                (block_b(c, 0, 0), 0, width + g),
                (block_a(c, 0, 1), 1, 0),
                (block_b(c, 0, 1), 2, 0),
            ],
            width,
            cols,
            out,
        )
        out = finish(
            inverse,
            [last_a, last_b],
            [
                (block_a(c, 1, 0), 0, 0),
                (block_a(c, 1, 1), 0, width),
                (block_b(c, 1, 0), 1, 0),
                (block_b(c, 1, 1), 1, width),
            ],
            width,
            cols,
            out,
        )
    return out


def solution(mesh):
    in_specs = (P("pos", "pix"), P("pix", None))
    out_specs = P(None, "pix")
    run = functools.partial(body, mesh.shape["pos"], mesh.shape["pix"])
    return jax.shard_map(run, mesh=mesh, in_specs=in_specs, out_specs=out_specs, check_vma=False)
```

```python
import functools

import jax
import jax.numpy as jnp
from jax import lax
from jax.experimental import pallas as pl
from jax.experimental.pallas import tpu as pltpu
from jax.sharding import PartitionSpec as P

F32 = jnp.float32
BF16 = jnp.bfloat16
VMEM_LIMIT = 40 * 1024 * 1024
LANES = 128
CHUNKS = 2
AHEAD = 6
UNIT = 512
PANEL = 4
LAST = (((1,), (1,)), ((), ()))
PLAIN = (((1,), (0,)), ((), ()))
ANYWHERE = pl.BlockSpec(memory_space=pl.ANY)
HBM = pl.BlockSpec(memory_space=pltpu.MemorySpace.HBM)
WHOLE = pl.BlockSpec(memory_space=pltpu.VMEM)
TABLE = pl.BlockSpec(memory_space=pltpu.SMEM)
PARAMS = pltpu.CompilerParams(vmem_limit_bytes=VMEM_LIMIT)


def split(x):
    head = x.astype(BF16)
    return head, (x - head.astype(F32)).astype(BF16)


def dot(a, b, dims):
    return lax.dot_general(a, b, dims, preferred_element_type=F32)


def in_hbm(x):
    return pltpu.with_memory_space_constraint(x, pltpu.MemorySpace.HBM)


def stream(copies, use):
    for copy in copies[:AHEAD]:
        copy.start()
    for k, copy in enumerate(copies):
        copy.wait()
        if k + AHEAD < len(copies):
            copies[k + AHEAD].start()
        use(k)


def tall_kernel(x_hbm, s_hbm, out_ref, x_buf, s_buf, x_sems, s_sem):
    blocks, _, unit = x_buf.shape
    rank = s_hbm.shape[0]
    copies = [
        pltpu.make_async_copy(x_hbm.at[:, pl.ds(k * unit, unit)], x_buf.at[k], x_sems.at[k])
        for k in range(blocks)
    ]
    sketch = pltpu.make_async_copy(s_hbm, s_buf, s_sem)
    sketch.start()

    def use(k):
        if k == 0:
            sketch.wait()
        s_head, s_rest = split(s_buf[:, k * unit : (k + 1) * unit])
        s_both = jnp.concatenate([s_head, s_rest], axis=0)
        x_head, x_rest = split(x_buf[k])
        both = dot(s_both, x_head, LAST)
        part = both[:rank] + (both[rank:] + dot(s_head, x_rest, LAST))
        if k == 0:
            out_ref[...] = part
        else:
            out_ref[...] += part

    stream(copies, use)


def tall_partial(probes, sketch_t):
    rows, cols = probes.shape
    rank = sketch_t.shape[0]
    unit = min(UNIT, cols)
    blocks = cols // unit
    return pl.pallas_call(
        tall_kernel,
        in_specs=[HBM, HBM],
        out_specs=WHOLE,
        out_shape=jax.ShapeDtypeStruct((rank, rows), F32),
        scratch_shapes=[
            pltpu.VMEM((blocks, rows, unit), F32),
            pltpu.VMEM((rank, cols), F32),
            pltpu.SemaphoreType.DMA((blocks,)),
            pltpu.SemaphoreType.DMA,
        ],
        compiler_params=PARAMS,
        cost_estimate=pl.CostEstimate(
            flops=6 * rows * cols * rank, bytes_accessed=4 * rows * cols, transcendentals=0
        ),
        name="tall_partial",
    )(in_hbm(probes), in_hbm(sketch_t))


def multiply_blocks(both_ref, which_ref, x_hbm, x_buf, sems, plan, outs):
    rank = outs[0].shape[0]
    unit = x_buf.shape[2]
    copies = [
        pltpu.make_async_copy(
            x_hbm.at[:, pl.ds(pl.multiple_of(which_ref[k] * unit, unit), unit)],
            x_buf.at[k],
            sems.at[k],
        )
        for k in range(len(plan))
    ]

    def use(k):
        both = both_ref[...]
        x_head, x_rest = split(x_buf[k])
        first = dot(both, x_head, PLAIN)
        second = dot(both[:rank], x_rest, PLAIN)
        out, offset = plan[k]
        outs[out][:, offset : offset + unit] = first[:rank] + (first[rank:] + second)

    return copies, use


def first_kernel(plan, grams, which_ref, one_ref, two_ref, x_hbm, both_ref, gram_ref, *refs):
    outs, (x_buf, sems) = refs[:-2], refs[-2:]
    copies, use = multiply_blocks(both_ref, which_ref, x_hbm, x_buf, sems, plan, outs)

    def use_first(k):
        if k == 0:
            tall = one_ref[...] + two_ref[...]
            head, rest = split(tall)
            both_ref[...] = jnp.concatenate([head, rest], axis=0)
        use(k)

    stream(copies, use_first)
    tall = one_ref[...] + two_ref[...]
    r = tall.shape[0]
    head, rest = split(tall)
    tail = (tall - head.astype(F32) - rest.astype(F32)).astype(BF16)
    three = jnp.concatenate([head, rest, tail], axis=0)
    g = dot(three, three, LAST)
    cross = g[:r, r : 2 * r] + g[r : 2 * r, :r]
    small = g[:r, 2 * r :] + g[2 * r :, :r] + g[r : 2 * r, r : 2 * r]
    gram = g[:r, :r] + (cross + small)
    gram_ref[...] = jnp.concatenate([gram, jnp.zeros((r, LANES - r), F32)], axis=1)
    for out, offset in grams:
        outs[out][:, offset : offset + LANES] = gram_ref[...]


def rest_kernel(plan, grams, which_ref, both_ref, gram_ref, x_hbm, after_ref, *refs):
    outs, (x_buf, sems) = refs[:-2], refs[-2:]
    copies, use = multiply_blocks(both_ref, which_ref, x_hbm, x_buf, sems, plan, outs)
    stream(copies, use)
    for out, offset in grams:
        outs[out][:, offset : offset + LANES] = gram_ref[...]


def layout(outputs, sub):
    unit = min(UNIT, sub)
    plan, grams, widths, which = [], [], [], []
    for out, (blocks, with_gram) in enumerate(outputs):
        extra = LANES if with_gram else 0
        for j, block in enumerate(blocks):
            for part in range(sub // unit):
                plan.append((out, j * sub + part * unit + (extra if j else 0)))
                which.append(block * (sub // unit) + part)
        if with_gram:
            grams.append((out, sub))
        widths.append(len(blocks) * sub + extra)
    return unit, plan, grams, widths, jnp.stack(which)


def products(kernel, inputs, in_specs, made, probes, outputs, sub, name):
    rows = probes.shape[0]
    rank = inputs[1].shape[0]
    unit, plan, grams, widths, which = layout(outputs, sub)
    shapes = [*made, *[jax.ShapeDtypeStruct((rank, width), F32) for width in widths]]
    return pl.pallas_call(
        functools.partial(kernel, plan, grams),
        in_specs=[TABLE, *in_specs],
        out_specs=[WHOLE] * len(shapes),
        out_shape=shapes,
        scratch_shapes=[
            pltpu.VMEM((len(plan), rows, unit), F32),
            pltpu.SemaphoreType.DMA((len(plan),)),
        ],
        compiler_params=PARAMS,
        cost_estimate=pl.CostEstimate(
            flops=6 * rows * rank * unit * len(plan),
            bytes_accessed=4 * rows * unit * len(plan),
            transcendentals=0,
        ),
        name=name,
    )(which, *inputs)


def first_products(one, two, probes, outputs, sub):
    rank, rows = one.shape
    made = [
        jax.ShapeDtypeStruct((2 * rank, rows), BF16),
        jax.ShapeDtypeStruct((rank, LANES), F32),
    ]
    both, gram, *outs = products(
        first_kernel,
        [one, two, in_hbm(probes)],
        [WHOLE, WHOLE, HBM],
        made,
        probes,
        outputs,
        sub,
        "first_products",
    )
    return both, gram, outs


def rest_products(both, gram, probes, outputs, sub, after):
    return products(
        rest_kernel,
        [both, gram, in_hbm(probes), after],
        [WHOLE, WHOLE, HBM, ANYWHERE],
        [],
        probes,
        outputs,
        sub,
        "rest_products",
    )


def inverse_kernel(gram_ref, out_ref):
    rank = out_ref.shape[0]
    rows = lax.broadcasted_iota(jnp.int32, (rank, LANES), 0)
    cols = lax.broadcasted_iota(jnp.int32, (rank, LANES), 1)
    work = jnp.where(cols < rank, gram_ref[...], (cols == rows + rank).astype(F32))
    scale = jnp.ones((rank, LANES), F32)
    for start in range(0, rank, PANEL):
        panel = [
            jnp.broadcast_to(work[:, k : k + 1], (rank, LANES))
            for k in range(start, start + PANEL)
        ]
        for j in range(PANEL):
            k = start + j
            over = 1.0 / panel[j][k : k + 1, :]
            scale = jnp.where(rows == k, over, scale)
            factor = jnp.where(rows > k, panel[j] * over, 0.0)
            work = work - factor * work[k : k + 1, :]
            for later in range(j + 1, PANEL):
                panel[later] = panel[later] - factor * panel[later][k : k + 1, :]
    out_ref[...] = (work * jnp.sqrt(scale))[:, rank : 2 * rank]


def inverse_factor(chunk, start):
    rank = chunk.shape[0]
    return pl.pallas_call(
        inverse_kernel,
        grid=(1,),
        in_specs=[pl.BlockSpec((rank, LANES), lambda i: (0, start // LANES))],
        out_specs=pl.BlockSpec((rank, rank), lambda i: (0, 0)),
        out_shape=jax.ShapeDtypeStruct((rank, rank), F32),
        compiler_params=PARAMS,
        cost_estimate=pl.CostEstimate(
            flops=20_000_000, bytes_accessed=8 * rank * LANES, transcendentals=rank
        ),
        name="inverse_factor",
    )(chunk)


def finish_kernel(plan, where_ref, inverse_ref, *refs):
    out_hbm, buf, sems = refs[-3:]
    _, rank, width = buf.shape
    head, rest = split(inverse_ref[...])
    both = jnp.concatenate([head, rest], axis=0)
    copies = []
    for k, (source, offset) in enumerate(plan):
        p_head, p_rest = split(refs[source][:, offset : offset + width])
        first = dot(both, p_head, PLAIN)
        buf[k] = first[:rank] + (first[rank:] + dot(head, p_rest, PLAIN))
        where = pl.ds(pl.multiple_of(where_ref[k] * width, width), width)
        copies.append(pltpu.make_async_copy(buf.at[k], out_hbm.at[:, where], sems.at[k]))
        copies[k].start()
    for copy in copies:
        copy.wait()


def finish(inverse, sources, pieces, width, total, before=None):
    rank = inverse.shape[0]
    count = len(pieces)
    in_specs = [TABLE, WHOLE, *[WHOLE] * len(sources)]
    args = [jnp.stack([piece[0] for piece in pieces]), inverse, *sources]
    aliases = {}
    if before is not None:
        in_specs.append(HBM)
        args.append(before)
        aliases = {len(args) - 1: 0}
    return pl.pallas_call(
        functools.partial(finish_kernel, [piece[1:] for piece in pieces]),
        in_specs=in_specs,
        out_specs=HBM,
        out_shape=jax.ShapeDtypeStruct((rank, total), F32),
        scratch_shapes=[
            pltpu.VMEM((count, rank, width), F32),
            pltpu.SemaphoreType.DMA((count,)),
        ],
        input_output_aliases=aliases,
        compiler_params=PARAMS,
        cost_estimate=pl.CostEstimate(
            flops=6 * rank * rank * width * count,
            bytes_accessed=8 * rank * width * count,
            transcendentals=0,
        ),
        name="finish",
    )(*args)


def body(n_pos, n_pix, probes, sketch):
    def swap(value, axis, size, bit):
        return lax.ppermute(value, axis, [(i, i ^ bit) for i in range(size)])

    def over(value, bit):
        return swap(value, "pos", n_pos, bit)

    me = lax.axis_index("pos").astype(jnp.int32)
    near, far = me & 1, (me >> 1) & 1
    cols = probes.shape[1]
    width = cols // (8 * CHUNKS)

    tall = tall_partial(probes, sketch.T)
    bit = 1
    while 2 * bit < n_pix:
        tall = tall + swap(tall, "pix", n_pix, bit)
        bit *= 2
    other = swap(tall, "pix", n_pix, bit)

    def block_a(c, p, q):
        return 8 * c + 2 * (near ^ p) + (far ^ q)

    def block_b(c, p, q):
        return 8 * c + 4 + 2 * (far ^ p) + (near ^ q)

    def outputs(c, p):
        return [
            ([block_a(c, p, 1), block_a(c, p, 0)], c == 0),
            ([block_b(c, p, 1), block_b(c, p, 0)], False),
        ]

    both, gram, away = first_products(tall, other, probes, outputs(0, 1), width)

    inverse, out, after = None, None, away[0]
    for c in range(CHUNKS):
        g = LANES if c == 0 else 0
        last = c == CHUNKS - 1
        made = rest_products(
            both, gram, probes, outputs(c, 0) + ([] if last else outputs(c + 1, 1)), width, after
        )
        away_a, away_b = away
        (own_a, own_b), away = made[:2], made[2:]
        got_a = over(away_a, 1)
        sum_a = own_a + got_a
        sum_b = own_b + over(away_b, 2)
        after = got_a
        send_a, send_b = sum_a[:, : width + g], sum_b[:, :width]
        if c > 0:
            send_a, send_b, whole = lax.optimization_barrier((send_a, send_b, whole))
        got_a = over(send_a, 2)
        got_b = over(send_b, 1)
        whole = jnp.concatenate(
            [
                sum_a[:, width + g :] + got_a[:, :width],
                sum_a[:, width : width + g] + got_a[:, width:],
                sum_b[:, width:] + got_b,
            ],
            axis=1,
        )
        total = whole
        bit = 4
        while bit < n_pos:
            total = total + over(total, bit)
            bit *= 2
        if c == 0:
            inverse = inverse_factor(total, width)
        mine_a, mine_b = total[:, :width], total[:, width + g :]
        if c > 0:
            mine_a, mine_b, inverse = lax.optimization_barrier((mine_a, mine_b, inverse))
        next_a = over(mine_a, 2)
        next_b = over(mine_b, 1)
        last_a = over(jnp.concatenate([mine_a, next_a], axis=1), 1)
        last_b = over(jnp.concatenate([mine_b, next_b], axis=1), 2)
        sources = [total, next_a, next_b]
        pieces = [
            (block_a(c, 0, 0), 0, 0),
            (block_b(c, 0, 0), 0, width + g),
            (block_a(c, 0, 1), 1, 0),
            (block_b(c, 0, 1), 2, 0),
        ]
        if last:
            out = finish(inverse, sources, pieces, width, cols, out)
            sources, pieces = [], []
        k = len(sources)
        sources += [last_a, last_b]
        pieces += [
            (block_a(c, 1, 0), k, 0),
            (block_a(c, 1, 1), k, width),
            (block_b(c, 1, 0), k + 1, 0),
            (block_b(c, 1, 1), k + 1, width),
        ]
        out = finish(inverse, sources, pieces, width, cols, out)
    return out


def solution(mesh):
    in_specs = (P("pos", "pix"), P("pix", None))
    out_specs = P(None, "pix")
    run = functools.partial(body, mesh.shape["pos"], mesh.shape["pix"])
    return jax.shard_map(run, mesh=mesh, in_specs=in_specs, out_specs=out_specs, check_vma=False)
```

```python
import functools

import jax
import jax.numpy as jnp
from jax import lax
from jax.experimental import pallas as pl
from jax.experimental.pallas import tpu as pltpu
from jax.sharding import PartitionSpec as P

F32 = jnp.float32
BF16 = jnp.bfloat16
VMEM_LIMIT = 40 * 1024 * 1024
LANES = 128
CHUNKS = 2
AHEAD = 8
UNIT = 512
PANEL = 4
LAST = (((1,), (1,)), ((), ()))
PLAIN = (((1,), (0,)), ((), ()))
ANYWHERE = pl.BlockSpec(memory_space=pl.ANY)
HBM = pl.BlockSpec(memory_space=pltpu.MemorySpace.HBM)
WHOLE = pl.BlockSpec(memory_space=pltpu.VMEM)
TABLE = pl.BlockSpec(memory_space=pltpu.SMEM)
PARAMS = pltpu.CompilerParams(vmem_limit_bytes=VMEM_LIMIT)


def split(x):
    head = x.astype(BF16)
    return head, (x - head.astype(F32)).astype(BF16)


def dot(a, b, dims):
    return lax.dot_general(a, b, dims, preferred_element_type=F32)


def in_hbm(x):
    return pltpu.with_memory_space_constraint(x, pltpu.MemorySpace.HBM)


def stream(copies, use):
    for copy in copies[:AHEAD]:
        copy.start()
    for k, copy in enumerate(copies):
        copy.wait()
        if k + AHEAD < len(copies):
            copies[k + AHEAD].start()
        use(k)


def tall_kernel(x_hbm, s_hbm, out_ref, x_buf, s_buf, x_sems, s_sem):
    blocks, _, unit = x_buf.shape
    rank = s_hbm.shape[0]
    copies = [
        pltpu.make_async_copy(x_hbm.at[:, pl.ds(k * unit, unit)], x_buf.at[k], x_sems.at[k])
        for k in range(blocks)
    ]
    sketch = pltpu.make_async_copy(s_hbm, s_buf, s_sem)
    sketch.start()

    def use(k):
        if k == 0:
            sketch.wait()
        s_head, s_rest = split(s_buf[:, k * unit : (k + 1) * unit])
        s_both = jnp.concatenate([s_head, s_rest], axis=0)
        x_head, x_rest = split(x_buf[k])
        both = dot(s_both, x_head, LAST)
        part = both[:rank] + (both[rank:] + dot(s_head, x_rest, LAST))
        if k == 0:
            out_ref[...] = part
        else:
            out_ref[...] += part

    stream(copies, use)


def tall_partial(probes, sketch_t):
    rows, cols = probes.shape
    rank = sketch_t.shape[0]
    unit = min(2 * UNIT, cols)
    blocks = cols // unit
    return pl.pallas_call(
        tall_kernel,
        in_specs=[HBM, HBM],
        out_specs=WHOLE,
        out_shape=jax.ShapeDtypeStruct((rank, rows), F32),
        scratch_shapes=[
            pltpu.VMEM((blocks, rows, unit), F32),
            pltpu.VMEM((rank, cols), F32),
            pltpu.SemaphoreType.DMA((blocks,)),
            pltpu.SemaphoreType.DMA,
        ],
        compiler_params=PARAMS,
        cost_estimate=pl.CostEstimate(
            flops=6 * rows * cols * rank, bytes_accessed=4 * rows * cols, transcendentals=0
        ),
        name="tall_partial",
    )(in_hbm(probes), in_hbm(sketch_t))


def multiply_blocks(both_ref, which_ref, x_hbm, x_buf, sems, plan, outs):
    rank = outs[0].shape[0]
    unit = x_buf.shape[2]
    copies = [
        pltpu.make_async_copy(
            x_hbm.at[:, pl.ds(pl.multiple_of(which_ref[k] * unit, unit), unit)],
            x_buf.at[k],
            sems.at[k],
        )
        for k in range(len(plan))
    ]

    def use(k):
        both = both_ref[...]
        x_head, x_rest = split(x_buf[k])
        first = dot(both, x_head, PLAIN)
        second = dot(both[:rank], x_rest, PLAIN)
        out, offset = plan[k]
        outs[out][:, offset : offset + unit] = first[:rank] + (first[rank:] + second)

    return copies, use


def first_kernel(plan, grams, which_ref, one_ref, two_ref, x_hbm, both_ref, gram_ref, *refs):
    outs, (x_buf, sems) = refs[:-2], refs[-2:]
    copies, use = multiply_blocks(both_ref, which_ref, x_hbm, x_buf, sems, plan, outs)

    def use_first(k):
        if k == 0:
            tall = one_ref[...] + two_ref[...]
            head, rest = split(tall)
            both_ref[...] = jnp.concatenate([head, rest], axis=0)
        use(k)

    stream(copies, use_first)
    tall = one_ref[...] + two_ref[...]
    r = tall.shape[0]
    head, rest = split(tall)
    tail = (tall - head.astype(F32) - rest.astype(F32)).astype(BF16)
    three = jnp.concatenate([head, rest, tail], axis=0)
    g = dot(three, three, LAST)
    cross = g[:r, r : 2 * r] + g[r : 2 * r, :r]
    small = g[:r, 2 * r :] + g[2 * r :, :r] + g[r : 2 * r, r : 2 * r]
    gram = g[:r, :r] + (cross + small)
    gram_ref[...] = jnp.concatenate([gram, jnp.zeros((r, LANES - r), F32)], axis=1)
    for out, offset in grams:
        outs[out][:, offset : offset + LANES] = gram_ref[...]


def rest_kernel(plan, grams, which_ref, both_ref, gram_ref, x_hbm, after_ref, *refs):
    outs, (x_buf, sems) = refs[:-2], refs[-2:]
    copies, use = multiply_blocks(both_ref, which_ref, x_hbm, x_buf, sems, plan, outs)
    stream(copies, use)
    for out, offset in grams:
        outs[out][:, offset : offset + LANES] = gram_ref[...]


def layout(outputs, sub):
    unit = min(UNIT, sub)
    plan, grams, widths, which = [], [], [], []
    for out, (blocks, with_gram) in enumerate(outputs):
        extra = LANES if with_gram else 0
        for j, block in enumerate(blocks):
            for part in range(sub // unit):
                plan.append((out, j * sub + part * unit + (extra if j else 0)))
                which.append(block * (sub // unit) + part)
        if with_gram:
            grams.append((out, sub))
        widths.append(len(blocks) * sub + extra)
    return unit, plan, grams, widths, jnp.stack(which)


def products(kernel, inputs, in_specs, made, probes, outputs, sub, name):
    rows = probes.shape[0]
    rank = inputs[1].shape[0]
    unit, plan, grams, widths, which = layout(outputs, sub)
    shapes = [*made, *[jax.ShapeDtypeStruct((rank, width), F32) for width in widths]]
    return pl.pallas_call(
        functools.partial(kernel, plan, grams),
        in_specs=[TABLE, *in_specs],
        out_specs=[WHOLE] * len(shapes),
        out_shape=shapes,
        scratch_shapes=[
            pltpu.VMEM((len(plan), rows, unit), F32),
            pltpu.SemaphoreType.DMA((len(plan),)),
        ],
        compiler_params=PARAMS,
        cost_estimate=pl.CostEstimate(
            flops=6 * rows * rank * unit * len(plan),
            bytes_accessed=4 * rows * unit * len(plan),
            transcendentals=0,
        ),
        name=name,
    )(which, *inputs)


def first_products(one, two, probes, outputs, sub):
    rank, rows = one.shape
    made = [
        jax.ShapeDtypeStruct((2 * rank, rows), BF16),
        jax.ShapeDtypeStruct((rank, LANES), F32),
    ]
    both, gram, *outs = products(
        first_kernel,
        [one, two, in_hbm(probes)],
        [WHOLE, WHOLE, HBM],
        made,
        probes,
        outputs,
        sub,
        "first_products",
    )
    return both, gram, outs


def rest_products(both, gram, probes, outputs, sub, after):
    return products(
        rest_kernel,
        [both, gram, in_hbm(probes), after],
        [WHOLE, WHOLE, HBM, ANYWHERE],
        [],
        probes,
        outputs,
        sub,
        "rest_products",
    )


def inverse_kernel(gram_ref, out_ref):
    rank = out_ref.shape[0]
    rows = lax.broadcasted_iota(jnp.int32, (rank, LANES), 0)
    cols = lax.broadcasted_iota(jnp.int32, (rank, LANES), 1)
    work = jnp.where(cols < rank, gram_ref[...], (cols == rows + rank).astype(F32))
    scale = jnp.ones((rank, LANES), F32)
    for start in range(0, rank, PANEL):
        panel = [
            jnp.broadcast_to(work[:, k : k + 1], (rank, LANES))
            for k in range(start, start + PANEL)
        ]
        for j in range(PANEL):
            k = start + j
            over = 1.0 / panel[j][k : k + 1, :]
            scale = jnp.where(rows == k, over, scale)
            factor = jnp.where(rows > k, panel[j] * over, 0.0)
            work = work - factor * work[k : k + 1, :]
            for later in range(j + 1, PANEL):
                panel[later] = panel[later] - factor * panel[later][k : k + 1, :]
    out_ref[...] = (work * jnp.sqrt(scale))[:, rank : 2 * rank]


def inverse_factor(chunk, start):
    rank = chunk.shape[0]
    return pl.pallas_call(
        inverse_kernel,
        grid=(1,),
        in_specs=[pl.BlockSpec((rank, LANES), lambda i: (0, start // LANES))],
        out_specs=pl.BlockSpec((rank, rank), lambda i: (0, 0)),
        out_shape=jax.ShapeDtypeStruct((rank, rank), F32),
        compiler_params=PARAMS,
        cost_estimate=pl.CostEstimate(
            flops=20_000_000, bytes_accessed=8 * rank * LANES, transcendentals=rank
        ),
        name="inverse_factor",
    )(chunk)


def finish_kernel(plan, where_ref, inverse_ref, *refs):
    out_hbm, buf, sems = refs[-3:]
    _, rank, width = buf.shape
    head, rest = split(inverse_ref[...])
    both = jnp.concatenate([head, rest], axis=0)
    copies = []
    for k, (source, offset) in enumerate(plan):
        p_head, p_rest = split(refs[source][:, offset : offset + width])
        first = dot(both, p_head, PLAIN)
        buf[k] = first[:rank] + (first[rank:] + dot(head, p_rest, PLAIN))
        where = pl.ds(pl.multiple_of(where_ref[k] * width, width), width)
        copies.append(pltpu.make_async_copy(buf.at[k], out_hbm.at[:, where], sems.at[k]))
        copies[k].start()
    for copy in copies:
        copy.wait()


def finish(inverse, sources, pieces, width, total, before=None):
    rank = inverse.shape[0]
    count = len(pieces)
    in_specs = [TABLE, WHOLE, *[WHOLE] * len(sources)]
    args = [jnp.stack([piece[0] for piece in pieces]), inverse, *sources]
    aliases = {}
    if before is not None:
        in_specs.append(HBM)
        args.append(before)
        aliases = {len(args) - 1: 0}
    return pl.pallas_call(
        functools.partial(finish_kernel, [piece[1:] for piece in pieces]),
        in_specs=in_specs,
        out_specs=HBM,
        out_shape=jax.ShapeDtypeStruct((rank, total), F32),
        scratch_shapes=[
            pltpu.VMEM((count, rank, width), F32),
            pltpu.SemaphoreType.DMA((count,)),
        ],
        input_output_aliases=aliases,
        compiler_params=PARAMS,
        cost_estimate=pl.CostEstimate(
            flops=6 * rank * rank * width * count,
            bytes_accessed=8 * rank * width * count,
            transcendentals=0,
        ),
        name="finish",
    )(*args)


def body(n_pos, n_pix, probes, sketch):
    def swap(value, axis, size, bit):
        return lax.ppermute(value, axis, [(i, i ^ bit) for i in range(size)])

    def over(value, bit):
        return swap(value, "pos", n_pos, bit)

    me = lax.axis_index("pos").astype(jnp.int32)
    near, far = me & 1, (me >> 1) & 1
    cols = probes.shape[1]
    width = cols // (8 * CHUNKS)

    tall = tall_partial(probes, sketch.T)
    bit = 1
    while 2 * bit < n_pix:
        tall = tall + swap(tall, "pix", n_pix, bit)
        bit *= 2
    other = swap(tall, "pix", n_pix, bit)

    def block_a(c, p, q):
        return 8 * c + 2 * (near ^ p) + (far ^ q)

    def block_b(c, p, q):
        return 8 * c + 4 + 2 * (far ^ p) + (near ^ q)

    def outputs(c, p):
        return [
            ([block_a(c, p, 1), block_a(c, p, 0)], c == 0),
            ([block_b(c, p, 1), block_b(c, p, 0)], False),
        ]

    both, gram, away = first_products(tall, other, probes, outputs(0, 1), width)

    def after(value, *others):
        return lax.optimization_barrier((value, *others))[0]

    whole, total = [], []
    ready = away[0]
    for c in range(CHUNKS):
        g = LANES if c == 0 else 0
        more = outputs(c + 1, 1) if c + 1 < CHUNKS else []
        made = rest_products(both, gram, probes, outputs(c, 0) + more, width, ready)
        away_a, away_b = away
        (own_a, own_b), away = made[:2], made[2:]
        if c > 0:
            away_a, away_b = after(away_a, whole[-1]), after(away_b, whole[-1])
        ready = over(away_a, 1)
        sum_a = own_a + ready
        sum_b = own_b + over(away_b, 2)
        got_a = over(sum_a[:, : width + g], 2)
        got_b = over(sum_b[:, :width], 1)
        whole.append(
            jnp.concatenate(
                [
                    sum_a[:, width + g :] + got_a[:, :width],
                    sum_a[:, width : width + g] + got_a[:, width:],
                    sum_b[:, width:] + got_b,
                ],
                axis=1,
            )
        )
        added = whole[-1]
        bit = 4
        while bit < n_pos:
            added = added + over(added, bit)
            bit *= 2
        total.append(added)

    out, inverse, done = None, None, ()
    for c in range(CHUNKS):
        g = LANES if c == 0 else 0
        mine_a, mine_b = total[c][:, :width], total[c][:, width + g :]
        wait = whole[c + 1 : c + 2] + ([] if c == 0 else [inverse, *done])
        if wait:
            mine_a, mine_b = after(mine_a, *wait), after(mine_b, *wait)
        next_a = over(mine_a, 2)
        next_b = over(mine_b, 1)
        done = (next_a, next_b)
        if c == 0:
            inverse = inverse_factor(after(total[0], *done), width)
        last_a = over(jnp.concatenate([mine_a, next_a], axis=1), 1)
        last_b = over(jnp.concatenate([mine_b, next_b], axis=1), 2)
        out = finish(
            inverse,
            [total[c], next_a, next_b, last_a, last_b],
            [
                (block_a(c, 0, 0), 0, 0),
                (block_b(c, 0, 0), 0, width + g),
                (block_a(c, 0, 1), 1, 0),
                (block_b(c, 0, 1), 2, 0),
                (block_a(c, 1, 0), 3, 0),
                (block_a(c, 1, 1), 3, width),
                (block_b(c, 1, 0), 4, 0),
                (block_b(c, 1, 1), 4, width),
            ],
            width,
            cols,
            out,
        )
    return out


def solution(mesh):
    in_specs = (P("pos", "pix"), P("pix", None))
    out_specs = P(None, "pix")
    run = functools.partial(body, mesh.shape["pos"], mesh.shape["pix"])
    return jax.shard_map(run, mesh=mesh, in_specs=in_specs, out_specs=out_specs, check_vma=False)
```

```python
import functools

import jax
import jax.numpy as jnp
from jax import lax
from jax.experimental import pallas as pl
from jax.experimental.pallas import tpu as pltpu
from jax.sharding import PartitionSpec as P

F32 = jnp.float32
BF16 = jnp.bfloat16
VMEM_LIMIT = 40 * 1024 * 1024
LANES = 128
CHUNKS = 2
AHEAD = 8
UNIT = 512
TILE = 256
PANEL = 4
LAST = (((1,), (1,)), ((), ()))
PLAIN = (((1,), (0,)), ((), ()))
ANYWHERE = pl.BlockSpec(memory_space=pl.ANY)
HBM = pl.BlockSpec(memory_space=pltpu.MemorySpace.HBM)
WHOLE = pl.BlockSpec(memory_space=pltpu.VMEM)
TABLE = pl.BlockSpec(memory_space=pltpu.SMEM)
PARAMS = pltpu.CompilerParams(vmem_limit_bytes=VMEM_LIMIT)


def split(x):
    head = x.astype(BF16)
    return head, (x - head.astype(F32)).astype(BF16)


def dot(a, b, dims):
    return lax.dot_general(a, b, dims, preferred_element_type=F32)


def tiles(size):
    step = min(TILE, size)
    return [slice(start, start + step) for start in range(0, size, step)]


def in_hbm(x):
    return pltpu.with_memory_space_constraint(x, pltpu.MemorySpace.HBM)


def stream(copies, use):
    for copy in copies[:AHEAD]:
        copy.start()
    for k, copy in enumerate(copies):
        copy.wait()
        if k + AHEAD < len(copies):
            copies[k + AHEAD].start()
        use(k)


def tall_kernel(x_hbm, s_hbm, out_ref, x_buf, s_buf, x_sems, s_sem):
    blocks, _, unit = x_buf.shape
    rank = s_hbm.shape[0]
    copies = [
        pltpu.make_async_copy(x_hbm.at[:, pl.ds(k * unit, unit)], x_buf.at[k], x_sems.at[k])
        for k in range(blocks)
    ]
    sketch = pltpu.make_async_copy(s_hbm, s_buf, s_sem)
    sketch.start()

    def use(k):
        if k == 0:
            sketch.wait()
        s_head, s_rest = split(s_buf[:, k * unit : (k + 1) * unit])
        s_both = jnp.concatenate([s_head, s_rest], axis=0)
        for rows in tiles(x_buf.shape[1]):
            total = None
            for cols in tiles(unit):
                x_head, x_rest = split(x_buf[k, rows, cols])
                both = dot(s_both[:, cols], x_head, LAST)
                part = both[:rank] + (both[rank:] + dot(s_head[:, cols], x_rest, LAST))
                total = part if total is None else total + part
            if k == 0:
                out_ref[:, rows] = total
            else:
                out_ref[:, rows] += total

    stream(copies, use)


def tall_partial(probes, sketch_t):
    rows, cols = probes.shape
    rank = sketch_t.shape[0]
    unit = min(UNIT, cols)
    blocks = cols // unit
    return pl.pallas_call(
        tall_kernel,
        in_specs=[HBM, HBM],
        out_specs=WHOLE,
        out_shape=jax.ShapeDtypeStruct((rank, rows), F32),
        scratch_shapes=[
            pltpu.VMEM((blocks, rows, unit), F32),
            pltpu.VMEM((rank, cols), F32),
            pltpu.SemaphoreType.DMA((blocks,)),
            pltpu.SemaphoreType.DMA,
        ],
        compiler_params=PARAMS,
        cost_estimate=pl.CostEstimate(
            flops=6 * rows * cols * rank, bytes_accessed=4 * rows * cols, transcendentals=0
        ),
        name="tall_partial",
    )(in_hbm(probes), in_hbm(sketch_t))


def multiply_blocks(both_ref, which_ref, x_hbm, x_buf, sems, plan, outs):
    rank = outs[0].shape[0]
    unit = x_buf.shape[2]
    copies = [
        pltpu.make_async_copy(
            x_hbm.at[:, pl.ds(pl.multiple_of(which_ref[k] * unit, unit), unit)],
            x_buf.at[k],
            sems.at[k],
        )
        for k in range(len(plan))
    ]

    def use(k):
        out, offset = plan[k]
        for cols in tiles(unit):
            total = None
            for rows in tiles(x_buf.shape[1]):
                x_head, x_rest = split(x_buf[k, rows, cols])
                both = dot(both_ref[:, rows], x_head, PLAIN)
                part = both[:rank] + (both[rank:] + dot(both_ref[:rank, rows], x_rest, PLAIN))
                total = part if total is None else total + part
            outs[out][:, offset + cols.start : offset + cols.stop] = total

    return copies, use


def first_kernel(plan, grams, which_ref, one_ref, two_ref, x_hbm, both_ref, gram_ref, *refs):
    outs, (x_buf, sems) = refs[:-2], refs[-2:]
    copies, use = multiply_blocks(both_ref, which_ref, x_hbm, x_buf, sems, plan, outs)

    def use_first(k):
        if k == 0:
            tall = one_ref[...] + two_ref[...]
            head, rest = split(tall)
            both_ref[...] = jnp.concatenate([head, rest], axis=0)
        use(k)

    stream(copies, use_first)
    tall = one_ref[...] + two_ref[...]
    r = tall.shape[0]
    head, rest = split(tall)
    tail = (tall - head.astype(F32) - rest.astype(F32)).astype(BF16)
    three = jnp.concatenate([head, rest, tail], axis=0)
    g = dot(three, three, LAST)
    cross = g[:r, r : 2 * r] + g[r : 2 * r, :r]
    small = g[:r, 2 * r :] + g[2 * r :, :r] + g[r : 2 * r, r : 2 * r]
    gram = g[:r, :r] + (cross + small)
    gram_ref[...] = jnp.concatenate([gram, jnp.zeros((r, LANES - r), F32)], axis=1)
    for out, offset in grams:
        outs[out][:, offset : offset + LANES] = gram_ref[...]


def rest_kernel(plan, grams, which_ref, both_ref, gram_ref, x_hbm, after_ref, *refs):
    outs, (x_buf, sems) = refs[:-2], refs[-2:]
    copies, use = multiply_blocks(both_ref, which_ref, x_hbm, x_buf, sems, plan, outs)
    stream(copies, use)
    for out, offset in grams:
        outs[out][:, offset : offset + LANES] = gram_ref[...]


def layout(outputs, sub):
    unit = min(UNIT, sub)
    plan, grams, widths, which = [], [], [], []
    for out, (blocks, with_gram) in enumerate(outputs):
        extra = LANES if with_gram else 0
        for j, block in enumerate(blocks):
            for part in range(sub // unit):
                plan.append((out, j * sub + part * unit + (extra if j else 0)))
                which.append(block * (sub // unit) + part)
        if with_gram:
            grams.append((out, sub))
        widths.append(len(blocks) * sub + extra)
    return unit, plan, grams, widths, jnp.stack(which)


def products(kernel, inputs, in_specs, made, probes, outputs, sub, name):
    rows = probes.shape[0]
    rank = inputs[1].shape[0]
    unit, plan, grams, widths, which = layout(outputs, sub)
    shapes = [*made, *[jax.ShapeDtypeStruct((rank, width), F32) for width in widths]]
    return pl.pallas_call(
        functools.partial(kernel, plan, grams),
        in_specs=[TABLE, *in_specs],
        out_specs=[WHOLE] * len(shapes),
        out_shape=shapes,
        scratch_shapes=[
            pltpu.VMEM((len(plan), rows, unit), F32),
            pltpu.SemaphoreType.DMA((len(plan),)),
        ],
        compiler_params=PARAMS,
        cost_estimate=pl.CostEstimate(
            flops=6 * rows * rank * unit * len(plan),
            bytes_accessed=4 * rows * unit * len(plan),
            transcendentals=0,
        ),
        name=name,
    )(which, *inputs)


def first_products(one, two, probes, outputs, sub):
    rank, rows = one.shape
    made = [
        jax.ShapeDtypeStruct((2 * rank, rows), BF16),
        jax.ShapeDtypeStruct((rank, LANES), F32),
    ]
    both, gram, *outs = products(
        first_kernel,
        [one, two, in_hbm(probes)],
        [WHOLE, WHOLE, HBM],
        made,
        probes,
        outputs,
        sub,
        "first_products",
    )
    return both, gram, outs


def rest_products(both, gram, probes, outputs, sub, after):
    return products(
        rest_kernel,
        [both, gram, in_hbm(probes), after],
        [WHOLE, WHOLE, HBM, ANYWHERE],
        [],
        probes,
        outputs,
        sub,
        "rest_products",
    )


def inverse_kernel(gram_ref, out_ref):
    rank = out_ref.shape[0]
    rows = lax.broadcasted_iota(jnp.int32, (rank, LANES), 0)
    cols = lax.broadcasted_iota(jnp.int32, (rank, LANES), 1)
    work = jnp.where(cols < rank, gram_ref[...], (cols == rows + rank).astype(F32))
    scale = jnp.ones((rank, LANES), F32)
    for start in range(0, rank, PANEL):
        panel = [
            jnp.broadcast_to(work[:, k : k + 1], (rank, LANES))
            for k in range(start, start + PANEL)
        ]
        for j in range(PANEL):
            k = start + j
            over = 1.0 / panel[j][k : k + 1, :]
            scale = jnp.where(rows == k, over, scale)
            factor = jnp.where(rows > k, panel[j] * over, 0.0)
            work = work - factor * work[k : k + 1, :]
            for later in range(j + 1, PANEL):
                panel[later] = panel[later] - factor * panel[later][k : k + 1, :]
    out_ref[...] = (work * jnp.sqrt(scale))[:, rank : 2 * rank]


def inverse_factor(chunk, start):
    rank = chunk.shape[0]
    return pl.pallas_call(
        inverse_kernel,
        grid=(1,),
        in_specs=[pl.BlockSpec((rank, LANES), lambda i: (0, start // LANES))],
        out_specs=pl.BlockSpec((rank, rank), lambda i: (0, 0)),
        out_shape=jax.ShapeDtypeStruct((rank, rank), F32),
        compiler_params=PARAMS,
        cost_estimate=pl.CostEstimate(
            flops=20_000_000, bytes_accessed=8 * rank * LANES, transcendentals=rank
        ),
        name="inverse_factor",
    )(chunk)


def finish_kernel(plan, where_ref, inverse_ref, *refs):
    out_hbm, buf, sems = refs[-3:]
    _, rank, width = buf.shape
    head, rest = split(inverse_ref[...])
    both = jnp.concatenate([head, rest], axis=0)
    copies = []
    for k, (source, offset) in enumerate(plan):
        p_head, p_rest = split(refs[source][:, offset : offset + width])
        first = dot(both, p_head, PLAIN)
        buf[k] = first[:rank] + (first[rank:] + dot(head, p_rest, PLAIN))
        where = pl.ds(pl.multiple_of(where_ref[k] * width, width), width)
        copies.append(pltpu.make_async_copy(buf.at[k], out_hbm.at[:, where], sems.at[k]))
        copies[k].start()
    for copy in copies:
        copy.wait()


def finish(inverse, sources, pieces, width, total, before=None):
    rank = inverse.shape[0]
    count = len(pieces)
    in_specs = [TABLE, WHOLE, *[WHOLE] * len(sources)]
    args = [jnp.stack([piece[0] for piece in pieces]), inverse, *sources]
    aliases = {}
    if before is not None:
        in_specs.append(HBM)
        args.append(before)
        aliases = {len(args) - 1: 0}
    return pl.pallas_call(
        functools.partial(finish_kernel, [piece[1:] for piece in pieces]),
        in_specs=in_specs,
        out_specs=HBM,
        out_shape=jax.ShapeDtypeStruct((rank, total), F32),
        scratch_shapes=[
            pltpu.VMEM((count, rank, width), F32),
            pltpu.SemaphoreType.DMA((count,)),
        ],
        input_output_aliases=aliases,
        compiler_params=PARAMS,
        cost_estimate=pl.CostEstimate(
            flops=6 * rank * rank * width * count,
            bytes_accessed=8 * rank * width * count,
            transcendentals=0,
        ),
        name="finish",
    )(*args)


def body(n_pos, n_pix, probes, sketch):
    def swap(value, axis, size, bit):
        return lax.ppermute(value, axis, [(i, i ^ bit) for i in range(size)])

    def over(value, bit):
        return swap(value, "pos", n_pos, bit)

    me = lax.axis_index("pos").astype(jnp.int32)
    near, far = me & 1, (me >> 1) & 1
    cols = probes.shape[1]
    width = cols // (8 * CHUNKS)

    tall = tall_partial(probes, sketch.T)
    bit = 1
    while 2 * bit < n_pix:
        tall = tall + swap(tall, "pix", n_pix, bit)
        bit *= 2
    other = swap(tall, "pix", n_pix, bit)

    def block_a(c, p, q):
        return 8 * c + 2 * (near ^ p) + (far ^ q)

    def block_b(c, p, q):
        return 8 * c + 4 + 2 * (far ^ p) + (near ^ q)

    def outputs(c, p):
        return [
            ([block_a(c, p, 1), block_a(c, p, 0)], c == 0),
            ([block_b(c, p, 1), block_b(c, p, 0)], False),
        ]

    both, gram, away = first_products(tall, other, probes, outputs(0, 1), width)

    def after(value, *others):
        return lax.optimization_barrier((value, *others))[0]

    whole, total = [], []
    ready = away[0]
    for c in range(CHUNKS):
        g = LANES if c == 0 else 0
        more = outputs(c + 1, 1) if c + 1 < CHUNKS else []
        made = rest_products(both, gram, probes, outputs(c, 0) + more, width, ready)
        away_a, away_b = away
        (own_a, own_b), away = made[:2], made[2:]
        if c > 0:
            away_a, away_b = after(away_a, whole[-1]), after(away_b, whole[-1])
        ready = over(away_a, 1)
        sum_a = own_a + ready
        sum_b = own_b + over(away_b, 2)
        got_a = over(sum_a[:, : width + g], 2)
        got_b = over(sum_b[:, :width], 1)
        whole.append(
            jnp.concatenate(
                [
                    sum_a[:, width + g :] + got_a[:, :width],
                    sum_a[:, width : width + g] + got_a[:, width:],
                    sum_b[:, width:] + got_b,
                ],
                axis=1,
            )
        )
        added = whole[-1]
        bit = 4
        while bit < n_pos:
            added = added + over(added, bit)
            bit *= 2
        total.append(added)

    out, inverse = None, None
    for c in range(CHUNKS):
        g = LANES if c == 0 else 0
        mine_a, mine_b = total[c][:, :width], total[c][:, width + g :]
        wait = whole[c + 1 : c + 2] + ([] if c == 0 else [inverse, last_a, last_b])
        if wait:
            mine_a, mine_b = after(mine_a, *wait), after(mine_b, *wait)
        next_a = over(mine_a, 2)
        next_b = over(mine_b, 1)
        if c == 0:
            inverse = inverse_factor(after(total[0], next_a, next_b), width)
        last_a = over(jnp.concatenate([mine_a, next_a], axis=1), 1)
        last_b = over(jnp.concatenate([mine_b, next_b], axis=1), 2)
        out = finish(
            inverse,
            [total[c], next_a, next_b, last_a, last_b],
            [
                (block_a(c, 0, 0), 0, 0),
                (block_b(c, 0, 0), 0, width + g),
                (block_a(c, 0, 1), 1, 0),
                (block_b(c, 0, 1), 2, 0),
                (block_a(c, 1, 0), 3, 0),
                (block_a(c, 1, 1), 3, width),
                (block_b(c, 1, 0), 4, 0),
                (block_b(c, 1, 1), 4, width),
            ],
            width,
            cols,
            out,
        )
    return out


def solution(mesh):
    in_specs = (P("pos", "pix"), P("pix", None))
    out_specs = P(None, "pix")
    run = functools.partial(body, mesh.shape["pos"], mesh.shape["pix"])
    return jax.shard_map(run, mesh=mesh, in_specs=in_specs, out_specs=out_specs, check_vma=False)
```

```python
import functools

import jax
import jax.numpy as jnp
from jax import lax
from jax.experimental import pallas as pl
from jax.experimental.pallas import tpu as pltpu
from jax.sharding import PartitionSpec as P

F32 = jnp.float32
BF16 = jnp.bfloat16
VMEM_LIMIT = 40 * 1024 * 1024
LANES = 128
CHUNKS = 1
AHEAD = 8
UNIT = 512
TILE = 256
PANEL = 4
LAST = (((1,), (1,)), ((), ()))
PLAIN = (((1,), (0,)), ((), ()))
ANYWHERE = pl.BlockSpec(memory_space=pl.ANY)
HBM = pl.BlockSpec(memory_space=pltpu.MemorySpace.HBM)
WHOLE = pl.BlockSpec(memory_space=pltpu.VMEM)
TABLE = pl.BlockSpec(memory_space=pltpu.SMEM)
PARAMS = pltpu.CompilerParams(vmem_limit_bytes=VMEM_LIMIT)


def split(x):
    head = x.astype(BF16)
    return head, (x - head.astype(F32)).astype(BF16)


def dot(a, b, dims):
    return lax.dot_general(a, b, dims, preferred_element_type=F32)


def tiles(size):
    step = min(TILE, size)
    return [slice(start, start + step) for start in range(0, size, step)]


def in_hbm(x):
    return pltpu.with_memory_space_constraint(x, pltpu.MemorySpace.HBM)


def stream(copies, use):
    for copy in copies[:AHEAD]:
        copy.start()
    for k, copy in enumerate(copies):
        copy.wait()
        if k + AHEAD < len(copies):
            copies[k + AHEAD].start()
        use(k)


def tall_kernel(x_hbm, s_hbm, out_ref, x_buf, s_buf, acc_ref, x_sems, s_sem):
    blocks, _, unit = x_buf.shape
    rank = s_hbm.shape[0]
    copies = [
        pltpu.make_async_copy(x_hbm.at[:, pl.ds(k * unit, unit)], x_buf.at[k], x_sems.at[k])
        for k in range(blocks)
    ]
    sketch = pltpu.make_async_copy(s_hbm, s_buf, s_sem)
    sketch.start()

    def use(k):
        if k == 0:
            sketch.wait()
        s_both = jnp.concatenate(split(s_buf[:, k * unit : (k + 1) * unit]), axis=0)
        x_head, x_rest = split(x_buf[k])
        part = dot(x_head, s_both, LAST) + dot(x_rest, s_both, LAST)
        if k == 0:
            acc_ref[...] = part
        else:
            acc_ref[...] += part

    stream(copies, use)
    acc = acc_ref[...].T
    out_ref[...] = acc[:rank] + acc[rank:]


def tall_partial(probes, sketch_t):
    rows, cols = probes.shape
    rank = sketch_t.shape[0]
    unit = min(UNIT, cols)
    blocks = cols // unit
    return pl.pallas_call(
        tall_kernel,
        in_specs=[HBM, HBM],
        out_specs=WHOLE,
        out_shape=jax.ShapeDtypeStruct((rank, rows), F32),
        scratch_shapes=[
            pltpu.VMEM((blocks, rows, unit), F32),
            pltpu.VMEM((rank, cols), F32),
            pltpu.VMEM((rows, 2 * rank), F32),
            pltpu.SemaphoreType.DMA((blocks,)),
            pltpu.SemaphoreType.DMA,
        ],
        compiler_params=PARAMS,
        cost_estimate=pl.CostEstimate(
            flops=8 * rows * cols * rank, bytes_accessed=4 * rows * cols, transcendentals=0
        ),
        name="tall_partial",
    )(in_hbm(probes), in_hbm(sketch_t))


def multiply_blocks(both_ref, which_ref, x_hbm, x_buf, sems, plan, outs):
    rank = outs[0].shape[0]
    unit = x_buf.shape[2]
    copies = [
        pltpu.make_async_copy(
            x_hbm.at[:, pl.ds(pl.multiple_of(which_ref[k] * unit, unit), unit)],
            x_buf.at[k],
            sems.at[k],
        )
        for k in range(len(plan))
    ]

    def use(k):
        out, offset = plan[k]
        for cols in tiles(unit):
            total = None
            for rows in tiles(x_buf.shape[1]):
                x_head, x_rest = split(x_buf[k, rows, cols])
                both = dot(both_ref[:, rows], x_head, PLAIN)
                part = both[:rank] + (both[rank:] + dot(both_ref[:rank, rows], x_rest, PLAIN))
                total = part if total is None else total + part
            outs[out][:, offset + cols.start : offset + cols.stop] = total

    return copies, use


def first_kernel(plan, early, grams, table, one_ref, two_ref, x_hbm, both_ref, gram_ref, *refs):
    outs, (x_buf, sems) = refs[:-2], refs[-2:]
    copies, use = multiply_blocks(both_ref, table, x_hbm, x_buf, sems, plan, outs)

    def use_first(k):
        if k == 0:
            tall = one_ref[...] + two_ref[...]
            head, rest = split(tall)
            both_ref[...] = jnp.concatenate([head, rest], axis=0)
        use(k)

    stream(copies[:early], use_first)

    @pl.when(table[len(plan)] == 1)
    def _():
        stream(copies[early:], lambda k: use(early + k))

    tall = one_ref[...] + two_ref[...]
    r = tall.shape[0]
    head, rest = split(tall)
    tail = (tall - head.astype(F32) - rest.astype(F32)).astype(BF16)
    three = jnp.concatenate([head, rest, tail], axis=0)
    g = dot(three, three, LAST)
    cross = g[:r, r : 2 * r] + g[r : 2 * r, :r]
    small = g[:r, 2 * r :] + g[2 * r :, :r] + g[r : 2 * r, r : 2 * r]
    gram = g[:r, :r] + (cross + small)
    gram_ref[...] = jnp.concatenate([gram, jnp.zeros((r, LANES - r), F32)], axis=1)
    for out, offset in grams:
        outs[out][:, offset : offset + LANES] = gram_ref[...]


def rest_kernel(plan, grams, table, both_ref, gram_ref, x_hbm, *refs):
    outs, (x_buf, sems) = refs[-4:-2], refs[-2:]
    copies, use = multiply_blocks(both_ref, table, x_hbm, x_buf, sems, plan, outs)

    @pl.when(table[len(plan)] == 0)
    def _():
        stream(copies, use)
        for out, offset in grams:
            outs[out][:, offset : offset + LANES] = gram_ref[...]

    @pl.when(table[len(plan)] == 1)
    def _():
        for out_ref, made_ref in zip(outs, refs[:2]):
            out_ref[...] = made_ref[...]


def layout(outputs, sub):
    unit = min(UNIT, sub)
    plan, grams, widths, which = [], [], [], []
    for out, (blocks, with_gram) in enumerate(outputs):
        extra = LANES if with_gram else 0
        for j, block in enumerate(blocks):
            for part in range(sub // unit):
                plan.append((out, j * sub + part * unit + (extra if j else 0)))
                which.append(block * (sub // unit) + part)
        if with_gram:
            grams.append((out, sub))
        widths.append(len(blocks) * sub + extra)
    return unit, plan, grams, widths, which


def product_call(kernel, inputs, in_specs, shapes, rows, unit, count, name):
    return pl.pallas_call(
        kernel,
        in_specs=[TABLE, *in_specs],
        out_specs=[WHOLE] * len(shapes),
        out_shape=shapes,
        scratch_shapes=[
            pltpu.VMEM((count, rows, unit), F32),
            pltpu.SemaphoreType.DMA((count,)),
        ],
        compiler_params=PARAMS,
        cost_estimate=pl.CostEstimate(
            flops=6 * rows * shapes[-1].shape[0] * unit * count,
            bytes_accessed=4 * rows * unit * count,
            transcendentals=0,
        ),
        name=name,
    )(*inputs)


def products(one, two, probes, away, own, sub, late):
    rank, rows = one.shape
    unit, plan, grams, widths, which = layout(away + own, sub)
    early = len(layout(away, sub)[1])
    chunks = [jax.ShapeDtypeStruct((rank, width), F32) for width in widths]
    made = [
        jax.ShapeDtypeStruct((2 * rank, rows), BF16),
        jax.ShapeDtypeStruct((rank, LANES), F32),
    ]
    x = in_hbm(probes)
    both, gram, *outs = product_call(
        functools.partial(first_kernel, plan, early, grams),
        [jnp.stack([*which, late]), one, two, x],
        [WHOLE, WHOLE, HBM],
        made + chunks,
        rows,
        unit,
        len(plan),
        "first_products",
    )
    away_outs, own_outs = outs[: len(away)], outs[len(away) :]
    unit, plan, grams, widths, which = layout(own, sub)
    own_outs = product_call(
        functools.partial(rest_kernel, plan, grams),
        [jnp.stack([*which, late]), both, gram, x, *own_outs],
        [WHOLE, WHOLE, HBM, WHOLE, WHOLE],
        chunks[len(away) :],
        rows,
        unit,
        len(plan),
        "rest_products",
    )
    return away_outs, own_outs


def inverse_kernel(gram_ref, out_ref):
    rank = out_ref.shape[0]
    rows = lax.broadcasted_iota(jnp.int32, (rank, LANES), 0)
    cols = lax.broadcasted_iota(jnp.int32, (rank, LANES), 1)
    work = jnp.where(cols < rank, gram_ref[...], (cols == rows + rank).astype(F32))
    scale = jnp.ones((rank, LANES), F32)
    for start in range(0, rank, PANEL):
        panel = [
            jnp.broadcast_to(work[:, k : k + 1], (rank, LANES))
            for k in range(start, start + PANEL)
        ]
        for j in range(PANEL):
            k = start + j
            over = 1.0 / panel[j][k : k + 1, :]
            scale = jnp.where(rows == k, over, scale)
            factor = jnp.where(rows > k, panel[j] * over, 0.0)
            work = work - factor * work[k : k + 1, :]
            for later in range(j + 1, PANEL):
                panel[later] = panel[later] - factor * panel[later][k : k + 1, :]
    out_ref[...] = (work * jnp.sqrt(scale))[:, rank : 2 * rank]


def inverse_factor(chunk, start):
    rank = chunk.shape[0]
    return pl.pallas_call(
        inverse_kernel,
        grid=(1,),
        in_specs=[pl.BlockSpec((rank, LANES), lambda i: (0, start // LANES))],
        out_specs=pl.BlockSpec((rank, rank), lambda i: (0, 0)),
        out_shape=jax.ShapeDtypeStruct((rank, rank), F32),
        compiler_params=PARAMS,
        cost_estimate=pl.CostEstimate(
            flops=20_000_000, bytes_accessed=8 * rank * LANES, transcendentals=rank
        ),
        name="inverse_factor",
    )(chunk)


def finish_kernel(plan, where_ref, inverse_ref, *refs):
    out_hbm, buf, sems = refs[-3:]
    _, rank, width = buf.shape
    head, rest = split(inverse_ref[...])
    both = jnp.concatenate([head, rest], axis=0)
    copies = []
    for k, (source, offset) in enumerate(plan):
        p_head, p_rest = split(refs[source][:, offset : offset + width])
        first = dot(both, p_head, PLAIN)
        buf[k] = first[:rank] + (first[rank:] + dot(head, p_rest, PLAIN))
        where = pl.ds(pl.multiple_of(where_ref[k] * width, width), width)
        copies.append(pltpu.make_async_copy(buf.at[k], out_hbm.at[:, where], sems.at[k]))
        copies[k].start()
    for copy in copies:
        copy.wait()


def finish(inverse, sources, pieces, width, total, before=None):
    rank = inverse.shape[0]
    count = len(pieces)
    in_specs = [TABLE, WHOLE, *[WHOLE] * len(sources)]
    args = [jnp.stack([piece[0] for piece in pieces]), inverse, *sources]
    aliases = {}
    if before is not None:
        in_specs.append(HBM)
        args.append(before)
        aliases = {len(args) - 1: 0}
    return pl.pallas_call(
        functools.partial(finish_kernel, [piece[1:] for piece in pieces]),
        in_specs=in_specs,
        out_specs=HBM,
        out_shape=jax.ShapeDtypeStruct((rank, total), F32),
        scratch_shapes=[
            pltpu.VMEM((count, rank, width), F32),
            pltpu.SemaphoreType.DMA((count,)),
        ],
        input_output_aliases=aliases,
        compiler_params=PARAMS,
        cost_estimate=pl.CostEstimate(
            flops=6 * rank * rank * width * count,
            bytes_accessed=8 * rank * width * count,
            transcendentals=0,
        ),
        name="finish",
    )(*args)


def body(n_pos, n_pix, probes, sketch):
    def swap(value, axis, size, bit):
        return lax.ppermute(value, axis, [(i, i ^ bit) for i in range(size)])

    def over(value, bit):
        return swap(value, "pos", n_pos, bit)

    me = lax.axis_index("pos").astype(jnp.int32)
    near, far = me & 1, (me >> 1) & 1
    cols = probes.shape[1]
    width = cols // (8 * CHUNKS)

    tall = tall_partial(probes, sketch.T)
    bit = 1
    while 2 * bit < n_pix:
        tall = tall + swap(tall, "pix", n_pix, bit)
        bit *= 2
    other = swap(tall, "pix", n_pix, bit)

    def block_a(c, p, q):
        return 8 * c + 2 * (near ^ p) + (far ^ q)

    def block_b(c, p, q):
        return 8 * c + 4 + 2 * (far ^ p) + (near ^ q)

    def outputs(c, p):
        return [
            ([block_a(c, p, 1), block_a(c, p, 0)], c == 0),
            ([block_b(c, p, 1), block_b(c, p, 0)], False),
        ]

    late = 1 - (lax.axis_index("pix").astype(jnp.int32) & 1)
    (away_a, away_b), (own_a, own_b) = products(
        tall, other, probes, outputs(0, 1), outputs(0, 0), width, late
    )

    g = LANES
    sum_a = own_a + over(away_a, 1)
    sum_b = own_b + over(away_b, 2)
    got_a = over(sum_a[:, : width + g], 2)
    got_b = over(sum_b[:, :width], 1)
    total = jnp.concatenate(
        [
            sum_a[:, width + g :] + got_a[:, :width],
            sum_a[:, width : width + g] + got_a[:, width:],
            sum_b[:, width:] + got_b,
        ],
        axis=1,
    )
    bit = 4
    while bit < n_pos:
        total = total + over(total, bit)
        bit *= 2
    inverse = inverse_factor(total, width)

    mine_a, mine_b = total[:, :width], total[:, width + g :]
    next_a = over(mine_a, 2)
    next_b = over(mine_b, 1)
    last_a = over(jnp.concatenate([mine_a, next_a], axis=1), 1)
    last_b = over(jnp.concatenate([mine_b, next_b], axis=1), 2)
    out = finish(
        inverse,
        [total, next_a, next_b],
        [
            (block_a(0, 0, 0), 0, 0),
            (block_b(0, 0, 0), 0, width + g),
            (block_a(0, 0, 1), 1, 0),
            (block_b(0, 0, 1), 2, 0),
        ],
        width,
        cols,
    )
    return finish(
        inverse,
        [last_a, last_b],
        [
            (block_a(0, 1, 0), 0, 0),
            (block_a(0, 1, 1), 0, width),
            (block_b(0, 1, 0), 1, 0),
            (block_b(0, 1, 1), 1, width),
        ],
        width,
        cols,
        out,
    )


def solution(mesh):
    in_specs = (P("pos", "pix"), P("pix", None))
    out_specs = P(None, "pix")
    run = functools.partial(body, mesh.shape["pos"], mesh.shape["pix"])
    return jax.shard_map(run, mesh=mesh, in_specs=in_specs, out_specs=out_specs, check_vma=False)
```

```python
import functools

import jax
import jax.numpy as jnp
from jax import lax
from jax.experimental import pallas as pl
from jax.experimental.pallas import tpu as pltpu
from jax.sharding import PartitionSpec as P

F32 = jnp.float32
BF16 = jnp.bfloat16
VMEM_LIMIT = 40 * 1024 * 1024
LANES = 128
CHUNKS = 2
AHEAD = 8
UNIT = 512
TILE = 256
PANEL = 4
LAST = (((1,), (1,)), ((), ()))
PLAIN = (((1,), (0,)), ((), ()))
ANYWHERE = pl.BlockSpec(memory_space=pl.ANY)
HBM = pl.BlockSpec(memory_space=pltpu.MemorySpace.HBM)
WHOLE = pl.BlockSpec(memory_space=pltpu.VMEM)
TABLE = pl.BlockSpec(memory_space=pltpu.SMEM)
PARAMS = pltpu.CompilerParams(vmem_limit_bytes=VMEM_LIMIT)


def split(x):
    head = x.astype(BF16)
    return head, (x - head.astype(F32)).astype(BF16)


def dot(a, b, dims):
    return lax.dot_general(a, b, dims, preferred_element_type=F32)


def tiles(size):
    step = min(TILE, size)
    return [slice(start, start + step) for start in range(0, size, step)]


def in_hbm(x):
    return pltpu.with_memory_space_constraint(x, pltpu.MemorySpace.HBM)


def stream(copies, use):
    for copy in copies[:AHEAD]:
        copy.start()
    for k, copy in enumerate(copies):
        copy.wait()
        if k + AHEAD < len(copies):
            copies[k + AHEAD].start()
        use(k)


def tall_kernel(x_hbm, s_hbm, out_ref, x_buf, s_buf, head_buf, rest_buf, x_sems, s_sem):
    blocks, _, unit = x_buf.shape
    rank = s_hbm.shape[0]
    copies = [
        pltpu.make_async_copy(x_hbm.at[:, pl.ds(k * unit, unit)], x_buf.at[k], x_sems.at[k])
        for k in range(blocks)
    ]
    sketch = pltpu.make_async_copy(s_hbm, s_buf, s_sem)
    sketch.start()

    def use(k):
        if k == 0:
            sketch.wait()
        s_head, s_rest = split(s_buf[:, k * unit : (k + 1) * unit])
        s_both = jnp.concatenate([s_head, s_rest], axis=0)
        head_buf[k % 2], rest_buf[k % 2] = split(x_buf[k])
        both = dot(s_both, head_buf[k % 2], LAST)
        part = both[:rank] + (both[rank:] + dot(s_head, rest_buf[k % 2], LAST))
        if k == 0:
            out_ref[...] = part
        else:
            out_ref[...] += part

    stream(copies, use)


def tall_partial(probes, sketch_t):
    rows, cols = probes.shape
    rank = sketch_t.shape[0]
    unit = min(UNIT, cols)
    blocks = cols // unit
    return pl.pallas_call(
        tall_kernel,
        in_specs=[HBM, HBM],
        out_specs=WHOLE,
        out_shape=jax.ShapeDtypeStruct((rank, rows), F32),
        scratch_shapes=[
            pltpu.VMEM((blocks, rows, unit), F32),
            pltpu.VMEM((rank, cols), F32),
            pltpu.VMEM((2, rows, unit), BF16),
            pltpu.VMEM((2, rows, unit), BF16),
            pltpu.SemaphoreType.DMA((blocks,)),
            pltpu.SemaphoreType.DMA,
        ],
        compiler_params=PARAMS,
        cost_estimate=pl.CostEstimate(
            flops=6 * rows * cols * rank, bytes_accessed=4 * rows * cols, transcendentals=0
        ),
        name="tall_partial",
    )(in_hbm(probes), in_hbm(sketch_t))


def multiply_blocks(both_ref, which_ref, x_hbm, x_buf, sems, plan, outs):
    rank = outs[0].shape[0]
    unit = x_buf.shape[2]
    copies = [
        pltpu.make_async_copy(
            x_hbm.at[:, pl.ds(pl.multiple_of(which_ref[k] * unit, unit), unit)],
            x_buf.at[k],
            sems.at[k],
        )
        for k in range(len(plan))
    ]

    def use(k):
        out, offset = plan[k]
        for cols in tiles(unit):
            total = None
            for rows in tiles(x_buf.shape[1]):
                x_head, x_rest = split(x_buf[k, rows, cols])
                both = dot(both_ref[:, rows], x_head, PLAIN)
                part = both[:rank] + (both[rank:] + dot(both_ref[:rank, rows], x_rest, PLAIN))
                total = part if total is None else total + part
            outs[out][:, offset + cols.start : offset + cols.stop] = total

    return copies, use


def first_kernel(plan, grams, which_ref, one_ref, two_ref, x_hbm, both_ref, gram_ref, *refs):
    outs, (x_buf, sems) = refs[:-2], refs[-2:]
    copies, use = multiply_blocks(both_ref, which_ref, x_hbm, x_buf, sems, plan, outs)

    def use_first(k):
        if k == 0:
            tall = one_ref[...] + two_ref[...]
            head, rest = split(tall)
            both_ref[...] = jnp.concatenate([head, rest], axis=0)
        use(k)

    stream(copies, use_first)
    tall = one_ref[...] + two_ref[...]
    r = tall.shape[0]
    head, rest = split(tall)
    tail = (tall - head.astype(F32) - rest.astype(F32)).astype(BF16)
    three = jnp.concatenate([head, rest, tail], axis=0)
    g = dot(three, three, LAST)
    cross = g[:r, r : 2 * r] + g[r : 2 * r, :r]
    small = g[:r, 2 * r :] + g[2 * r :, :r] + g[r : 2 * r, r : 2 * r]
    gram = g[:r, :r] + (cross + small)
    gram_ref[...] = jnp.concatenate([gram, jnp.zeros((r, LANES - r), F32)], axis=1)
    for out, offset in grams:
        outs[out][:, offset : offset + LANES] = gram_ref[...]


def rest_kernel(plan, grams, which_ref, both_ref, gram_ref, x_hbm, after_ref, *refs):
    outs, (x_buf, sems) = refs[:-2], refs[-2:]
    copies, use = multiply_blocks(both_ref, which_ref, x_hbm, x_buf, sems, plan, outs)
    stream(copies, use)
    for out, offset in grams:
        outs[out][:, offset : offset + LANES] = gram_ref[...]


def layout(outputs, sub):
    unit = min(UNIT, sub)
    plan, grams, widths, which = [], [], [], []
    for out, (blocks, with_gram) in enumerate(outputs):
        extra = LANES if with_gram else 0
        for j, block in enumerate(blocks):
            for part in range(sub // unit):
                plan.append((out, j * sub + part * unit + (extra if j else 0)))
                which.append(block * (sub // unit) + part)
        if with_gram:
            grams.append((out, sub))
        widths.append(len(blocks) * sub + extra)
    return unit, plan, grams, widths, jnp.stack(which)


def products(kernel, inputs, in_specs, made, probes, outputs, sub, name):
    rows = probes.shape[0]
    rank = inputs[1].shape[0]
    unit, plan, grams, widths, which = layout(outputs, sub)
    shapes = [*made, *[jax.ShapeDtypeStruct((rank, width), F32) for width in widths]]
    return pl.pallas_call(
        functools.partial(kernel, plan, grams),
        in_specs=[TABLE, *in_specs],
        out_specs=[WHOLE] * len(shapes),
        out_shape=shapes,
        scratch_shapes=[
            pltpu.VMEM((len(plan), rows, unit), F32),
            pltpu.SemaphoreType.DMA((len(plan),)),
        ],
        compiler_params=PARAMS,
        cost_estimate=pl.CostEstimate(
            flops=6 * rows * rank * unit * len(plan),
            bytes_accessed=4 * rows * unit * len(plan),
            transcendentals=0,
        ),
        name=name,
    )(which, *inputs)


def first_products(one, two, probes, outputs, sub):
    rank, rows = one.shape
    made = [
        jax.ShapeDtypeStruct((2 * rank, rows), BF16),
        jax.ShapeDtypeStruct((rank, LANES), F32),
    ]
    both, gram, *outs = products(
        first_kernel,
        [one, two, in_hbm(probes)],
        [WHOLE, WHOLE, HBM],
        made,
        probes,
        outputs,
        sub,
        "first_products",
    )
    return both, gram, outs


def rest_products(both, gram, probes, outputs, sub, after):
    return products(
        rest_kernel,
        [both, gram, in_hbm(probes), after],
        [WHOLE, WHOLE, HBM, ANYWHERE],
        [],
        probes,
        outputs,
        sub,
        "rest_products",
    )


def inverse_kernel(gram_ref, out_ref):
    rank = out_ref.shape[0]
    rows = lax.broadcasted_iota(jnp.int32, (rank, LANES), 0)
    cols = lax.broadcasted_iota(jnp.int32, (rank, LANES), 1)
    work = jnp.where(cols < rank, gram_ref[...], (cols == rows + rank).astype(F32))
    scale = jnp.ones((rank, LANES), F32)
    for start in range(0, rank, PANEL):
        panel = [
            jnp.broadcast_to(work[:, k : k + 1], (rank, LANES))
            for k in range(start, start + PANEL)
        ]
        for j in range(PANEL):
            k = start + j
            over = 1.0 / panel[j][k : k + 1, :]
            scale = jnp.where(rows == k, over, scale)
            factor = jnp.where(rows > k, panel[j] * over, 0.0)
            work = work - factor * work[k : k + 1, :]
            for later in range(j + 1, PANEL):
                panel[later] = panel[later] - factor * panel[later][k : k + 1, :]
    out_ref[...] = (work * jnp.sqrt(scale))[:, rank : 2 * rank]


def inverse_factor(chunk, start):
    rank = chunk.shape[0]
    return pl.pallas_call(
        inverse_kernel,
        grid=(1,),
        in_specs=[pl.BlockSpec((rank, LANES), lambda i: (0, start // LANES))],
        out_specs=pl.BlockSpec((rank, rank), lambda i: (0, 0)),
        out_shape=jax.ShapeDtypeStruct((rank, rank), F32),
        compiler_params=PARAMS,
        cost_estimate=pl.CostEstimate(
            flops=20_000_000, bytes_accessed=8 * rank * LANES, transcendentals=rank
        ),
        name="inverse_factor",
    )(chunk)


def finish_kernel(plan, where_ref, inverse_ref, *refs):
    out_hbm, buf, sems = refs[-3:]
    _, rank, width = buf.shape
    head, rest = split(inverse_ref[...])
    both = jnp.concatenate([head, rest], axis=0)
    copies = []
    for k, (source, offset) in enumerate(plan):
        p_head, p_rest = split(refs[source][:, offset : offset + width])
        first = dot(both, p_head, PLAIN)
        buf[k] = first[:rank] + (first[rank:] + dot(head, p_rest, PLAIN))
        where = pl.ds(pl.multiple_of(where_ref[k] * width, width), width)
        copies.append(pltpu.make_async_copy(buf.at[k], out_hbm.at[:, where], sems.at[k]))
        copies[k].start()
    for copy in copies:
        copy.wait()


def finish(inverse, sources, pieces, width, total, before=None):
    rank = inverse.shape[0]
    count = len(pieces)
    in_specs = [TABLE, WHOLE, *[WHOLE] * len(sources)]
    args = [jnp.stack([piece[0] for piece in pieces]), inverse, *sources]
    aliases = {}
    if before is not None:
        in_specs.append(HBM)
        args.append(before)
        aliases = {len(args) - 1: 0}
    return pl.pallas_call(
        functools.partial(finish_kernel, [piece[1:] for piece in pieces]),
        in_specs=in_specs,
        out_specs=HBM,
        out_shape=jax.ShapeDtypeStruct((rank, total), F32),
        scratch_shapes=[
            pltpu.VMEM((count, rank, width), F32),
            pltpu.SemaphoreType.DMA((count,)),
        ],
        input_output_aliases=aliases,
        compiler_params=PARAMS,
        cost_estimate=pl.CostEstimate(
            flops=6 * rank * rank * width * count,
            bytes_accessed=8 * rank * width * count,
            transcendentals=0,
        ),
        name="finish",
    )(*args)


def body(n_pos, n_pix, probes, sketch):
    def swap(value, axis, size, bit):
        return lax.ppermute(value, axis, [(i, i ^ bit) for i in range(size)])

    def over(value, turn):
        pairs = [
            (i * n_pix + j, (i ^ (1 << ((turn + j + 1) % 2))) * n_pix + j)
            for i in range(n_pos)
            for j in range(n_pix)
        ]
        return lax.ppermute(value, ("pos", "pix"), pairs)

    def after(value, *others):
        return lax.optimization_barrier((value, *others))[0]

    me = lax.axis_index("pos").astype(jnp.int32)
    odd = lax.axis_index("pix").astype(jnp.int32) & 1
    first_bit, second_bit = (me >> (1 - odd)) & 1, (me >> odd) & 1
    cols = probes.shape[1]
    width = cols // (4 * CHUNKS)

    tall = tall_partial(probes, sketch.T)
    bit = 1
    while 2 * bit < n_pix:
        tall = tall + swap(tall, "pix", n_pix, bit)
        bit *= 2
    other = swap(tall, "pix", n_pix, bit)

    def block(c, p, q):
        return 4 * c + 2 * (first_bit ^ p) + (second_bit ^ q)

    def outputs(c, p):
        return [([block(c, p, 1), block(c, p, 0)], c == 0)]

    both, gram, away = first_products(tall, other, probes, outputs(0, 1), width)

    ready, total = away[0], []
    for c in range(CHUNKS):
        g = LANES if c == 0 else 0
        more = outputs(c + 1, 1) if c + 1 < CHUNKS else []
        own, *made = rest_products(both, gram, probes, outputs(c, 0) + more, width, ready)
        ready = over(away[0], 0)
        away = made
        part = own + ready
        if away:
            away[0] = after(away[0], part)
        got = over(part[:, : width + g], 1)
        whole = part[:, width + g :] + got[:, :width]
        if g:
            whole = jnp.concatenate([whole, part[:, width : width + g] + got[:, width:]], axis=1)
        bit = 4
        while bit < n_pos:
            whole = whole + swap(whole, "pos", n_pos, bit)
            bit *= 2
        total.append(whole)

    inverse, sources, pieces = None, [], []
    for c in range(CHUNKS):
        mine = total[c][:, :width]
        if inverse is not None:
            mine = after(mine, inverse, far)
        near = over(mine, 1)
        if inverse is None:
            inverse = inverse_factor(after(total[0], near), width)
        far = over(jnp.concatenate([mine, near], axis=1), 0)
        k = len(sources)
        sources += [mine, near, far]
        pieces += [
            (block(c, 0, 0), k, 0),
            (block(c, 0, 1), k + 1, 0),
            (block(c, 1, 0), k + 2, 0),
            (block(c, 1, 1), k + 2, width),
        ]
    out = finish(inverse, sources[:-1], pieces[:-2], width, cols)
    pieces = [(where, 0, start) for where, _, start in pieces[-2:]]
    return finish(inverse, sources[-1:], pieces, width, cols, out)


def solution(mesh):
    in_specs = (P("pos", "pix"), P("pix", None))
    out_specs = P(None, "pix")
    run = functools.partial(body, mesh.shape["pos"], mesh.shape["pix"])
    return jax.shard_map(run, mesh=mesh, in_specs=in_specs, out_specs=out_specs, check_vma=False)
```

```python
import functools

import jax
import jax.numpy as jnp
from jax import lax
from jax.experimental import pallas as pl
from jax.experimental.pallas import tpu as pltpu
from jax.sharding import PartitionSpec as P

F32 = jnp.float32
BF16 = jnp.bfloat16
VMEM_LIMIT = 40 * 1024 * 1024
LANES = 128
CHUNKS = 2
AHEAD = 8
UNIT = 512
TILE = 256
PANEL = 4
LAST = (((1,), (1,)), ((), ()))
PLAIN = (((1,), (0,)), ((), ()))
ANYWHERE = pl.BlockSpec(memory_space=pl.ANY)
HBM = pl.BlockSpec(memory_space=pltpu.MemorySpace.HBM)
WHOLE = pl.BlockSpec(memory_space=pltpu.VMEM)
TABLE = pl.BlockSpec(memory_space=pltpu.SMEM)
PARAMS = pltpu.CompilerParams(vmem_limit_bytes=VMEM_LIMIT)


def split(x):
    head = x.astype(BF16)
    return head, (x - head.astype(F32)).astype(BF16)


def dot(a, b, dims):
    return lax.dot_general(a, b, dims, preferred_element_type=F32)


def tiles(size):
    step = min(TILE, size)
    return [slice(start, start + step) for start in range(0, size, step)]


def in_hbm(x):
    return pltpu.with_memory_space_constraint(x, pltpu.MemorySpace.HBM)


def stream(copies, use):
    for copy in copies[:AHEAD]:
        copy.start()
    for k, copy in enumerate(copies):
        copy.wait()
        if k + AHEAD < len(copies):
            copies[k + AHEAD].start()
        use(k)


def tall_kernel(x_hbm, s_hbm, out_ref, x_buf, s_buf, head_buf, rest_buf, x_sems, s_sems):
    blocks, _, unit = x_buf.shape
    rank = s_hbm.shape[0]

    def copies(k):
        where = pl.ds(k * unit, unit)
        return (
            pltpu.make_async_copy(s_hbm.at[:, where], s_buf.at[k], s_sems.at[k]),
            pltpu.make_async_copy(x_hbm.at[:, where], x_buf.at[k], x_sems.at[k]),
        )

    for k in range(blocks):
        for copy in copies(k):
            copy.start()
    for k in range(blocks):
        for copy in copies(k):
            copy.wait()
        s_head, s_rest = split(s_buf[k])
        s_both = jnp.concatenate([s_head, s_rest], axis=0)
        x_head, x_rest = split(x_buf[k])
        head_buf[k] = x_head
        rest_buf[k] = x_rest
        both = dot(s_both, x_head, LAST)
        part = both[:rank] + (both[rank:] + dot(s_head, x_rest, LAST))
        if k == 0:
            out_ref[...] = part
        else:
            out_ref[...] += part


def tall_partial(probes, sketch_t):
    rows, cols = probes.shape
    rank = sketch_t.shape[0]
    unit = min(2 * UNIT, cols)
    blocks = cols // unit
    return pl.pallas_call(
        tall_kernel,
        in_specs=[HBM, HBM],
        out_specs=WHOLE,
        out_shape=jax.ShapeDtypeStruct((rank, rows), F32),
        scratch_shapes=[
            pltpu.VMEM((blocks, rows, unit), F32),
            pltpu.VMEM((blocks, rank, unit), F32),
            pltpu.VMEM((blocks, rows, unit), BF16),
            pltpu.VMEM((blocks, rows, unit), BF16),
            pltpu.SemaphoreType.DMA((blocks,)),
            pltpu.SemaphoreType.DMA((blocks,)),
        ],
        compiler_params=PARAMS,
        cost_estimate=pl.CostEstimate(
            flops=6 * rows * cols * rank, bytes_accessed=4 * rows * cols, transcendentals=0
        ),
        name="tall_partial",
    )(in_hbm(probes), in_hbm(sketch_t))


def multiply_blocks(both_ref, which_ref, x_hbm, x_buf, sems, plan, outs):
    rank = outs[0].shape[0]
    unit = x_buf.shape[2]
    copies = [
        pltpu.make_async_copy(
            x_hbm.at[:, pl.ds(pl.multiple_of(which_ref[k] * unit, unit), unit)],
            x_buf.at[k],
            sems.at[k],
        )
        for k in range(len(plan))
    ]

    def use(k):
        out, offset = plan[k]
        for cols in tiles(unit):
            total = None
            for rows in tiles(x_buf.shape[1]):
                x_head, x_rest = split(x_buf[k, rows, cols])
                both = dot(both_ref[:, rows], x_head, PLAIN)
                part = both[:rank] + (both[rank:] + dot(both_ref[:rank, rows], x_rest, PLAIN))
                total = part if total is None else total + part
            outs[out][:, offset + cols.start : offset + cols.stop] = total

    return copies, use


def first_kernel(plan, grams, which_ref, one_ref, two_ref, x_hbm, both_ref, gram_ref, *refs):
    outs, (x_buf, sems) = refs[:-2], refs[-2:]
    copies, use = multiply_blocks(both_ref, which_ref, x_hbm, x_buf, sems, plan, outs)

    def use_first(k):
        if k == 0:
            tall = one_ref[...] + two_ref[...]
            head, rest = split(tall)
            both_ref[...] = jnp.concatenate([head, rest], axis=0)
        use(k)

    stream(copies, use_first)
    tall = one_ref[...] + two_ref[...]
    r = tall.shape[0]
    head, rest = split(tall)
    tail = (tall - head.astype(F32) - rest.astype(F32)).astype(BF16)
    three = jnp.concatenate([head, rest, tail], axis=0)
    g = dot(three, three, LAST)
    cross = g[:r, r : 2 * r] + g[r : 2 * r, :r]
    small = g[:r, 2 * r :] + g[2 * r :, :r] + g[r : 2 * r, r : 2 * r]
    gram = g[:r, :r] + (cross + small)
    gram_ref[...] = jnp.concatenate([gram, jnp.zeros((r, LANES - r), F32)], axis=1)
    for out, offset in grams:
        outs[out][:, offset : offset + LANES] = gram_ref[...]


def rest_kernel(plan, grams, which_ref, both_ref, gram_ref, x_hbm, after_ref, *refs):
    outs, (x_buf, sems) = refs[:-2], refs[-2:]
    copies, use = multiply_blocks(both_ref, which_ref, x_hbm, x_buf, sems, plan, outs)
    stream(copies, use)
    for out, offset in grams:
        outs[out][:, offset : offset + LANES] = gram_ref[...]


def layout(outputs, sub):
    unit = min(UNIT, sub)
    plan, grams, widths, which = [], [], [], []
    for out, (blocks, with_gram) in enumerate(outputs):
        extra = LANES if with_gram else 0
        for j, block in enumerate(blocks):
            for part in range(sub // unit):
                plan.append((out, j * sub + part * unit + (extra if j else 0)))
                which.append(block * (sub // unit) + part)
        if with_gram:
            grams.append((out, sub))
        widths.append(len(blocks) * sub + extra)
    return unit, plan, grams, widths, jnp.stack(which)


def products(kernel, inputs, in_specs, made, probes, outputs, sub, name):
    rows = probes.shape[0]
    rank = inputs[1].shape[0]
    unit, plan, grams, widths, which = layout(outputs, sub)
    shapes = [*made, *[jax.ShapeDtypeStruct((rank, width), F32) for width in widths]]
    return pl.pallas_call(
        functools.partial(kernel, plan, grams),
        in_specs=[TABLE, *in_specs],
        out_specs=[WHOLE] * len(shapes),
        out_shape=shapes,
        scratch_shapes=[
            pltpu.VMEM((len(plan), rows, unit), F32),
            pltpu.SemaphoreType.DMA((len(plan),)),
        ],
        compiler_params=PARAMS,
        cost_estimate=pl.CostEstimate(
            flops=6 * rows * rank * unit * len(plan),
            bytes_accessed=4 * rows * unit * len(plan),
            transcendentals=0,
        ),
        name=name,
    )(which, *inputs)


def first_products(one, two, probes, outputs, sub):
    rank, rows = one.shape
    made = [
        jax.ShapeDtypeStruct((2 * rank, rows), BF16),
        jax.ShapeDtypeStruct((rank, LANES), F32),
    ]
    both, gram, *outs = products(
        first_kernel,
        [one, two, in_hbm(probes)],
        [WHOLE, WHOLE, HBM],
        made,
        probes,
        outputs,
        sub,
        "first_products",
    )
    return both, gram, outs


def rest_products(both, gram, probes, outputs, sub, after):
    return products(
        rest_kernel,
        [both, gram, in_hbm(probes), after],
        [WHOLE, WHOLE, HBM, ANYWHERE],
        [],
        probes,
        outputs,
        sub,
        "rest_products",
    )


def inverse_kernel(gram_ref, out_ref):
    rank = out_ref.shape[0]
    rows = lax.broadcasted_iota(jnp.int32, (rank, LANES), 0)
    cols = lax.broadcasted_iota(jnp.int32, (rank, LANES), 1)
    work = jnp.where(cols < rank, gram_ref[...], (cols == rows + rank).astype(F32))
    scale = jnp.ones((rank, LANES), F32)
    for start in range(0, rank, PANEL):
        panel = [
            jnp.broadcast_to(work[:, k : k + 1], (rank, LANES))
            for k in range(start, start + PANEL)
        ]
        for j in range(PANEL):
            k = start + j
            over = 1.0 / panel[j][k : k + 1, :]
            scale = jnp.where(rows == k, over, scale)
            factor = jnp.where(rows > k, panel[j] * over, 0.0)
            work = work - factor * work[k : k + 1, :]
            for later in range(j + 1, PANEL):
                panel[later] = panel[later] - factor * panel[later][k : k + 1, :]
    out_ref[...] = (work * jnp.sqrt(scale))[:, rank : 2 * rank]


def inverse_factor(chunk, start):
    rank = chunk.shape[0]
    return pl.pallas_call(
        inverse_kernel,
        grid=(1,),
        in_specs=[pl.BlockSpec((rank, LANES), lambda i: (0, start // LANES))],
        out_specs=pl.BlockSpec((rank, rank), lambda i: (0, 0)),
        out_shape=jax.ShapeDtypeStruct((rank, rank), F32),
        compiler_params=PARAMS,
        cost_estimate=pl.CostEstimate(
            flops=20_000_000, bytes_accessed=8 * rank * LANES, transcendentals=rank
        ),
        name="inverse_factor",
    )(chunk)


def finish_kernel(plan, where_ref, inverse_ref, *refs):
    out_hbm, buf, sems = refs[-3:]
    _, rank, width = buf.shape
    head, rest = split(inverse_ref[...])
    both = jnp.concatenate([head, rest], axis=0)
    copies = []
    for k, (source, offset) in enumerate(plan):
        p_head, p_rest = split(refs[source][:, offset : offset + width])
        first = dot(both, p_head, PLAIN)
        buf[k] = first[:rank] + (first[rank:] + dot(head, p_rest, PLAIN))
        where = pl.ds(pl.multiple_of(where_ref[k] * width, width), width)
        copies.append(pltpu.make_async_copy(buf.at[k], out_hbm.at[:, where], sems.at[k]))
        copies[k].start()
    for copy in copies:
        copy.wait()


def finish(inverse, sources, pieces, width, total, before=None):
    rank = inverse.shape[0]
    count = len(pieces)
    in_specs = [TABLE, WHOLE, *[WHOLE] * len(sources)]
    args = [jnp.stack([piece[0] for piece in pieces]), inverse, *sources]
    aliases = {}
    if before is not None:
        in_specs.append(HBM)
        args.append(before)
        aliases = {len(args) - 1: 0}
    return pl.pallas_call(
        functools.partial(finish_kernel, [piece[1:] for piece in pieces]),
        in_specs=in_specs,
        out_specs=HBM,
        out_shape=jax.ShapeDtypeStruct((rank, total), F32),
        scratch_shapes=[
            pltpu.VMEM((count, rank, width), F32),
            pltpu.SemaphoreType.DMA((count,)),
        ],
        input_output_aliases=aliases,
        compiler_params=PARAMS,
        cost_estimate=pl.CostEstimate(
            flops=6 * rank * rank * width * count,
            bytes_accessed=8 * rank * width * count,
            transcendentals=0,
        ),
        name="finish",
    )(*args)


def body(n_pos, n_pix, probes, sketch):
    def swap(value, axis, size, bit):
        return lax.ppermute(value, axis, [(i, i ^ bit) for i in range(size)])

    def over(value, bit):
        return swap(value, "pos", n_pos, bit)

    me = lax.axis_index("pos").astype(jnp.int32)
    near, far = me & 1, (me >> 1) & 1
    cols = probes.shape[1]
    width = cols // (8 * CHUNKS)

    tall = tall_partial(probes, sketch.T)
    bit = 1
    while 2 * bit < n_pix:
        tall = tall + swap(tall, "pix", n_pix, bit)
        bit *= 2
    other = swap(tall, "pix", n_pix, bit)

    def block_a(c, p, q):
        return 8 * c + 2 * (near ^ p) + (far ^ q)

    def block_b(c, p, q):
        return 8 * c + 4 + 2 * (far ^ p) + (near ^ q)

    def outputs(c, p):
        return [
            ([block_a(c, p, 1), block_a(c, p, 0)], c == 0),
            ([block_b(c, p, 1), block_b(c, p, 0)], False),
        ]

    both, gram, away = first_products(tall, other, probes, outputs(0, 1), width)

    inverse, after = None, away[0]
    sources, pieces = [], []
    for c in range(CHUNKS):
        g = LANES if c == 0 else 0
        last = c == CHUNKS - 1
        made = rest_products(
            both, gram, probes, outputs(c, 0) + ([] if last else outputs(c + 1, 1)), width, after
        )
        away_a, away_b = away
        (own_a, own_b), away = made[:2], made[2:]
        if c > 0:
            away_a, away_b, sum_a, sum_b = lax.optimization_barrier((away_a, away_b, sum_a, sum_b))
        got_a = over(away_a, 1)
        sum_a = own_a + got_a
        sum_b = own_b + over(away_b, 2)
        send_a, send_b = sum_a[:, : width + g], sum_b[:, :width]
        if c > 0:
            send_a, send_b, whole = lax.optimization_barrier((send_a, send_b, whole))
        got_a = over(send_a, 2)
        got_b = over(send_b, 1)
        whole = jnp.concatenate(
            [
                sum_a[:, width + g :] + got_a[:, :width],
                sum_a[:, width : width + g] + got_a[:, width:],
                sum_b[:, width:] + got_b,
            ],
            axis=1,
        )
        after = total = whole
        bit = 4
        while bit < n_pos:
            total = total + over(total, bit)
            bit *= 2
        if c == 0:
            inverse = inverse_factor(total, width)
        mine_a, mine_b = total[:, :width], total[:, width + g :]
        if c > 0:
            mine_a, mine_b, inverse = lax.optimization_barrier((mine_a, mine_b, inverse))
        next_a = over(mine_a, 2)
        next_b = over(mine_b, 1)
        last_a = over(jnp.concatenate([mine_a, next_a], axis=1), 1)
        last_b = over(jnp.concatenate([mine_b, next_b], axis=1), 2)
        k = len(sources)
        sources += [total, next_a, next_b, last_a, last_b]
        pieces += [
            (block_a(c, 0, 0), k, 0),
            (block_b(c, 0, 0), k, width + g),
            (block_a(c, 0, 1), k + 1, 0),
            (block_b(c, 0, 1), k + 2, 0),
            (block_a(c, 1, 0), k + 3, 0),
            (block_a(c, 1, 1), k + 3, width),
            (block_b(c, 1, 0), k + 4, 0),
            (block_b(c, 1, 1), k + 4, width),
        ]
    out = finish(inverse, sources[:-2], pieces[:-4], width, cols)
    pieces = [(where, source - k - 3, start) for where, source, start in pieces[-4:]]
    return finish(inverse, sources[-2:], pieces, width, cols, out)


def solution(mesh):
    in_specs = (P("pos", "pix"), P("pix", None))
    out_specs = P(None, "pix")
    run = functools.partial(body, mesh.shape["pos"], mesh.shape["pix"])
    return jax.shard_map(run, mesh=mesh, in_specs=in_specs, out_specs=out_specs, check_vma=False)
```

```python
import functools

import jax
import jax.numpy as jnp
from jax import lax
from jax.experimental import pallas as pl
from jax.experimental.pallas import tpu as pltpu
from jax.sharding import PartitionSpec as P

F32 = jnp.float32
BF16 = jnp.bfloat16
VMEM_LIMIT = 40 * 1024 * 1024
LANES = 128
CHUNKS = 2
AHEAD = 8
UNIT = 512
TILE = 256
PANEL = 4
LAST = (((1,), (1,)), ((), ()))
PLAIN = (((1,), (0,)), ((), ()))
ANYWHERE = pl.BlockSpec(memory_space=pl.ANY)
HBM = pl.BlockSpec(memory_space=pltpu.MemorySpace.HBM)
WHOLE = pl.BlockSpec(memory_space=pltpu.VMEM)
TABLE = pl.BlockSpec(memory_space=pltpu.SMEM)
PARAMS = pltpu.CompilerParams(vmem_limit_bytes=VMEM_LIMIT)


def split(x):
    head = x.astype(BF16)
    return head, (x - head.astype(F32)).astype(BF16)


def dot(a, b, dims):
    return lax.dot_general(a, b, dims, preferred_element_type=F32)


def tiles(size):
    step = min(TILE, size)
    return [slice(start, start + step) for start in range(0, size, step)]


def in_hbm(x):
    return pltpu.with_memory_space_constraint(x, pltpu.MemorySpace.HBM)


def stream(copies, use):
    for copy in copies[:AHEAD]:
        copy.start()
    for k, copy in enumerate(copies):
        copy.wait()
        if k + AHEAD < len(copies):
            copies[k + AHEAD].start()
        use(k)


def tall_kernel(x_hbm, s_hbm, out_ref, x_buf, s_buf, head_buf, rest_buf, x_sems, s_sems):
    blocks, _, unit = x_buf.shape
    rank = s_hbm.shape[0]

    def copies(k):
        where = pl.ds(k * unit, unit)
        return (
            pltpu.make_async_copy(s_hbm.at[:, where], s_buf.at[k], s_sems.at[k]),
            pltpu.make_async_copy(x_hbm.at[:, where], x_buf.at[k], x_sems.at[k]),
        )

    for k in range(blocks):
        for copy in copies(k):
            copy.start()
    for k in range(blocks):
        for copy in copies(k):
            copy.wait()
        s_head, s_rest = split(s_buf[k])
        s_both = jnp.concatenate([s_head, s_rest], axis=0)
        x_head, x_rest = split(x_buf[k])
        head_buf[k] = x_head
        rest_buf[k] = x_rest
        both = dot(s_both, x_head, LAST)
        part = both[:rank] + (both[rank:] + dot(s_head, x_rest, LAST))
        if k == 0:
            out_ref[...] = part
        else:
            out_ref[...] += part


def tall_partial(probes, sketch_t):
    rows, cols = probes.shape
    rank = sketch_t.shape[0]
    unit = min(2 * UNIT, cols)
    blocks = cols // unit
    return pl.pallas_call(
        tall_kernel,
        in_specs=[HBM, HBM],
        out_specs=WHOLE,
        out_shape=jax.ShapeDtypeStruct((rank, rows), F32),
        scratch_shapes=[
            pltpu.VMEM((blocks, rows, unit), F32),
            pltpu.VMEM((blocks, rank, unit), F32),
            pltpu.VMEM((blocks, rows, unit), BF16),
            pltpu.VMEM((blocks, rows, unit), BF16),
            pltpu.SemaphoreType.DMA((blocks,)),
            pltpu.SemaphoreType.DMA((blocks,)),
        ],
        compiler_params=PARAMS,
        cost_estimate=pl.CostEstimate(
            flops=6 * rows * cols * rank, bytes_accessed=4 * rows * cols, transcendentals=0
        ),
        name="tall_partial",
    )(in_hbm(probes), in_hbm(sketch_t))


def multiply_blocks(both_ref, which_ref, x_hbm, x_buf, sems, plan, outs):
    rank = outs[0].shape[0]
    unit = x_buf.shape[2]
    copies = [
        pltpu.make_async_copy(
            x_hbm.at[:, pl.ds(pl.multiple_of(which_ref[k] * unit, unit), unit)],
            x_buf.at[k],
            sems.at[k],
        )
        for k in range(len(plan))
    ]

    def use(k):
        out, offset = plan[k]
        for cols in tiles(unit):
            total = None
            for rows in tiles(x_buf.shape[1]):
                x_head, x_rest = split(x_buf[k, rows, cols])
                both = dot(both_ref[:, rows], x_head, PLAIN)
                part = both[:rank] + (both[rank:] + dot(both_ref[:rank, rows], x_rest, PLAIN))
                total = part if total is None else total + part
            outs[out][:, offset + cols.start : offset + cols.stop] = total

    return copies, use


def first_kernel(plan, grams, which_ref, tall_ref, x_hbm, both_ref, gram_ref, *refs):
    outs, (x_buf, sems) = refs[:-2], refs[-2:]
    copies, use = multiply_blocks(both_ref, which_ref, x_hbm, x_buf, sems, plan, outs)

    def use_first(k):
        if k == 0:
            head, rest = split(tall_ref[...])
            both_ref[...] = jnp.concatenate([head, rest], axis=0)
        use(k)

    stream(copies, use_first)
    tall = tall_ref[...]
    r = tall.shape[0]
    head, rest = split(tall)
    tail = (tall - head.astype(F32) - rest.astype(F32)).astype(BF16)
    three = jnp.concatenate([head, rest, tail], axis=0)
    g = dot(three, three, LAST)
    cross = g[:r, r : 2 * r] + g[r : 2 * r, :r]
    small = g[:r, 2 * r :] + g[2 * r :, :r] + g[r : 2 * r, r : 2 * r]
    gram = g[:r, :r] + (cross + small)
    gram_ref[...] = jnp.concatenate([gram, jnp.zeros((r, LANES - r), F32)], axis=1)
    for out, offset in grams:
        outs[out][:, offset : offset + LANES] = gram_ref[...]


def rest_kernel(plan, grams, which_ref, both_ref, gram_ref, x_hbm, after_ref, *refs):
    outs, (x_buf, sems) = refs[:-2], refs[-2:]
    copies, use = multiply_blocks(both_ref, which_ref, x_hbm, x_buf, sems, plan, outs)
    stream(copies, use)
    for out, offset in grams:
        outs[out][:, offset : offset + LANES] = gram_ref[...]


def layout(outputs, sub):
    unit = min(UNIT, sub)
    plan, grams, widths, which = [], [], [], []
    for out, (blocks, with_gram) in enumerate(outputs):
        extra = LANES if with_gram else 0
        for j, block in enumerate(blocks):
            for part in range(sub // unit):
                plan.append((out, j * sub + part * unit + (extra if j else 0)))
                which.append(block * (sub // unit) + part)
        if with_gram:
            grams.append((out, sub))
        widths.append(len(blocks) * sub + extra)
    return unit, plan, grams, widths, jnp.stack(which)


def products(kernel, inputs, in_specs, made, probes, outputs, sub, name):
    rows = probes.shape[0]
    rank = made[1].shape[0] if made else inputs[1].shape[0]
    unit, plan, grams, widths, which = layout(outputs, sub)
    shapes = [*made, *[jax.ShapeDtypeStruct((rank, width), F32) for width in widths]]
    return pl.pallas_call(
        functools.partial(kernel, plan, grams),
        in_specs=[TABLE, *in_specs],
        out_specs=[WHOLE] * len(shapes),
        out_shape=shapes,
        scratch_shapes=[
            pltpu.VMEM((len(plan), rows, unit), F32),
            pltpu.SemaphoreType.DMA((len(plan),)),
        ],
        compiler_params=PARAMS,
        cost_estimate=pl.CostEstimate(
            flops=6 * rows * rank * unit * len(plan),
            bytes_accessed=4 * rows * unit * len(plan),
            transcendentals=0,
        ),
        name=name,
    )(which, *inputs)


def first_products(tall, probes, outputs, sub):
    rank, rows = tall.shape
    made = [
        jax.ShapeDtypeStruct((2 * rank, rows), BF16),
        jax.ShapeDtypeStruct((rank, LANES), F32),
    ]
    both, gram, *outs = products(
        first_kernel,
        [tall, in_hbm(probes)],
        [WHOLE, HBM],
        made,
        probes,
        outputs,
        sub,
        "first_products",
    )
    return both, gram, outs


def rest_products(both, gram, probes, outputs, sub, after):
    return products(
        rest_kernel,
        [both, gram, in_hbm(probes), after],
        [WHOLE, WHOLE, HBM, ANYWHERE],
        [],
        probes,
        outputs,
        sub,
        "rest_products",
    )


def inverse_kernel(gram_ref, out_ref):
    rank = out_ref.shape[0]
    rows = lax.broadcasted_iota(jnp.int32, (rank, LANES), 0)
    cols = lax.broadcasted_iota(jnp.int32, (rank, LANES), 1)
    work = jnp.where(cols < rank, gram_ref[...], (cols == rows + rank).astype(F32))
    scale = jnp.ones((rank, LANES), F32)
    for start in range(0, rank, PANEL):
        panel = [
            jnp.broadcast_to(work[:, k : k + 1], (rank, LANES))
            for k in range(start, start + PANEL)
        ]
        for j in range(PANEL):
            k = start + j
            over = 1.0 / panel[j][k : k + 1, :]
            scale = jnp.where(rows == k, over, scale)
            factor = jnp.where(rows > k, panel[j] * over, 0.0)
            work = work - factor * work[k : k + 1, :]
            for later in range(j + 1, PANEL):
                panel[later] = panel[later] - factor * panel[later][k : k + 1, :]
    out_ref[...] = (work * jnp.sqrt(scale))[:, rank : 2 * rank]


def inverse_factor(chunk, start):
    rank = chunk.shape[0]
    return pl.pallas_call(
        inverse_kernel,
        grid=(1,),
        in_specs=[pl.BlockSpec((rank, LANES), lambda i: (0, start // LANES))],
        out_specs=pl.BlockSpec((rank, rank), lambda i: (0, 0)),
        out_shape=jax.ShapeDtypeStruct((rank, rank), F32),
        compiler_params=PARAMS,
        cost_estimate=pl.CostEstimate(
            flops=20_000_000, bytes_accessed=8 * rank * LANES, transcendentals=rank
        ),
        name="inverse_factor",
    )(chunk)


def finish_kernel(plan, where_ref, inverse_ref, *refs):
    out_hbm, buf, sems = refs[-3:]
    _, rank, width = buf.shape
    head, rest = split(inverse_ref[...])
    both = jnp.concatenate([head, rest], axis=0)
    copies = []
    for k, (source, offset) in enumerate(plan):
        p_head, p_rest = split(refs[source][:, offset : offset + width])
        first = dot(both, p_head, PLAIN)
        buf[k] = first[:rank] + (first[rank:] + dot(head, p_rest, PLAIN))
        where = pl.ds(pl.multiple_of(where_ref[k] * width, width), width)
        copies.append(pltpu.make_async_copy(buf.at[k], out_hbm.at[:, where], sems.at[k]))
        copies[k].start()
    for copy in copies:
        copy.wait()


def finish(inverse, sources, pieces, width, total, before=None):
    rank = inverse.shape[0]
    count = len(pieces)
    in_specs = [TABLE, WHOLE, *[WHOLE] * len(sources)]
    args = [jnp.stack([piece[0] for piece in pieces]), inverse, *sources]
    aliases = {}
    if before is not None:
        in_specs.append(HBM)
        args.append(before)
        aliases = {len(args) - 1: 0}
    return pl.pallas_call(
        functools.partial(finish_kernel, [piece[1:] for piece in pieces]),
        in_specs=in_specs,
        out_specs=HBM,
        out_shape=jax.ShapeDtypeStruct((rank, total), F32),
        scratch_shapes=[
            pltpu.VMEM((count, rank, width), F32),
            pltpu.SemaphoreType.DMA((count,)),
        ],
        input_output_aliases=aliases,
        compiler_params=PARAMS,
        cost_estimate=pl.CostEstimate(
            flops=6 * rank * rank * width * count,
            bytes_accessed=8 * rank * width * count,
            transcendentals=0,
        ),
        name="finish",
    )(*args)


def body(n_pos, n_pix, probes, sketch):
    def swap(value, axis, size, bit):
        return lax.ppermute(value, axis, [(i, i ^ bit) for i in range(size)])

    def over(value, bit):
        return swap(value, "pos", n_pos, bit)

    me = lax.axis_index("pos").astype(jnp.int32)
    near, far = me & 1, (me >> 1) & 1
    cols = probes.shape[1]
    width = cols // (8 * CHUNKS)

    tall = tall_partial(probes, sketch.T)
    if n_pix == 4:
        even = (lax.axis_index("pix") & 1) == 0
        tall = tall + lax.ppermute(tall, "pix", [(1, 0), (3, 2)])
        tall = tall + lax.ppermute(tall, "pix", [(0, 2), (2, 0)])
        handed = lax.ppermute(tall, "pix", [(0, 1), (2, 3)])
        tall = jnp.where(even, tall, handed)
    else:
        tall = lax.psum(tall, "pix")

    def block_a(c, p, q):
        return 8 * c + 2 * (near ^ p) + (far ^ q)

    def block_b(c, p, q):
        return 8 * c + 4 + 2 * (far ^ p) + (near ^ q)

    def outputs(c, p):
        return [
            ([block_a(c, p, 1), block_a(c, p, 0)], c == 0),
            ([block_b(c, p, 1), block_b(c, p, 0)], False),
        ]

    both, gram, away = first_products(tall, probes, outputs(0, 1), width)

    inverse, after = None, away[0]
    sources, pieces = [], []
    for c in range(CHUNKS):
        g = LANES if c == 0 else 0
        last = c == CHUNKS - 1
        made = rest_products(
            both, gram, probes, outputs(c, 0) + ([] if last else outputs(c + 1, 1)), width, after
        )
        away_a, away_b = away
        (own_a, own_b), away = made[:2], made[2:]
        got_a = over(away_a, 1)
        sum_a = own_a + got_a
        sum_b = own_b + over(away_b, 2)
        after = got_a
        send_a, send_b = sum_a[:, : width + g], sum_b[:, :width]
        if c > 0:
            send_a, send_b, whole = lax.optimization_barrier((send_a, send_b, whole))
        got_a = over(send_a, 2)
        got_b = over(send_b, 1)
        whole = jnp.concatenate(
            [
                sum_a[:, width + g :] + got_a[:, :width],
                sum_a[:, width : width + g] + got_a[:, width:],
                sum_b[:, width:] + got_b,
            ],
            axis=1,
        )
        total = whole
        bit = 4
        while bit < n_pos:
            total = total + over(total, bit)
            bit *= 2
        if c == 0:
            inverse = inverse_factor(total, width)
        mine_a, mine_b = total[:, :width], total[:, width + g :]
        if c > 0:
            mine_a, mine_b, inverse = lax.optimization_barrier((mine_a, mine_b, inverse))
        next_a = over(mine_a, 2)
        next_b = over(mine_b, 1)
        last_a = over(jnp.concatenate([mine_a, next_a], axis=1), 1)
        last_b = over(jnp.concatenate([mine_b, next_b], axis=1), 2)
        k = len(sources)
        sources += [total, next_a, next_b, last_a, last_b]
        pieces += [
            (block_a(c, 0, 0), k, 0),
            (block_b(c, 0, 0), k, width + g),
            (block_a(c, 0, 1), k + 1, 0),
            (block_b(c, 0, 1), k + 2, 0),
            (block_a(c, 1, 0), k + 3, 0),
            (block_a(c, 1, 1), k + 3, width),
            (block_b(c, 1, 0), k + 4, 0),
            (block_b(c, 1, 1), k + 4, width),
        ]
    out = finish(inverse, sources[:-2], pieces[:-4], width, cols)
    pieces = [(where, source - k - 3, start) for where, source, start in pieces[-4:]]
    return finish(inverse, sources[-2:], pieces, width, cols, out)


def solution(mesh):
    in_specs = (P("pos", "pix"), P("pix", None))
    out_specs = P(None, "pix")
    run = functools.partial(body, mesh.shape["pos"], mesh.shape["pix"])
    return jax.shard_map(run, mesh=mesh, in_specs=in_specs, out_specs=out_specs, check_vma=False)
```

```python
import functools

import jax
import jax.numpy as jnp
from jax import lax
from jax.experimental import pallas as pl
from jax.experimental.pallas import tpu as pltpu
from jax.sharding import PartitionSpec as P

F32 = jnp.float32
BF16 = jnp.bfloat16
VMEM_LIMIT = 40 * 1024 * 1024
LANES = 128
CHUNKS = 2
AHEAD = 8
UNIT = 512
TILE = 256
PANEL = 4
LAST = (((1,), (1,)), ((), ()))
PLAIN = (((1,), (0,)), ((), ()))
ANYWHERE = pl.BlockSpec(memory_space=pl.ANY)
HBM = pl.BlockSpec(memory_space=pltpu.MemorySpace.HBM)
WHOLE = pl.BlockSpec(memory_space=pltpu.VMEM)
TABLE = pl.BlockSpec(memory_space=pltpu.SMEM)
PARAMS = pltpu.CompilerParams(vmem_limit_bytes=VMEM_LIMIT)


def split(x):
    head = x.astype(BF16)
    return head, (x - head.astype(F32)).astype(BF16)


def dot(a, b, dims):
    return lax.dot_general(a, b, dims, preferred_element_type=F32)


def tiles(size):
    step = min(TILE, size)
    return [slice(start, start + step) for start in range(0, size, step)]


def in_hbm(x):
    return pltpu.with_memory_space_constraint(x, pltpu.MemorySpace.HBM)


def stream(copies, use):
    for copy in copies[:AHEAD]:
        copy.start()
    for k, copy in enumerate(copies):
        copy.wait()
        if k + AHEAD < len(copies):
            copies[k + AHEAD].start()
        use(k)


def tall_kernel(x_hbm, s_hbm, out_ref, x_buf, s_buf, head_buf, rest_buf, x_sems, s_sems):
    blocks, _, unit = x_buf.shape
    rank = s_hbm.shape[0]

    def copies(k):
        where = pl.ds(k * unit, unit)
        return (
            pltpu.make_async_copy(s_hbm.at[:, where], s_buf.at[k], s_sems.at[k]),
            pltpu.make_async_copy(x_hbm.at[:, where], x_buf.at[k], x_sems.at[k]),
        )

    for k in range(blocks):
        for copy in copies(k):
            copy.start()
    for k in range(blocks):
        for copy in copies(k):
            copy.wait()
        s_head, s_rest = split(s_buf[k])
        s_both = jnp.concatenate([s_head, s_rest], axis=0)
        x_head, x_rest = split(x_buf[k])
        head_buf[k] = x_head
        rest_buf[k] = x_rest
        both = dot(s_both, x_head, LAST)
        part = both[:rank] + (both[rank:] + dot(s_head, x_rest, LAST))
        if k == 0:
            out_ref[...] = part
        else:
            out_ref[...] += part


def tall_partial(probes, sketch_t):
    rows, cols = probes.shape
    rank = sketch_t.shape[0]
    unit = min(2 * UNIT, cols)
    blocks = cols // unit
    return pl.pallas_call(
        tall_kernel,
        in_specs=[HBM, HBM],
        out_specs=WHOLE,
        out_shape=jax.ShapeDtypeStruct((rank, rows), F32),
        scratch_shapes=[
            pltpu.VMEM((blocks, rows, unit), F32),
            pltpu.VMEM((blocks, rank, unit), F32),
            pltpu.VMEM((blocks, rows, unit), BF16),
            pltpu.VMEM((blocks, rows, unit), BF16),
            pltpu.SemaphoreType.DMA((blocks,)),
            pltpu.SemaphoreType.DMA((blocks,)),
        ],
        compiler_params=PARAMS,
        cost_estimate=pl.CostEstimate(
            flops=6 * rows * cols * rank, bytes_accessed=4 * rows * cols, transcendentals=0
        ),
        name="tall_partial",
    )(in_hbm(probes), in_hbm(sketch_t))


def multiply_blocks(both_ref, which_ref, x_hbm, x_buf, sems, plan, outs):
    rank = outs[0].shape[0]
    unit = x_buf.shape[2]
    copies = [
        pltpu.make_async_copy(
            x_hbm.at[:, pl.ds(pl.multiple_of(which_ref[k] * unit, unit), unit)],
            x_buf.at[k],
            sems.at[k],
        )
        for k in range(len(plan))
    ]

    def use(k):
        out, offset = plan[k]
        for cols in tiles(unit):
            total = None
            for rows in tiles(x_buf.shape[1]):
                x_head, x_rest = split(x_buf[k, rows, cols])
                both = dot(both_ref[:, rows], x_head, PLAIN)
                part = both[:rank] + (both[rank:] + dot(both_ref[:rank, rows], x_rest, PLAIN))
                total = part if total is None else total + part
            outs[out][:, offset + cols.start : offset + cols.stop] = total

    return copies, use


def first_kernel(plan, grams, which_ref, one_ref, two_ref, x_hbm, both_ref, gram_ref, *refs):
    outs, (x_buf, sems) = refs[:-2], refs[-2:]
    copies, use = multiply_blocks(both_ref, which_ref, x_hbm, x_buf, sems, plan, outs)

    def whole_tall():
        odd = which_ref[len(plan)] == 1
        one, two = one_ref[...], two_ref[...]
        return jnp.concatenate([jnp.where(odd, two, one), jnp.where(odd, one, two)], axis=1)

    def use_first(k):
        if k == 0:
            both_ref[...] = jnp.concatenate(split(whole_tall()), axis=0)
        use(k)

    stream(copies, use_first)
    tall = whole_tall()
    r = tall.shape[0]
    head, rest = split(tall)
    tail = (tall - head.astype(F32) - rest.astype(F32)).astype(BF16)
    three = jnp.concatenate([head, rest, tail], axis=0)
    g = dot(three, three, LAST)
    cross = g[:r, r : 2 * r] + g[r : 2 * r, :r]
    small = g[:r, 2 * r :] + g[2 * r :, :r] + g[r : 2 * r, r : 2 * r]
    gram = g[:r, :r] + (cross + small)
    gram_ref[...] = jnp.concatenate([gram, jnp.zeros((r, LANES - r), F32)], axis=1)
    for out, offset in grams:
        outs[out][:, offset : offset + LANES] = gram_ref[...]


def rest_kernel(plan, grams, which_ref, both_ref, gram_ref, x_hbm, after_ref, *refs):
    outs, (x_buf, sems) = refs[:-2], refs[-2:]
    copies, use = multiply_blocks(both_ref, which_ref, x_hbm, x_buf, sems, plan, outs)
    stream(copies, use)
    for out, offset in grams:
        outs[out][:, offset : offset + LANES] = gram_ref[...]


def layout(outputs, sub):
    unit = min(UNIT, sub)
    plan, grams, widths, which = [], [], [], []
    for out, (blocks, with_gram) in enumerate(outputs):
        extra = LANES if with_gram else 0
        for j, block in enumerate(blocks):
            for part in range(sub // unit):
                plan.append((out, j * sub + part * unit + (extra if j else 0)))
                which.append(block * (sub // unit) + part)
        if with_gram:
            grams.append((out, sub))
        widths.append(len(blocks) * sub + extra)
    return unit, plan, grams, widths, which


def products(kernel, inputs, in_specs, made, probes, outputs, sub, name, table=()):
    rows = probes.shape[0]
    rank = inputs[1].shape[0]
    unit, plan, grams, widths, which = layout(outputs, sub)
    shapes = [*made, *[jax.ShapeDtypeStruct((rank, width), F32) for width in widths]]
    return pl.pallas_call(
        functools.partial(kernel, plan, grams),
        in_specs=[TABLE, *in_specs],
        out_specs=[WHOLE] * len(shapes),
        out_shape=shapes,
        scratch_shapes=[
            pltpu.VMEM((len(plan), rows, unit), F32),
            pltpu.SemaphoreType.DMA((len(plan),)),
        ],
        compiler_params=PARAMS,
        cost_estimate=pl.CostEstimate(
            flops=6 * rows * rank * unit * len(plan),
            bytes_accessed=4 * rows * unit * len(plan),
            transcendentals=0,
        ),
        name=name,
    )(jnp.stack([*which, *table]), *inputs)


def first_products(one, two, odd, probes, outputs, sub):
    rank, rows = one.shape[0], 2 * one.shape[1]
    made = [
        jax.ShapeDtypeStruct((2 * rank, rows), BF16),
        jax.ShapeDtypeStruct((rank, LANES), F32),
    ]
    both, gram, *outs = products(
        first_kernel,
        [one, two, in_hbm(probes)],
        [WHOLE, WHOLE, HBM],
        made,
        probes,
        outputs,
        sub,
        "first_products",
        (odd,),
    )
    return both, gram, outs


def rest_products(both, gram, probes, outputs, sub, after):
    return products(
        rest_kernel,
        [both, gram, in_hbm(probes), after],
        [WHOLE, WHOLE, HBM, ANYWHERE],
        [],
        probes,
        outputs,
        sub,
        "rest_products",
    )


def inverse_kernel(gram_ref, out_ref):
    rank = out_ref.shape[0]
    rows = lax.broadcasted_iota(jnp.int32, (rank, LANES), 0)
    cols = lax.broadcasted_iota(jnp.int32, (rank, LANES), 1)
    work = jnp.where(cols < rank, gram_ref[...], (cols == rows + rank).astype(F32))
    scale = jnp.ones((rank, LANES), F32)
    for start in range(0, rank, PANEL):
        panel = [
            jnp.broadcast_to(work[:, k : k + 1], (rank, LANES))
            for k in range(start, start + PANEL)
        ]
        for j in range(PANEL):
            k = start + j
            over = 1.0 / panel[j][k : k + 1, :]
            scale = jnp.where(rows == k, over, scale)
            factor = jnp.where(rows > k, panel[j] * over, 0.0)
            work = work - factor * work[k : k + 1, :]
            for later in range(j + 1, PANEL):
                panel[later] = panel[later] - factor * panel[later][k : k + 1, :]
    out_ref[...] = (work * jnp.sqrt(scale))[:, rank : 2 * rank]


def inverse_factor(chunk, start):
    rank = chunk.shape[0]
    return pl.pallas_call(
        inverse_kernel,
        grid=(1,),
        in_specs=[pl.BlockSpec((rank, LANES), lambda i: (0, start // LANES))],
        out_specs=pl.BlockSpec((rank, rank), lambda i: (0, 0)),
        out_shape=jax.ShapeDtypeStruct((rank, rank), F32),
        compiler_params=PARAMS,
        cost_estimate=pl.CostEstimate(
            flops=20_000_000, bytes_accessed=8 * rank * LANES, transcendentals=rank
        ),
        name="inverse_factor",
    )(chunk)


def finish_kernel(plan, where_ref, inverse_ref, *refs):
    out_hbm, buf, sems = refs[-3:]
    _, rank, width = buf.shape
    head, rest = split(inverse_ref[...])
    both = jnp.concatenate([head, rest], axis=0)
    copies = []
    for k, (source, offset) in enumerate(plan):
        p_head, p_rest = split(refs[source][:, offset : offset + width])
        first = dot(both, p_head, PLAIN)
        buf[k] = first[:rank] + (first[rank:] + dot(head, p_rest, PLAIN))
        where = pl.ds(pl.multiple_of(where_ref[k] * width, width), width)
        copies.append(pltpu.make_async_copy(buf.at[k], out_hbm.at[:, where], sems.at[k]))
        copies[k].start()
    for copy in copies:
        copy.wait()


def finish(inverse, sources, pieces, width, total, before=None):
    rank = inverse.shape[0]
    count = len(pieces)
    in_specs = [TABLE, WHOLE, *[WHOLE] * len(sources)]
    args = [jnp.stack([piece[0] for piece in pieces]), inverse, *sources]
    aliases = {}
    if before is not None:
        in_specs.append(HBM)
        args.append(before)
        aliases = {len(args) - 1: 0}
    return pl.pallas_call(
        functools.partial(finish_kernel, [piece[1:] for piece in pieces]),
        in_specs=in_specs,
        out_specs=HBM,
        out_shape=jax.ShapeDtypeStruct((rank, total), F32),
        scratch_shapes=[
            pltpu.VMEM((count, rank, width), F32),
            pltpu.SemaphoreType.DMA((count,)),
        ],
        input_output_aliases=aliases,
        compiler_params=PARAMS,
        cost_estimate=pl.CostEstimate(
            flops=6 * rank * rank * width * count,
            bytes_accessed=8 * rank * width * count,
            transcendentals=0,
        ),
        name="finish",
    )(*args)


def body(n_pos, n_pix, probes, sketch):
    def swap(value, axis, size, bit):
        return lax.ppermute(value, axis, [(i, i ^ bit) for i in range(size)])

    def over(value, bit):
        return swap(value, "pos", n_pos, bit)

    me = lax.axis_index("pos").astype(jnp.int32)
    near, far = me & 1, (me >> 1) & 1
    cols = probes.shape[1]
    width = cols // (8 * CHUNKS)

    tall = tall_partial(probes, sketch.T)
    odd = lax.axis_index("pix").astype(jnp.int32) & 1
    if n_pix == 4:
        tall = tall + swap(tall, "pix", n_pix, 1)
        middle = tall.shape[1] // 2
        half = jnp.where(odd == 1, tall[:, middle:], tall[:, :middle])
        half = half + swap(half, "pix", n_pix, 2)
        rest = swap(half, "pix", n_pix, 1)
    else:
        tall = lax.psum(tall, "pix")
        middle = tall.shape[1] // 2
        half = jnp.where(odd == 1, tall[:, middle:], tall[:, :middle])
        rest = jnp.where(odd == 1, tall[:, :middle], tall[:, middle:])

    def block_a(c, p, q):
        return 8 * c + 2 * (near ^ p) + (far ^ q)

    def block_b(c, p, q):
        return 8 * c + 4 + 2 * (far ^ p) + (near ^ q)

    def outputs(c, p):
        return [
            ([block_a(c, p, 1), block_a(c, p, 0)], c == 0),
            ([block_b(c, p, 1), block_b(c, p, 0)], False),
        ]

    both, gram, away = first_products(half, rest, odd, probes, outputs(0, 1), width)

    plan = [(c, p) for c in range(CHUNKS) for p in (1, 0) if (c, p) != (0, 1)]
    rest = rest_products(
        both, gram, probes, [out for c, p in plan for out in outputs(c, p)], width, away[0]
    )
    made = {(0, 1): away}
    made.update({key: rest[2 * k : 2 * k + 2] for k, key in enumerate(plan)})

    inverse = None
    sources, pieces = [], []
    for c in range(CHUNKS):
        g = LANES if c == 0 else 0
        away_a, away_b = made[c, 1]
        own_a, own_b = made[c, 0]
        got_a = over(away_a, 1)
        sum_a = own_a + got_a
        sum_b = own_b + over(away_b, 2)
        send_a, send_b = sum_a[:, : width + g], sum_b[:, :width]
        if c > 0:
            send_a, send_b, whole = lax.optimization_barrier((send_a, send_b, whole))
        got_a = over(send_a, 2)
        got_b = over(send_b, 1)
        whole = jnp.concatenate(
            [
                sum_a[:, width + g :] + got_a[:, :width],
                sum_a[:, width : width + g] + got_a[:, width:],
                sum_b[:, width:] + got_b,
            ],
            axis=1,
        )
        total = whole
        bit = 4
        while bit < n_pos:
            total = total + over(total, bit)
            bit *= 2
        if c == 0:
            inverse = inverse_factor(total, width)
        mine_a, mine_b = total[:, :width], total[:, width + g :]
        if c > 0:
            mine_a, mine_b, inverse = lax.optimization_barrier((mine_a, mine_b, inverse))
        next_a = over(mine_a, 2)
        next_b = over(mine_b, 1)
        last_a = over(jnp.concatenate([mine_a, next_a], axis=1), 1)
        last_b = over(jnp.concatenate([mine_b, next_b], axis=1), 2)
        k = len(sources)
        sources += [total, next_a, next_b, last_a, last_b]
        pieces += [
            (block_a(c, 0, 0), k, 0),
            (block_b(c, 0, 0), k, width + g),
            (block_a(c, 0, 1), k + 1, 0),
            (block_b(c, 0, 1), k + 2, 0),
            (block_a(c, 1, 0), k + 3, 0),
            (block_a(c, 1, 1), k + 3, width),
            (block_b(c, 1, 0), k + 4, 0),
            (block_b(c, 1, 1), k + 4, width),
        ]
    out = finish(inverse, sources[:-2], pieces[:-4], width, cols)
    pieces = [(where, source - k - 3, start) for where, source, start in pieces[-4:]]
    return finish(inverse, sources[-2:], pieces, width, cols, out)


def solution(mesh):
    in_specs = (P("pos", "pix"), P("pix", None))
    out_specs = P(None, "pix")
    run = functools.partial(body, mesh.shape["pos"], mesh.shape["pix"])
    return jax.shard_map(run, mesh=mesh, in_specs=in_specs, out_specs=out_specs, check_vma=False)
```

```python
import functools

import jax
import jax.numpy as jnp
from jax import lax
from jax.experimental import pallas as pl
from jax.experimental.pallas import tpu as pltpu
from jax.sharding import PartitionSpec as P

F32 = jnp.float32
BF16 = jnp.bfloat16
VMEM_LIMIT = 40 * 1024 * 1024
LANES = 128
CHUNKS = 2
AHEAD = 8
UNIT = 512
TILE = 256
PANEL = 4
LAST = (((1,), (1,)), ((), ()))
PLAIN = (((1,), (0,)), ((), ()))
ANYWHERE = pl.BlockSpec(memory_space=pl.ANY)
HBM = pl.BlockSpec(memory_space=pltpu.MemorySpace.HBM)
WHOLE = pl.BlockSpec(memory_space=pltpu.VMEM)
TABLE = pl.BlockSpec(memory_space=pltpu.SMEM)
PARAMS = pltpu.CompilerParams(vmem_limit_bytes=VMEM_LIMIT)


def split(x):
    head = x.astype(BF16)
    return head, (x - head.astype(F32)).astype(BF16)


def dot(a, b, dims):
    return lax.dot_general(a, b, dims, preferred_element_type=F32)


def tiles(size):
    step = min(TILE, size)
    return [slice(start, start + step) for start in range(0, size, step)]


def in_hbm(x):
    return pltpu.with_memory_space_constraint(x, pltpu.MemorySpace.HBM)


def stream(copies, use):
    for copy in copies[:AHEAD]:
        copy.start()
    for k, copy in enumerate(copies):
        copy.wait()
        if k + AHEAD < len(copies):
            copies[k + AHEAD].start()
        use(k)


def tall_kernel(x_hbm, s_hbm, out_ref, x_buf, s_buf, head_buf, rest_buf, x_sems, s_sems):
    blocks, _, unit = x_buf.shape
    rank = s_hbm.shape[0]

    def copies(k):
        where = pl.ds(k * unit, unit)
        return (
            pltpu.make_async_copy(s_hbm.at[:, where], s_buf.at[k], s_sems.at[k]),
            pltpu.make_async_copy(x_hbm.at[:, where], x_buf.at[k], x_sems.at[k]),
        )

    for k in range(blocks):
        for copy in copies(k):
            copy.start()
    for k in range(blocks):
        for copy in copies(k):
            copy.wait()
        s_head, s_rest = split(s_buf[k])
        s_both = jnp.concatenate([s_head, s_rest], axis=0)
        x_head, x_rest = split(x_buf[k])
        head_buf[k] = x_head
        rest_buf[k] = x_rest
        both = dot(s_both, x_head, LAST)
        part = both[:rank] + (both[rank:] + dot(s_head, x_rest, LAST))
        if k == 0:
            out_ref[...] = part
        else:
            out_ref[...] += part


def tall_partial(probes, sketch_t):
    rows, cols = probes.shape
    rank = sketch_t.shape[0]
    unit = min(2 * UNIT, cols)
    blocks = cols // unit
    return pl.pallas_call(
        tall_kernel,
        in_specs=[HBM, HBM],
        out_specs=WHOLE,
        out_shape=jax.ShapeDtypeStruct((rank, rows), F32),
        scratch_shapes=[
            pltpu.VMEM((blocks, rows, unit), F32),
            pltpu.VMEM((blocks, rank, unit), F32),
            pltpu.VMEM((blocks, rows, unit), BF16),
            pltpu.VMEM((blocks, rows, unit), BF16),
            pltpu.SemaphoreType.DMA((blocks,)),
            pltpu.SemaphoreType.DMA((blocks,)),
        ],
        compiler_params=PARAMS,
        cost_estimate=pl.CostEstimate(
            flops=6 * rows * cols * rank, bytes_accessed=4 * rows * cols, transcendentals=0
        ),
        name="tall_partial",
    )(in_hbm(probes), in_hbm(sketch_t))


def multiply_blocks(both_ref, which_ref, x_hbm, x_buf, sems, plan, outs):
    rank = outs[0].shape[0]
    unit = x_buf.shape[2]
    copies = [
        pltpu.make_async_copy(
            x_hbm.at[:, pl.ds(pl.multiple_of(which_ref[k] * unit, unit), unit)],
            x_buf.at[k],
            sems.at[k],
        )
        for k in range(len(plan))
    ]

    def use(k):
        out, offset = plan[k]
        for cols in tiles(unit):
            total = None
            for rows in tiles(x_buf.shape[1]):
                x_head, x_rest = split(x_buf[k, rows, cols])
                both = dot(both_ref[:, rows], x_head, PLAIN)
                part = both[:rank] + (both[rank:] + dot(both_ref[:rank, rows], x_rest, PLAIN))
                total = part if total is None else total + part
            outs[out][:, offset + cols.start : offset + cols.stop] = total

    return copies, use


def first_kernel(plan, early, grams, table, one_ref, two_ref, x_hbm, both_ref, gram_ref, *refs):
    outs, (x_buf, sems) = refs[:-2], refs[-2:]
    copies, use = multiply_blocks(both_ref, table, x_hbm, x_buf, sems, plan, outs)

    def use_first(k):
        if k == 0:
            tall = one_ref[...] + two_ref[...]
            head, rest = split(tall)
            both_ref[...] = jnp.concatenate([head, rest], axis=0)
        use(k)

    stream(copies[:early], use_first)

    @pl.when(table[len(plan)] == 1)
    def _():
        stream(copies[early:], lambda k: use(early + k))

    tall = one_ref[...] + two_ref[...]
    r = tall.shape[0]
    head, rest = split(tall)
    tail = (tall - head.astype(F32) - rest.astype(F32)).astype(BF16)
    three = jnp.concatenate([head, rest, tail], axis=0)
    g = dot(three, three, LAST)
    cross = g[:r, r : 2 * r] + g[r : 2 * r, :r]
    small = g[:r, 2 * r :] + g[2 * r :, :r] + g[r : 2 * r, r : 2 * r]
    gram = g[:r, :r] + (cross + small)
    gram_ref[...] = jnp.concatenate([gram, jnp.zeros((r, LANES - r), F32)], axis=1)
    for out, offset in grams:
        outs[out][:, offset : offset + LANES] = gram_ref[...]


def rest_kernel(plan, grams, table, both_ref, gram_ref, x_hbm, *refs):
    count = len(refs) // 2 - 1
    outs, (x_buf, sems) = refs[count:-2], refs[-2:]
    copies, use = multiply_blocks(both_ref, table, x_hbm, x_buf, sems, plan, outs)

    @pl.when(table[len(plan)] == 0)
    def _():
        stream(copies, use)
        for out, offset in grams:
            outs[out][:, offset : offset + LANES] = gram_ref[...]

    @pl.when(table[len(plan)] == 1)
    def _():
        for out_ref, made_ref in zip(outs, refs[:count]):
            out_ref[...] = made_ref[...]


def layout(outputs, sub):
    unit = min(UNIT, sub)
    plan, grams, widths, which = [], [], [], []
    for out, (blocks, with_gram) in enumerate(outputs):
        extra = LANES if with_gram else 0
        for j, block in enumerate(blocks):
            for part in range(sub // unit):
                plan.append((out, j * sub + part * unit + (extra if j else 0)))
                which.append(block * (sub // unit) + part)
        if with_gram:
            grams.append((out, sub))
        widths.append(len(blocks) * sub + extra)
    return unit, plan, grams, widths, which


def product_call(kernel, inputs, in_specs, shapes, rows, unit, count, name):
    return pl.pallas_call(
        kernel,
        in_specs=[TABLE, *in_specs],
        out_specs=[WHOLE] * len(shapes),
        out_shape=shapes,
        scratch_shapes=[
            pltpu.VMEM((count, rows, unit), F32),
            pltpu.SemaphoreType.DMA((count,)),
        ],
        compiler_params=PARAMS,
        cost_estimate=pl.CostEstimate(
            flops=6 * rows * shapes[-1].shape[0] * unit * count,
            bytes_accessed=4 * rows * unit * count,
            transcendentals=0,
        ),
        name=name,
    )(*inputs)


def products(one, two, probes, away, own, sub, late):
    rank, rows = one.shape
    unit, plan, grams, widths, which = layout(away + own, sub)
    early = len(layout(away, sub)[1])
    chunks = [jax.ShapeDtypeStruct((rank, width), F32) for width in widths]
    made = [
        jax.ShapeDtypeStruct((2 * rank, rows), BF16),
        jax.ShapeDtypeStruct((rank, LANES), F32),
    ]
    x = in_hbm(probes)
    both, gram, *outs = product_call(
        functools.partial(first_kernel, plan, early, grams),
        [jnp.stack([*which, late]), one, two, x],
        [WHOLE, WHOLE, HBM],
        made + chunks,
        rows,
        unit,
        len(plan),
        "first_products",
    )
    away_outs, own_outs = outs[: len(away)], outs[len(away) :]
    unit, plan, grams, widths, which = layout(own, sub)
    own_outs = product_call(
        functools.partial(rest_kernel, plan, grams),
        [jnp.stack([*which, late]), both, gram, x, *own_outs],
        [WHOLE, WHOLE, HBM, *[WHOLE] * len(own_outs)],
        chunks[len(away) :],
        rows,
        unit,
        len(plan),
        "rest_products",
    )
    return away_outs, own_outs


def inverse_kernel(gram_ref, out_ref):
    rank = out_ref.shape[0]
    rows = lax.broadcasted_iota(jnp.int32, (rank, LANES), 0)
    cols = lax.broadcasted_iota(jnp.int32, (rank, LANES), 1)
    work = jnp.where(cols < rank, gram_ref[...], (cols == rows + rank).astype(F32))
    scale = jnp.ones((rank, LANES), F32)
    for start in range(0, rank, PANEL):
        panel = [
            jnp.broadcast_to(work[:, k : k + 1], (rank, LANES))
            for k in range(start, start + PANEL)
        ]
        for j in range(PANEL):
            k = start + j
            over = 1.0 / panel[j][k : k + 1, :]
            scale = jnp.where(rows == k, over, scale)
            factor = jnp.where(rows > k, panel[j] * over, 0.0)
            work = work - factor * work[k : k + 1, :]
            for later in range(j + 1, PANEL):
                panel[later] = panel[later] - factor * panel[later][k : k + 1, :]
    out_ref[...] = (work * jnp.sqrt(scale))[:, rank : 2 * rank]


def inverse_factor(chunk, start):
    rank = chunk.shape[0]
    return pl.pallas_call(
        inverse_kernel,
        grid=(1,),
        in_specs=[pl.BlockSpec((rank, LANES), lambda i: (0, start // LANES))],
        out_specs=pl.BlockSpec((rank, rank), lambda i: (0, 0)),
        out_shape=jax.ShapeDtypeStruct((rank, rank), F32),
        compiler_params=PARAMS,
        cost_estimate=pl.CostEstimate(
            flops=20_000_000, bytes_accessed=8 * rank * LANES, transcendentals=rank
        ),
        name="inverse_factor",
    )(chunk)


def finish_kernel(plan, where_ref, inverse_ref, *refs):
    out_hbm, buf, sems = refs[-3:]
    _, rank, width = buf.shape
    head, rest = split(inverse_ref[...])
    both = jnp.concatenate([head, rest], axis=0)
    copies = []
    for k, (source, offset) in enumerate(plan):
        p_head, p_rest = split(refs[source][:, offset : offset + width])
        first = dot(both, p_head, PLAIN)
        buf[k] = first[:rank] + (first[rank:] + dot(head, p_rest, PLAIN))
        where = pl.ds(pl.multiple_of(where_ref[k] * width, width), width)
        copies.append(pltpu.make_async_copy(buf.at[k], out_hbm.at[:, where], sems.at[k]))
        copies[k].start()
    for copy in copies:
        copy.wait()


def finish(inverse, sources, pieces, width, total, before=None):
    rank = inverse.shape[0]
    count = len(pieces)
    in_specs = [TABLE, WHOLE, *[WHOLE] * len(sources)]
    args = [jnp.stack([piece[0] for piece in pieces]), inverse, *sources]
    aliases = {}
    if before is not None:
        in_specs.append(HBM)
        args.append(before)
        aliases = {len(args) - 1: 0}
    return pl.pallas_call(
        functools.partial(finish_kernel, [piece[1:] for piece in pieces]),
        in_specs=in_specs,
        out_specs=HBM,
        out_shape=jax.ShapeDtypeStruct((rank, total), F32),
        scratch_shapes=[
            pltpu.VMEM((count, rank, width), F32),
            pltpu.SemaphoreType.DMA((count,)),
        ],
        input_output_aliases=aliases,
        compiler_params=PARAMS,
        cost_estimate=pl.CostEstimate(
            flops=6 * rank * rank * width * count,
            bytes_accessed=8 * rank * width * count,
            transcendentals=0,
        ),
        name="finish",
    )(*args)


def body(n_pos, n_pix, probes, sketch):
    def swap(value, axis, size, bit):
        return lax.ppermute(value, axis, [(i, i ^ bit) for i in range(size)])

    def over(value, bit):
        return swap(value, "pos", n_pos, bit)

    me = lax.axis_index("pos").astype(jnp.int32)
    near, far = me & 1, (me >> 1) & 1
    cols = probes.shape[1]
    width = cols // (8 * CHUNKS)

    tall = tall_partial(probes, sketch.T)
    bit = 1
    while 2 * bit < n_pix:
        tall = tall + swap(tall, "pix", n_pix, bit)
        bit *= 2
    other = swap(tall, "pix", n_pix, bit)

    def block_a(c, p, q):
        return 8 * c + 2 * (near ^ p) + (far ^ q)

    def block_b(c, p, q):
        return 8 * c + 4 + 2 * (far ^ p) + (near ^ q)

    def outputs(c, p):
        return [
            ([block_a(c, p, 1), block_a(c, p, 0)], c == 0),
            ([block_b(c, p, 1), block_b(c, p, 0)], False),
        ]

    late = lax.axis_index("pix").astype(jnp.int32) & 1
    plan = [(c, p) for c in range(CHUNKS) for p in (1, 0) if (c, p) != (0, 1)]
    away, rest = products(
        tall, other, probes, outputs(0, 1), [o for c, p in plan for o in outputs(c, p)], width, late
    )
    made = {(0, 1): away}
    made.update({key: rest[2 * k : 2 * k + 2] for k, key in enumerate(plan)})

    def after(value, *others):
        return lax.optimization_barrier((value, *others))[0]

    whole, total = [], []
    for c in range(CHUNKS):
        g = LANES if c == 0 else 0
        away_a, away_b = made[c, 1]
        own_a, own_b = made[c, 0]
        if c > 0:
            away_a, away_b = after(away_a, sum_a, sum_b), after(away_b, sum_a, sum_b)
        sum_a = own_a + over(away_a, 1)
        sum_b = own_b + over(away_b, 2)
        send_a, send_b = sum_a[:, : width + g], sum_b[:, :width]
        if c > 0:
            send_a, send_b = after(send_a, whole[-1]), after(send_b, whole[-1])
        got_a = over(send_a, 2)
        got_b = over(send_b, 1)
        whole.append(
            jnp.concatenate(
                [
                    sum_a[:, width + g :] + got_a[:, :width],
                    sum_a[:, width : width + g] + got_a[:, width:],
                    sum_b[:, width:] + got_b,
                ],
                axis=1,
            )
        )
        added = whole[-1]
        bit = 4
        while bit < n_pos:
            added = added + over(added, bit)
            bit *= 2
        total.append(added)

    inverse = inverse_factor(total[0], width)
    sources, pieces = [], []
    for c in range(CHUNKS):
        g = LANES if c == 0 else 0
        mine_a, mine_b = total[c][:, :width], total[c][:, width + g :]
        if c > 0:
            mine_a, mine_b = after(mine_a, inverse), after(mine_b, inverse)
        next_a = over(mine_a, 2)
        next_b = over(mine_b, 1)
        both_a = jnp.concatenate([mine_a, next_a], axis=1)
        both_b = jnp.concatenate([mine_b, next_b], axis=1)
        if c + 1 < CHUNKS:
            both_a, both_b = after(both_a, total[c + 1]), after(both_b, total[c + 1])
        last_a = over(both_a, 1)
        last_b = over(both_b, 2)
        k = len(sources)
        sources += [total[c], next_a, next_b, last_a, last_b]
        pieces += [
            (block_a(c, 0, 0), k, 0),
            (block_b(c, 0, 0), k, width + g),
            (block_a(c, 0, 1), k + 1, 0),
            (block_b(c, 0, 1), k + 2, 0),
            (block_a(c, 1, 0), k + 3, 0),
            (block_a(c, 1, 1), k + 3, width),
            (block_b(c, 1, 0), k + 4, 0),
            (block_b(c, 1, 1), k + 4, width),
        ]
    out = finish(inverse, sources[:-2], pieces[:-4], width, cols)
    pieces = [(where, source - k - 3, start) for where, source, start in pieces[-4:]]
    return finish(inverse, sources[-2:], pieces, width, cols, out)


def solution(mesh):
    in_specs = (P("pos", "pix"), P("pix", None))
    out_specs = P(None, "pix")
    run = functools.partial(body, mesh.shape["pos"], mesh.shape["pix"])
    return jax.shard_map(run, mesh=mesh, in_specs=in_specs, out_specs=out_specs, check_vma=False)
```

```python
import functools

import jax
import jax.numpy as jnp
from jax import lax
from jax.experimental import pallas as pl
from jax.experimental.pallas import tpu as pltpu
from jax.sharding import PartitionSpec as P

F32 = jnp.float32
BF16 = jnp.bfloat16
VMEM_LIMIT = 40 * 1024 * 1024
LANES = 128
CHUNKS = 2
AHEAD = 6
UNIT = 512
PANEL = 4
LAST = (((1,), (1,)), ((), ()))
PLAIN = (((1,), (0,)), ((), ()))
ANYWHERE = pl.BlockSpec(memory_space=pl.ANY)
HBM = pl.BlockSpec(memory_space=pltpu.MemorySpace.HBM)
WHOLE = pl.BlockSpec(memory_space=pltpu.VMEM)
TABLE = pl.BlockSpec(memory_space=pltpu.SMEM)
PARAMS = pltpu.CompilerParams(vmem_limit_bytes=VMEM_LIMIT)


def split(x):
    head = x.astype(BF16)
    return head, (x - head.astype(F32)).astype(BF16)


def dot(a, b, dims):
    return lax.dot_general(a, b, dims, preferred_element_type=F32)


def in_hbm(x):
    return pltpu.with_memory_space_constraint(x, pltpu.MemorySpace.HBM)


def stream(copies, use):
    for copy in copies[:AHEAD]:
        copy.start()
    for k, copy in enumerate(copies):
        copy.wait()
        if k + AHEAD < len(copies):
            copies[k + AHEAD].start()
        use(k)


def tall_kernel(x_hbm, s_hbm, out_ref, x_buf, s_buf, head_buf, rest_buf, x_sems, s_sems):
    blocks, _, unit = x_buf.shape
    rank = s_hbm.shape[0]

    def copies(k):
        where = pl.ds(k * unit, unit)
        return (
            pltpu.make_async_copy(s_hbm.at[:, where], s_buf.at[k], s_sems.at[k]),
            pltpu.make_async_copy(x_hbm.at[:, where], x_buf.at[k], x_sems.at[k]),
        )

    for k in range(blocks):
        for copy in copies(k):
            copy.start()
    for k in range(blocks):
        for copy in copies(k):
            copy.wait()
        s_head, s_rest = split(s_buf[k])
        s_both = jnp.concatenate([s_head, s_rest], axis=0)
        x_head, x_rest = split(x_buf[k])
        head_buf[k] = x_head
        rest_buf[k] = x_rest
        both = dot(s_both, x_head, LAST)
        part = both[:rank] + (both[rank:] + dot(s_head, x_rest, LAST))
        if k == 0:
            out_ref[...] = part
        else:
            out_ref[...] += part


def tall_partial(probes, sketch_t):
    rows, cols = probes.shape
    rank = sketch_t.shape[0]
    unit = min(2 * UNIT, cols)
    blocks = cols // unit
    return pl.pallas_call(
        tall_kernel,
        in_specs=[HBM, HBM],
        out_specs=WHOLE,
        out_shape=jax.ShapeDtypeStruct((rank, rows), F32),
        scratch_shapes=[
            pltpu.VMEM((blocks, rows, unit), F32),
            pltpu.VMEM((blocks, rank, unit), F32),
            pltpu.VMEM((blocks, rows, unit), BF16),
            pltpu.VMEM((blocks, rows, unit), BF16),
            pltpu.SemaphoreType.DMA((blocks,)),
            pltpu.SemaphoreType.DMA((blocks,)),
        ],
        compiler_params=PARAMS,
        cost_estimate=pl.CostEstimate(
            flops=6 * rows * cols * rank, bytes_accessed=4 * rows * cols, transcendentals=0
        ),
        name="tall_partial",
    )(in_hbm(probes), in_hbm(sketch_t))


def multiply_blocks(both_ref, which_ref, x_hbm, x_buf, sems, plan, outs):
    rank = outs[0].shape[0]
    unit = x_buf.shape[2]
    copies = [
        pltpu.make_async_copy(
            x_hbm.at[:, pl.ds(pl.multiple_of(which_ref[k] * unit, unit), unit)],
            x_buf.at[k],
            sems.at[k],
        )
        for k in range(len(plan))
    ]

    def use(k):
        both = both_ref[...]
        x_head, x_rest = split(x_buf[k])
        first = dot(both, x_head, PLAIN)
        second = dot(both[:rank], x_rest, PLAIN)
        out, offset = plan[k]
        outs[out][:, offset : offset + unit] = first[:rank] + (first[rank:] + second)

    return copies, use


def first_kernel(plan, grams, which_ref, one_ref, two_ref, x_hbm, both_ref, gram_ref, *refs):
    outs, (x_buf, sems) = refs[:-2], refs[-2:]
    copies, use = multiply_blocks(both_ref, which_ref, x_hbm, x_buf, sems, plan, outs)

    def use_first(k):
        if k == 0:
            tall = one_ref[...] + two_ref[...]
            head, rest = split(tall)
            both_ref[...] = jnp.concatenate([head, rest], axis=0)
        use(k)

    stream(copies, use_first)
    tall = one_ref[...] + two_ref[...]
    r = tall.shape[0]
    head, rest = split(tall)
    tail = (tall - head.astype(F32) - rest.astype(F32)).astype(BF16)
    three = jnp.concatenate([head, rest, tail], axis=0)
    g = dot(three, three, LAST)
    cross = g[:r, r : 2 * r] + g[r : 2 * r, :r]
    small = g[:r, 2 * r :] + g[2 * r :, :r] + g[r : 2 * r, r : 2 * r]
    gram = g[:r, :r] + (cross + small)
    gram_ref[...] = jnp.concatenate([gram, jnp.zeros((r, LANES - r), F32)], axis=1)
    for out, offset in grams:
        outs[out][:, offset : offset + LANES] = gram_ref[...]


def rest_kernel(plan, grams, which_ref, both_ref, gram_ref, x_hbm, after_ref, *refs):
    outs, (x_buf, sems) = refs[:-2], refs[-2:]
    copies, use = multiply_blocks(both_ref, which_ref, x_hbm, x_buf, sems, plan, outs)
    stream(copies, use)
    for out, offset in grams:
        outs[out][:, offset : offset + LANES] = gram_ref[...]


def layout(outputs, sub):
    unit = min(UNIT, sub)
    plan, grams, widths, which = [], [], [], []
    for out, (blocks, with_gram) in enumerate(outputs):
        extra = LANES if with_gram else 0
        for j, block in enumerate(blocks):
            for part in range(sub // unit):
                plan.append((out, j * sub + part * unit + (extra if j else 0)))
                which.append(block * (sub // unit) + part)
        if with_gram:
            grams.append((out, sub))
        widths.append(len(blocks) * sub + extra)
    return unit, plan, grams, widths, jnp.stack(which)


def products(kernel, inputs, in_specs, made, probes, outputs, sub, name):
    rows = probes.shape[0]
    rank = inputs[1].shape[0]
    unit, plan, grams, widths, which = layout(outputs, sub)
    shapes = [*made, *[jax.ShapeDtypeStruct((rank, width), F32) for width in widths]]
    return pl.pallas_call(
        functools.partial(kernel, plan, grams),
        in_specs=[TABLE, *in_specs],
        out_specs=[WHOLE] * len(shapes),
        out_shape=shapes,
        scratch_shapes=[
            pltpu.VMEM((len(plan), rows, unit), F32),
            pltpu.SemaphoreType.DMA((len(plan),)),
        ],
        compiler_params=PARAMS,
        cost_estimate=pl.CostEstimate(
            flops=6 * rows * rank * unit * len(plan),
            bytes_accessed=4 * rows * unit * len(plan),
            transcendentals=0,
        ),
        name=name,
    )(which, *inputs)


def first_products(one, two, probes, outputs, sub):
    rank, rows = one.shape
    made = [
        jax.ShapeDtypeStruct((2 * rank, rows), BF16),
        jax.ShapeDtypeStruct((rank, LANES), F32),
    ]
    both, gram, *outs = products(
        first_kernel,
        [one, two, in_hbm(probes)],
        [WHOLE, WHOLE, HBM],
        made,
        probes,
        outputs,
        sub,
        "first_products",
    )
    return both, gram, outs


def rest_products(both, gram, probes, outputs, sub, after):
    return products(
        rest_kernel,
        [both, gram, in_hbm(probes), after],
        [WHOLE, WHOLE, HBM, ANYWHERE],
        [],
        probes,
        outputs,
        sub,
        "rest_products",
    )


def inverse_kernel(gram_ref, out_ref):
    rank = out_ref.shape[0]
    rows = lax.broadcasted_iota(jnp.int32, (rank, LANES), 0)
    cols = lax.broadcasted_iota(jnp.int32, (rank, LANES), 1)
    work = jnp.where(cols < rank, gram_ref[...], (cols == rows + rank).astype(F32))
    scale = jnp.ones((rank, LANES), F32)
    for start in range(0, rank, PANEL):
        panel = [
            jnp.broadcast_to(work[:, k : k + 1], (rank, LANES))
            for k in range(start, start + PANEL)
        ]
        for j in range(PANEL):
            k = start + j
            over = 1.0 / panel[j][k : k + 1, :]
            scale = jnp.where(rows == k, over, scale)
            factor = jnp.where(rows > k, panel[j] * over, 0.0)
            work = work - factor * work[k : k + 1, :]
            for later in range(j + 1, PANEL):
                panel[later] = panel[later] - factor * panel[later][k : k + 1, :]
    out_ref[...] = (work * jnp.sqrt(scale))[:, rank : 2 * rank]


def inverse_factor(chunk, start):
    rank = chunk.shape[0]
    return pl.pallas_call(
        inverse_kernel,
        grid=(1,),
        in_specs=[pl.BlockSpec((rank, LANES), lambda i: (0, start // LANES))],
        out_specs=pl.BlockSpec((rank, rank), lambda i: (0, 0)),
        out_shape=jax.ShapeDtypeStruct((rank, rank), F32),
        compiler_params=PARAMS,
        cost_estimate=pl.CostEstimate(
            flops=20_000_000, bytes_accessed=8 * rank * LANES, transcendentals=rank
        ),
        name="inverse_factor",
    )(chunk)


def finish_kernel(plan, where_ref, inverse_ref, *refs):
    out_hbm, buf, sems = refs[-3:]
    _, rank, width = buf.shape
    head, rest = split(inverse_ref[...])
    both = jnp.concatenate([head, rest], axis=0)
    copies = []
    for k, (source, offset) in enumerate(plan):
        p_head, p_rest = split(refs[source][:, offset : offset + width])
        first = dot(both, p_head, PLAIN)
        buf[k] = first[:rank] + (first[rank:] + dot(head, p_rest, PLAIN))
        where = pl.ds(pl.multiple_of(where_ref[k] * width, width), width)
        copies.append(pltpu.make_async_copy(buf.at[k], out_hbm.at[:, where], sems.at[k]))
        copies[k].start()
    for copy in copies:
        copy.wait()


def finish(inverse, sources, pieces, width, total, before=None):
    rank = inverse.shape[0]
    count = len(pieces)
    in_specs = [TABLE, WHOLE, *[WHOLE] * len(sources)]
    args = [jnp.stack([piece[0] for piece in pieces]), inverse, *sources]
    aliases = {}
    if before is not None:
        in_specs.append(HBM)
        args.append(before)
        aliases = {len(args) - 1: 0}
    return pl.pallas_call(
        functools.partial(finish_kernel, [piece[1:] for piece in pieces]),
        in_specs=in_specs,
        out_specs=HBM,
        out_shape=jax.ShapeDtypeStruct((rank, total), F32),
        scratch_shapes=[
            pltpu.VMEM((count, rank, width), F32),
            pltpu.SemaphoreType.DMA((count,)),
        ],
        input_output_aliases=aliases,
        compiler_params=PARAMS,
        cost_estimate=pl.CostEstimate(
            flops=6 * rank * rank * width * count,
            bytes_accessed=8 * rank * width * count,
            transcendentals=0,
        ),
        name="finish",
    )(*args)


def body(n_pos, n_pix, probes, sketch):
    def swap(value, axis, size, bit):
        return lax.ppermute(value, axis, [(i, i ^ bit) for i in range(size)])

    def over(value, bit):
        return swap(value, "pos", n_pos, bit)

    me = lax.axis_index("pos").astype(jnp.int32)
    near, far = me & 1, (me >> 1) & 1
    cols = probes.shape[1]
    width = cols // (8 * CHUNKS)

    tall = tall_partial(probes, sketch.T)
    bit = 1
    while 2 * bit < n_pix:
        tall = tall + swap(tall, "pix", n_pix, bit)
        bit *= 2
    other = swap(tall, "pix", n_pix, bit)

    def block_a(c, p, q):
        return 8 * c + 2 * (near ^ p) + (far ^ q)

    def block_b(c, p, q):
        return 8 * c + 4 + 2 * (far ^ p) + (near ^ q)

    def outputs(c, p):
        return [
            ([block_a(c, p, 1), block_a(c, p, 0)], c == 0),
            ([block_b(c, p, 1), block_b(c, p, 0)], False),
        ]

    both, gram, away = first_products(tall, other, probes, outputs(0, 1), width)

    inverse, out, after = None, None, away[0]
    for c in range(CHUNKS):
        g = LANES if c == 0 else 0
        last = c == CHUNKS - 1
        made = rest_products(
            both, gram, probes, outputs(c, 0) + ([] if last else outputs(c + 1, 1)), width, after
        )
        away_a, away_b = away
        (own_a, own_b), away = made[:2], made[2:]
        got_a = over(away_a, 1)
        sum_a = own_a + got_a
        sum_b = own_b + over(away_b, 2)
        after = got_a
        send_a, send_b = sum_a[:, : width + g], sum_b[:, :width]
        if c > 0:
            send_a, send_b, whole = lax.optimization_barrier((send_a, send_b, whole))
        got_a = over(send_a, 2)
        got_b = over(send_b, 1)
        whole = jnp.concatenate(
            [
                sum_a[:, width + g :] + got_a[:, :width],
                sum_a[:, width : width + g] + got_a[:, width:],
                sum_b[:, width:] + got_b,
            ],
            axis=1,
        )
        total = whole
        bit = 4
        while bit < n_pos:
            total = total + over(total, bit)
            bit *= 2
        if c == 0:
            inverse = inverse_factor(total, width)
        mine_a, mine_b = total[:, :width], total[:, width + g :]
        if c > 0:
            mine_a, mine_b, inverse = lax.optimization_barrier((mine_a, mine_b, inverse))
        next_a = over(mine_a, 2)
        next_b = over(mine_b, 1)
        last_a = over(jnp.concatenate([mine_a, next_a], axis=1), 1)
        last_b = over(jnp.concatenate([mine_b, next_b], axis=1), 2)
        sources = [total, next_a, next_b]
        pieces = [
            (block_a(c, 0, 0), 0, 0),
            (block_b(c, 0, 0), 0, width + g),
            (block_a(c, 0, 1), 1, 0),
            (block_b(c, 0, 1), 2, 0),
        ]
        if last:
            out = finish(inverse, sources, pieces, width, cols, out)
            sources, pieces = [], []
        k = len(sources)
        sources += [last_a, last_b]
        pieces += [
            (block_a(c, 1, 0), k, 0),
            (block_a(c, 1, 1), k, width),
            (block_b(c, 1, 0), k + 1, 0),
            (block_b(c, 1, 1), k + 1, width),
        ]
        out = finish(inverse, sources, pieces, width, cols, out)
    return out


def solution(mesh):
    in_specs = (P("pos", "pix"), P("pix", None))
    out_specs = P(None, "pix")
    run = functools.partial(body, mesh.shape["pos"], mesh.shape["pix"])
    return jax.shard_map(run, mesh=mesh, in_specs=in_specs, out_specs=out_specs, check_vma=False)
```

```python
import functools

import jax
import jax.numpy as jnp
from jax import lax
from jax.experimental import pallas as pl
from jax.experimental.pallas import tpu as pltpu
from jax.sharding import PartitionSpec as P

F32 = jnp.float32
BF16 = jnp.bfloat16
VMEM_LIMIT = 40 * 1024 * 1024
LANES = 128
CHUNKS = 2
AHEAD = 16
UNIT = 256
TILE = 256
PANEL = 4
LAST = (((1,), (1,)), ((), ()))
PLAIN = (((1,), (0,)), ((), ()))
ANYWHERE = pl.BlockSpec(memory_space=pl.ANY)
HBM = pl.BlockSpec(memory_space=pltpu.MemorySpace.HBM)
WHOLE = pl.BlockSpec(memory_space=pltpu.VMEM)
TABLE = pl.BlockSpec(memory_space=pltpu.SMEM)
PARAMS = pltpu.CompilerParams(vmem_limit_bytes=VMEM_LIMIT)


def split(x):
    head = x.astype(BF16)
    return head, (x - head.astype(F32)).astype(BF16)


def dot(a, b, dims):
    return lax.dot_general(a, b, dims, preferred_element_type=F32)


def tiles(size):
    step = min(TILE, size)
    return [slice(start, start + step) for start in range(0, size, step)]


def in_hbm(x):
    return pltpu.with_memory_space_constraint(x, pltpu.MemorySpace.HBM)


def stream(copies, use):
    for copy in copies[:AHEAD]:
        copy.start()
    for k, copy in enumerate(copies):
        copy.wait()
        if k + AHEAD < len(copies):
            copies[k + AHEAD].start()
        use(k)


def tall_kernel(x_hbm, s_hbm, out_ref, x_buf, s_buf, head_buf, rest_buf, x_sems, s_sems):
    blocks, _, unit = x_buf.shape
    rank = s_hbm.shape[0]

    def copies(k):
        where = pl.ds(k * unit, unit)
        return (
            pltpu.make_async_copy(s_hbm.at[:, where], s_buf.at[k], s_sems.at[k]),
            pltpu.make_async_copy(x_hbm.at[:, where], x_buf.at[k], x_sems.at[k]),
        )

    for k in range(blocks):
        for copy in copies(k):
            copy.start()
    for k in range(blocks):
        for copy in copies(k):
            copy.wait()
        s_head, s_rest = split(s_buf[k])
        s_both = jnp.concatenate([s_head, s_rest], axis=0)
        x_head, x_rest = split(x_buf[k])
        head_buf[k] = x_head
        rest_buf[k] = x_rest
        both = dot(s_both, x_head, LAST)
        part = both[:rank] + (both[rank:] + dot(s_head, x_rest, LAST))
        if k == 0:
            out_ref[...] = part
        else:
            out_ref[...] += part


def tall_partial(probes, sketch_t):
    rows, cols = probes.shape
    rank = sketch_t.shape[0]
    unit = min(4 * UNIT, cols)
    blocks = cols // unit
    return pl.pallas_call(
        tall_kernel,
        in_specs=[HBM, HBM],
        out_specs=WHOLE,
        out_shape=jax.ShapeDtypeStruct((rank, rows), F32),
        scratch_shapes=[
            pltpu.VMEM((blocks, rows, unit), F32),
            pltpu.VMEM((blocks, rank, unit), F32),
            pltpu.VMEM((blocks, rows, unit), BF16),
            pltpu.VMEM((blocks, rows, unit), BF16),
            pltpu.SemaphoreType.DMA((blocks,)),
            pltpu.SemaphoreType.DMA((blocks,)),
        ],
        compiler_params=PARAMS,
        cost_estimate=pl.CostEstimate(
            flops=6 * rows * cols * rank, bytes_accessed=4 * rows * cols, transcendentals=0
        ),
        name="tall_partial",
    )(in_hbm(probes), in_hbm(sketch_t))


def multiply_blocks(both_ref, which_ref, x_hbm, x_buf, sems, plan, outs):
    rank = outs[0].shape[0]
    unit = x_buf.shape[2]
    copies = [
        pltpu.make_async_copy(
            x_hbm.at[:, pl.ds(pl.multiple_of(which_ref[k] * unit, unit), unit)],
            x_buf.at[k],
            sems.at[k],
        )
        for k in range(len(plan))
    ]

    def use(k):
        out, offset = plan[k]
        for cols in tiles(unit):
            total = None
            for rows in tiles(x_buf.shape[1]):
                x_head, x_rest = split(x_buf[k, rows, cols])
                both = dot(both_ref[:, rows], x_head, PLAIN)
                part = both[:rank] + (both[rank:] + dot(both_ref[:rank, rows], x_rest, PLAIN))
                total = part if total is None else total + part
            outs[out][:, offset + cols.start : offset + cols.stop] = total

    return copies, use


def first_kernel(plan, grams, which_ref, one_ref, two_ref, x_hbm, both_ref, gram_ref, *refs):
    outs, (x_buf, sems) = refs[:-2], refs[-2:]
    copies, use = multiply_blocks(both_ref, which_ref, x_hbm, x_buf, sems, plan, outs)

    def use_first(k):
        if k == 0:
            tall = one_ref[...] + two_ref[...]
            head, rest = split(tall)
            both_ref[...] = jnp.concatenate([head, rest], axis=0)
        use(k)

    stream(copies, use_first)
    tall = one_ref[...] + two_ref[...]
    r = tall.shape[0]
    head, rest = split(tall)
    tail = (tall - head.astype(F32) - rest.astype(F32)).astype(BF16)
    three = jnp.concatenate([head, rest, tail], axis=0)
    g = dot(three, three, LAST)
    cross = g[:r, r : 2 * r] + g[r : 2 * r, :r]
    small = g[:r, 2 * r :] + g[2 * r :, :r] + g[r : 2 * r, r : 2 * r]
    gram = g[:r, :r] + (cross + small)
    gram_ref[...] = jnp.concatenate([gram, jnp.zeros((r, LANES - r), F32)], axis=1)
    for out, offset in grams:
        outs[out][:, offset : offset + LANES] = gram_ref[...]


def rest_kernel(plan, grams, which_ref, both_ref, gram_ref, x_hbm, after_ref, *refs):
    outs, (x_buf, sems) = refs[:-2], refs[-2:]
    copies, use = multiply_blocks(both_ref, which_ref, x_hbm, x_buf, sems, plan, outs)
    stream(copies, use)
    for out, offset in grams:
        outs[out][:, offset : offset + LANES] = gram_ref[...]


def layout(outputs, sub):
    unit = min(UNIT, sub)
    plan, grams, widths, which = [], [], [], []
    for out, (blocks, with_gram) in enumerate(outputs):
        extra = LANES if with_gram else 0
        for j, block in enumerate(blocks):
            for part in range(sub // unit):
                plan.append((out, j * sub + part * unit + (extra if j else 0)))
                which.append(block * (sub // unit) + part)
        if with_gram:
            grams.append((out, sub))
        widths.append(len(blocks) * sub + extra)
    return unit, plan, grams, widths, jnp.stack(which)


def products(kernel, inputs, in_specs, made, probes, outputs, sub, name):
    rows = probes.shape[0]
    rank = inputs[1].shape[0]
    unit, plan, grams, widths, which = layout(outputs, sub)
    shapes = [*made, *[jax.ShapeDtypeStruct((rank, width), F32) for width in widths]]
    return pl.pallas_call(
        functools.partial(kernel, plan, grams),
        in_specs=[TABLE, *in_specs],
        out_specs=[WHOLE] * len(shapes),
        out_shape=shapes,
        scratch_shapes=[
            pltpu.VMEM((len(plan), rows, unit), F32),
            pltpu.SemaphoreType.DMA((len(plan),)),
        ],
        compiler_params=PARAMS,
        cost_estimate=pl.CostEstimate(
            flops=6 * rows * rank * unit * len(plan),
            bytes_accessed=4 * rows * unit * len(plan),
            transcendentals=0,
        ),
        name=name,
    )(which, *inputs)


def first_products(one, two, probes, outputs, sub):
    rank, rows = one.shape
    made = [
        jax.ShapeDtypeStruct((2 * rank, rows), BF16),
        jax.ShapeDtypeStruct((rank, LANES), F32),
    ]
    both, gram, *outs = products(
        first_kernel,
        [one, two, in_hbm(probes)],
        [WHOLE, WHOLE, HBM],
        made,
        probes,
        outputs,
        sub,
        "first_products",
    )
    return both, gram, outs


def rest_products(both, gram, probes, outputs, sub, after):
    return products(
        rest_kernel,
        [both, gram, in_hbm(probes), after],
        [WHOLE, WHOLE, HBM, ANYWHERE],
        [],
        probes,
        outputs,
        sub,
        "rest_products",
    )


def inverse_kernel(gram_ref, out_ref):
    rank = out_ref.shape[0]
    rows = lax.broadcasted_iota(jnp.int32, (rank, LANES), 0)
    cols = lax.broadcasted_iota(jnp.int32, (rank, LANES), 1)
    work = jnp.where(cols < rank, gram_ref[...], (cols == rows + rank).astype(F32))
    scale = jnp.ones((rank, LANES), F32)
    for start in range(0, rank, PANEL):
        panel = [
            jnp.broadcast_to(work[:, k : k + 1], (rank, LANES))
            for k in range(start, start + PANEL)
        ]
        for j in range(PANEL):
            k = start + j
            over = 1.0 / panel[j][k : k + 1, :]
            scale = jnp.where(rows == k, over, scale)
            factor = jnp.where(rows > k, panel[j] * over, 0.0)
            work = work - factor * work[k : k + 1, :]
            for later in range(j + 1, PANEL):
                panel[later] = panel[later] - factor * panel[later][k : k + 1, :]
    out_ref[...] = (work * jnp.sqrt(scale))[:, rank : 2 * rank]


def inverse_factor(chunk, start):
    rank = chunk.shape[0]
    return pl.pallas_call(
        inverse_kernel,
        grid=(1,),
        in_specs=[pl.BlockSpec((rank, LANES), lambda i: (0, start // LANES))],
        out_specs=pl.BlockSpec((rank, rank), lambda i: (0, 0)),
        out_shape=jax.ShapeDtypeStruct((rank, rank), F32),
        compiler_params=PARAMS,
        cost_estimate=pl.CostEstimate(
            flops=20_000_000, bytes_accessed=8 * rank * LANES, transcendentals=rank
        ),
        name="inverse_factor",
    )(chunk)


def finish_kernel(plan, where_ref, inverse_ref, *refs):
    out_hbm, buf, sems = refs[-3:]
    _, rank, width = buf.shape
    head, rest = split(inverse_ref[...])
    both = jnp.concatenate([head, rest], axis=0)
    copies = []
    for k, (source, offset) in enumerate(plan):
        p_head, p_rest = split(refs[source][:, offset : offset + width])
        first = dot(both, p_head, PLAIN)
        buf[k] = first[:rank] + (first[rank:] + dot(head, p_rest, PLAIN))
        where = pl.ds(pl.multiple_of(where_ref[k] * width, width), width)
        copies.append(pltpu.make_async_copy(buf.at[k], out_hbm.at[:, where], sems.at[k]))
        copies[k].start()
    for copy in copies:
        copy.wait()


def finish(inverse, sources, pieces, width, total, before=None):
    rank = inverse.shape[0]
    count = len(pieces)
    in_specs = [TABLE, WHOLE, *[WHOLE] * len(sources)]
    args = [jnp.stack([piece[0] for piece in pieces]), inverse, *sources]
    aliases = {}
    if before is not None:
        in_specs.append(HBM)
        args.append(before)
        aliases = {len(args) - 1: 0}
    return pl.pallas_call(
        functools.partial(finish_kernel, [piece[1:] for piece in pieces]),
        in_specs=in_specs,
        out_specs=HBM,
        out_shape=jax.ShapeDtypeStruct((rank, total), F32),
        scratch_shapes=[
            pltpu.VMEM((count, rank, width), F32),
            pltpu.SemaphoreType.DMA((count,)),
        ],
        input_output_aliases=aliases,
        compiler_params=PARAMS,
        cost_estimate=pl.CostEstimate(
            flops=6 * rank * rank * width * count,
            bytes_accessed=8 * rank * width * count,
            transcendentals=0,
        ),
        name="finish",
    )(*args)


def body(n_pos, n_pix, probes, sketch):
    def swap(value, axis, size, bit):
        return lax.ppermute(value, axis, [(i, i ^ bit) for i in range(size)])

    def over(value, bit):
        if bit > 2:
            return swap(value, "pos", n_pos, bit)
        pairs = [
            (i * n_pix + j, (i ^ (bit if j % 2 else 3 - bit)) * n_pix + j)
            for i in range(n_pos)
            for j in range(n_pix)
        ]
        return lax.ppermute(value, ("pos", "pix"), pairs)

    me = lax.axis_index("pos").astype(jnp.int32)
    odd = lax.axis_index("pix").astype(jnp.int32) & 1
    near, far = (me >> (1 - odd)) & 1, (me >> odd) & 1
    cols = probes.shape[1]
    width = cols // (8 * CHUNKS)

    tall = tall_partial(probes, sketch.T)
    bit = 1
    while 2 * bit < n_pix:
        tall = tall + swap(tall, "pix", n_pix, bit)
        bit *= 2
    other = swap(tall, "pix", n_pix, bit)

    def block_a(c, p, q):
        return 8 * c + 2 * (near ^ p) + (far ^ q)

    def block_b(c, p, q):
        return 8 * c + 4 + 2 * (far ^ p) + (near ^ q)

    def outputs(c, p):
        return [
            ([block_a(c, p, 1), block_a(c, p, 0)], c == 0),
            ([block_b(c, p, 1), block_b(c, p, 0)], False),
        ]

    both, gram, away = first_products(tall, other, probes, outputs(0, 1), width)

    inverse, out, after = None, None, away[0]
    for c in range(CHUNKS):
        g = LANES if c == 0 else 0
        last = c == CHUNKS - 1
        made = rest_products(
            both, gram, probes, outputs(c, 0) + ([] if last else outputs(c + 1, 1)), width, after
        )
        away_a, away_b = away
        (own_a, own_b), away = made[:2], made[2:]
        got_a = over(away_a, 1)
        sum_a = own_a + got_a
        sum_b = own_b + over(away_b, 2)
        after = got_a
        send_a, send_b = sum_a[:, : width + g], sum_b[:, :width]
        if c > 0:
            send_a, send_b, whole = lax.optimization_barrier((send_a, send_b, whole))
        got_a = over(send_a, 2)
        got_b = over(send_b, 1)
        whole = jnp.concatenate(
            [
                sum_a[:, width + g :] + got_a[:, :width],
                sum_a[:, width : width + g] + got_a[:, width:],
                sum_b[:, width:] + got_b,
            ],
            axis=1,
        )
        total = whole
        bit = 4
        while bit < n_pos:
            total = total + over(total, bit)
            bit *= 2
        if c == 0:
            inverse = inverse_factor(total, width)
        mine_a, mine_b = total[:, :width], total[:, width + g :]
        if c > 0:
            mine_a, mine_b, inverse = lax.optimization_barrier((mine_a, mine_b, inverse))
        next_a = over(mine_a, 2)
        next_b = over(mine_b, 1)
        last_a = over(jnp.concatenate([mine_a, next_a], axis=1), 1)
        last_b = over(jnp.concatenate([mine_b, next_b], axis=1), 2)
        sources = [total, next_a, next_b]
        pieces = [
            (block_a(c, 0, 0), 0, 0),
            (block_b(c, 0, 0), 0, width + g),
            (block_a(c, 0, 1), 1, 0),
            (block_b(c, 0, 1), 2, 0),
        ]
        if last:
            out = finish(inverse, sources, pieces, width, cols, out)
            sources, pieces = [], []
        k = len(sources)
        sources += [last_a, last_b]
        pieces += [
            (block_a(c, 1, 0), k, 0),
            (block_a(c, 1, 1), k, width),
            (block_b(c, 1, 0), k + 1, 0),
            (block_b(c, 1, 1), k + 1, width),
        ]
        out = finish(inverse, sources, pieces, width, cols, out)
    return out


def solution(mesh):
    in_specs = (P("pos", "pix"), P("pix", None))
    out_specs = P(None, "pix")
    run = functools.partial(body, mesh.shape["pos"], mesh.shape["pix"])
    return jax.shard_map(run, mesh=mesh, in_specs=in_specs, out_specs=out_specs, check_vma=False)
```

```python
import functools

import jax
import jax.numpy as jnp
from jax import lax
from jax.experimental import pallas as pl
from jax.experimental.pallas import tpu as pltpu
from jax.sharding import PartitionSpec as P

F32 = jnp.float32
BF16 = jnp.bfloat16
VMEM_LIMIT = 40 * 1024 * 1024
LANES = 128
CHUNKS = 2
AHEAD = 8
UNIT = 512
TILE = 256
PANEL = 4
LAST = (((1,), (1,)), ((), ()))
PLAIN = (((1,), (0,)), ((), ()))
ANYWHERE = pl.BlockSpec(memory_space=pl.ANY)
HBM = pl.BlockSpec(memory_space=pltpu.MemorySpace.HBM)
WHOLE = pl.BlockSpec(memory_space=pltpu.VMEM)
TABLE = pl.BlockSpec(memory_space=pltpu.SMEM)
PARAMS = pltpu.CompilerParams(vmem_limit_bytes=VMEM_LIMIT)


def split(x):
    head = x.astype(BF16)
    return head, (x - head.astype(F32)).astype(BF16)


def dot(a, b, dims):
    return lax.dot_general(a, b, dims, preferred_element_type=F32)


def tiles(size):
    step = min(TILE, size)
    return [slice(start, start + step) for start in range(0, size, step)]


def in_hbm(x):
    return pltpu.with_memory_space_constraint(x, pltpu.MemorySpace.HBM)


def stream(copies, use):
    for copy in copies[:AHEAD]:
        copy.start()
    for k, copy in enumerate(copies):
        copy.wait()
        if k + AHEAD < len(copies):
            copies[k + AHEAD].start()
        use(k)


def tall_kernel(x_hbm, s_hbm, out_ref, x_buf, s_buf, head_buf, rest_buf, x_sems, s_sems):
    blocks, _, unit = x_buf.shape
    rank = s_hbm.shape[0]

    def copies(k):
        where = pl.ds(k * unit, unit)
        return (
            pltpu.make_async_copy(s_hbm.at[:, where], s_buf.at[k], s_sems.at[k]),
            pltpu.make_async_copy(x_hbm.at[:, where], x_buf.at[k], x_sems.at[k]),
        )

    for k in range(blocks):
        for copy in copies(k):
            copy.start()
    for k in range(blocks):
        for copy in copies(k):
            copy.wait()
        s_head, s_rest = split(s_buf[k])
        s_both = jnp.concatenate([s_head, s_rest], axis=0)
        x_head, x_rest = split(x_buf[k])
        head_buf[k] = x_head
        rest_buf[k] = x_rest
        both = dot(s_both, x_head, LAST)
        part = both[:rank] + (both[rank:] + dot(s_head, x_rest, LAST))
        if k == 0:
            out_ref[...] = part
        else:
            out_ref[...] += part


def tall_partial(probes, sketch_t):
    rows, cols = probes.shape
    rank = sketch_t.shape[0]
    unit = min(2 * UNIT, cols)
    blocks = cols // unit
    return pl.pallas_call(
        tall_kernel,
        in_specs=[HBM, HBM],
        out_specs=WHOLE,
        out_shape=jax.ShapeDtypeStruct((rank, rows), F32),
        scratch_shapes=[
            pltpu.VMEM((blocks, rows, unit), F32),
            pltpu.VMEM((blocks, rank, unit), F32),
            pltpu.VMEM((blocks, rows, unit), BF16),
            pltpu.VMEM((blocks, rows, unit), BF16),
            pltpu.SemaphoreType.DMA((blocks,)),
            pltpu.SemaphoreType.DMA((blocks,)),
        ],
        compiler_params=PARAMS,
        cost_estimate=pl.CostEstimate(
            flops=6 * rows * cols * rank, bytes_accessed=4 * rows * cols, transcendentals=0
        ),
        name="tall_partial",
    )(in_hbm(probes), in_hbm(sketch_t))


def multiply_blocks(both_ref, which_ref, x_hbm, x_buf, sems, plan, outs):
    rank = outs[0].shape[0]
    unit = x_buf.shape[2]
    copies = [
        pltpu.make_async_copy(
            x_hbm.at[:, pl.ds(pl.multiple_of(which_ref[k] * unit, unit), unit)],
            x_buf.at[k],
            sems.at[k],
        )
        for k in range(len(plan))
    ]

    def use(k):
        out, offset = plan[k]
        for cols in tiles(unit):
            total = None
            for rows in tiles(x_buf.shape[1]):
                x_head, x_rest = split(x_buf[k, rows, cols])
                both = dot(both_ref[:, rows], x_head, PLAIN)
                part = both[:rank] + (both[rank:] + dot(both_ref[:rank, rows], x_rest, PLAIN))
                total = part if total is None else total + part
            outs[out][:, offset + cols.start : offset + cols.stop] = total

    return copies, use


def first_kernel(plan, grams, which_ref, one_ref, two_ref, x_hbm, both_ref, gram_ref, *refs):
    outs, (x_buf, sems) = refs[:-2], refs[-2:]
    copies, use = multiply_blocks(both_ref, which_ref, x_hbm, x_buf, sems, plan, outs)

    def use_first(k):
        if k == 0:
            tall = one_ref[...] + two_ref[...]
            head, rest = split(tall)
            both_ref[...] = jnp.concatenate([head, rest], axis=0)
        use(k)

    stream(copies, use_first)
    tall = one_ref[...] + two_ref[...]
    r = tall.shape[0]
    head, rest = split(tall)
    tail = (tall - head.astype(F32) - rest.astype(F32)).astype(BF16)
    three = jnp.concatenate([head, rest, tail], axis=0)
    g = dot(three, three, LAST)
    cross = g[:r, r : 2 * r] + g[r : 2 * r, :r]
    small = g[:r, 2 * r :] + g[2 * r :, :r] + g[r : 2 * r, r : 2 * r]
    gram = g[:r, :r] + (cross + small)
    gram_ref[...] = jnp.concatenate([gram, jnp.zeros((r, LANES - r), F32)], axis=1)
    for out, offset in grams:
        outs[out][:, offset : offset + LANES] = gram_ref[...]


def rest_kernel(plan, grams, which_ref, both_ref, gram_ref, x_hbm, after_ref, *refs):
    outs, (x_buf, sems) = refs[:-2], refs[-2:]
    copies, use = multiply_blocks(both_ref, which_ref, x_hbm, x_buf, sems, plan, outs)
    stream(copies, use)
    for out, offset in grams:
        outs[out][:, offset : offset + LANES] = gram_ref[...]


def layout(outputs, sub):
    unit = min(UNIT, sub)
    plan, grams, widths, which = [], [], [], []
    for out, (blocks, with_gram) in enumerate(outputs):
        extra = LANES if with_gram else 0
        for j, block in enumerate(blocks):
            for part in range(sub // unit):
                plan.append((out, j * sub + part * unit + (extra if j else 0)))
                which.append(block * (sub // unit) + part)
        if with_gram:
            grams.append((out, sub))
        widths.append(len(blocks) * sub + extra)
    return unit, plan, grams, widths, which


def products(kernel, inputs, in_specs, made, probes, outputs, sub, name):
    rows = probes.shape[0]
    rank = inputs[1].shape[0]
    unit, plan, grams, widths, which = layout(outputs, sub)
    shapes = [*made, *[jax.ShapeDtypeStruct((rank, width), F32) for width in widths]]
    return pl.pallas_call(
        functools.partial(kernel, plan, grams),
        in_specs=[TABLE, *in_specs],
        out_specs=[WHOLE] * len(shapes),
        out_shape=shapes,
        scratch_shapes=[
            pltpu.VMEM((len(plan), rows, unit), F32),
            pltpu.SemaphoreType.DMA((len(plan),)),
        ],
        compiler_params=PARAMS,
        cost_estimate=pl.CostEstimate(
            flops=6 * rows * rank * unit * len(plan),
            bytes_accessed=4 * rows * unit * len(plan),
            transcendentals=0,
        ),
        name=name,
    )(jnp.stack(which), *inputs)


def first_products(one, two, probes, outputs, sub):
    rank, rows = one.shape
    made = [
        jax.ShapeDtypeStruct((2 * rank, rows), BF16),
        jax.ShapeDtypeStruct((rank, LANES), F32),
    ]
    both, gram, *outs = products(
        first_kernel,
        [one, two, in_hbm(probes)],
        [WHOLE, WHOLE, HBM],
        made,
        probes,
        outputs,
        sub,
        "first_products",
    )
    return both, gram, outs


def rest_products(both, gram, probes, outputs, sub, after):
    return products(
        rest_kernel,
        [both, gram, in_hbm(probes), after],
        [WHOLE, WHOLE, HBM, ANYWHERE],
        [],
        probes,
        outputs,
        sub,
        "rest_products",
    )


def inverse_kernel(gram_ref, out_ref):
    rank = out_ref.shape[0]
    rows = lax.broadcasted_iota(jnp.int32, (rank, LANES), 0)
    cols = lax.broadcasted_iota(jnp.int32, (rank, LANES), 1)
    work = jnp.where(cols < rank, gram_ref[...], (cols == rows + rank).astype(F32))
    scale = jnp.ones((rank, LANES), F32)
    for start in range(0, rank, PANEL):
        panel = [
            jnp.broadcast_to(work[:, k : k + 1], (rank, LANES))
            for k in range(start, start + PANEL)
        ]
        for j in range(PANEL):
            k = start + j
            over = 1.0 / panel[j][k : k + 1, :]
            scale = jnp.where(rows == k, over, scale)
            factor = jnp.where(rows > k, panel[j] * over, 0.0)
            work = work - factor * work[k : k + 1, :]
            for later in range(j + 1, PANEL):
                panel[later] = panel[later] - factor * panel[later][k : k + 1, :]
    out_ref[...] = (work * jnp.sqrt(scale))[:, rank : 2 * rank]


def inverse_factor(chunk, start):
    rank = chunk.shape[0]
    return pl.pallas_call(
        inverse_kernel,
        grid=(1,),
        in_specs=[pl.BlockSpec((rank, LANES), lambda i: (0, start // LANES))],
        out_specs=pl.BlockSpec((rank, rank), lambda i: (0, 0)),
        out_shape=jax.ShapeDtypeStruct((rank, rank), F32),
        compiler_params=PARAMS,
        cost_estimate=pl.CostEstimate(
            flops=20_000_000, bytes_accessed=8 * rank * LANES, transcendentals=rank
        ),
        name="inverse_factor",
    )(chunk)


def finish_kernel(plan, where_ref, inverse_ref, *refs):
    out_hbm, buf, sems = refs[-3:]
    _, rank, width = buf.shape
    head, rest = split(inverse_ref[...])
    both = jnp.concatenate([head, rest], axis=0)
    copies = []
    for k, (source, offset) in enumerate(plan):
        p_head, p_rest = split(refs[source][:, offset : offset + width])
        first = dot(both, p_head, PLAIN)
        buf[k] = first[:rank] + (first[rank:] + dot(head, p_rest, PLAIN))
        where = pl.ds(pl.multiple_of(where_ref[k] * width, width), width)
        copies.append(pltpu.make_async_copy(buf.at[k], out_hbm.at[:, where], sems.at[k]))
        copies[k].start()
    for copy in copies:
        copy.wait()


def finish(inverse, sources, pieces, width, total, before=None):
    rank = inverse.shape[0]
    count = len(pieces)
    in_specs = [TABLE, WHOLE, *[WHOLE] * len(sources)]
    args = [jnp.stack([piece[0] for piece in pieces]), inverse, *sources]
    aliases = {}
    if before is not None:
        in_specs.append(HBM)
        args.append(before)
        aliases = {len(args) - 1: 0}
    return pl.pallas_call(
        functools.partial(finish_kernel, [piece[1:] for piece in pieces]),
        in_specs=in_specs,
        out_specs=HBM,
        out_shape=jax.ShapeDtypeStruct((rank, total), F32),
        scratch_shapes=[
            pltpu.VMEM((count, rank, width), F32),
            pltpu.SemaphoreType.DMA((count,)),
        ],
        input_output_aliases=aliases,
        compiler_params=PARAMS,
        cost_estimate=pl.CostEstimate(
            flops=6 * rank * rank * width * count,
            bytes_accessed=8 * rank * width * count,
            transcendentals=0,
        ),
        name="finish",
    )(*args)


def body(n_pos, n_pix, probes, sketch):
    def swap(value, axis, size, bit):
        return lax.ppermute(value, axis, [(i, i ^ bit) for i in range(size)])

    def over(value, bit):
        if bit > 2:
            return swap(value, "pos", n_pos, bit)
        pairs = [
            (i * n_pix + j, (i ^ (bit if j % 2 else 3 - bit)) * n_pix + j)
            for i in range(n_pos)
            for j in range(n_pix)
        ]
        return lax.ppermute(value, ("pos", "pix"), pairs)

    me = lax.axis_index("pos").astype(jnp.int32)
    odd = lax.axis_index("pix").astype(jnp.int32) & 1
    near, far = (me >> (1 - odd)) & 1, (me >> odd) & 1
    cols = probes.shape[1]
    width = cols // (8 * CHUNKS)

    tall = tall_partial(probes, sketch.T)
    bit = 1
    while 2 * bit < n_pix:
        tall = tall + swap(tall, "pix", n_pix, bit)
        bit *= 2
    other = swap(tall, "pix", n_pix, bit)

    def block_a(c, p, q):
        return 8 * c + 2 * (near ^ p) + (far ^ q)

    def block_b(c, p, q):
        return 8 * c + 4 + 2 * (far ^ p) + (near ^ q)

    def outputs(c, p):
        return [
            ([block_a(c, p, 1), block_a(c, p, 0)], c == 0),
            ([block_b(c, p, 1), block_b(c, p, 0)], False),
        ]

    both, gram, away = first_products(tall, other, probes, outputs(0, 1), width)

    plan = [(c, p) for c in range(CHUNKS) for p in (1, 0) if (c, p) != (0, 1)]
    rest = rest_products(
        both, gram, probes, [out for c, p in plan for out in outputs(c, p)], width, away[0]
    )
    made = {(0, 1): away}
    made.update({key: rest[2 * k : 2 * k + 2] for k, key in enumerate(plan)})

    inverse = None
    sources, pieces = [], []
    for c in range(CHUNKS):
        g = LANES if c == 0 else 0
        away_a, away_b = made[c, 1]
        own_a, own_b = made[c, 0]
        if c > 0:
            own_a, own_b, whole = lax.optimization_barrier((own_a, own_b, whole))
        got_a = over(away_a, 1)
        sum_a = own_a + got_a
        sum_b = own_b + over(away_b, 2)
        send_a, send_b = sum_a[:, : width + g], sum_b[:, :width]
        got_a = over(send_a, 2)
        got_b = over(send_b, 1)
        whole = jnp.concatenate(
            [
                sum_a[:, width + g :] + got_a[:, :width],
                sum_a[:, width : width + g] + got_a[:, width:],
                sum_b[:, width:] + got_b,
            ],
            axis=1,
        )
        total = whole
        bit = 4
        while bit < n_pos:
            total = total + over(total, bit)
            bit *= 2
        if c == 0:
            inverse = inverse_factor(total, width)
        mine_a, mine_b = total[:, :width], total[:, width + g :]
        if c > 0:
            mine_a, mine_b, inverse = lax.optimization_barrier((mine_a, mine_b, inverse))
        next_a = over(mine_a, 2)
        next_b = over(mine_b, 1)
        last_a = over(jnp.concatenate([mine_a, next_a], axis=1), 1)
        last_b = over(jnp.concatenate([mine_b, next_b], axis=1), 2)
        k = len(sources)
        sources += [total, next_a, next_b, last_a, last_b]
        pieces += [
            (block_a(c, 0, 0), k, 0),
            (block_b(c, 0, 0), k, width + g),
            (block_a(c, 0, 1), k + 1, 0),
            (block_b(c, 0, 1), k + 2, 0),
            (block_a(c, 1, 0), k + 3, 0),
            (block_a(c, 1, 1), k + 3, width),
            (block_b(c, 1, 0), k + 4, 0),
            (block_b(c, 1, 1), k + 4, width),
        ]
    out = finish(inverse, sources[:-2], pieces[:-4], width, cols)
    pieces = [(where, source - k - 3, start) for where, source, start in pieces[-4:]]
    return finish(inverse, sources[-2:], pieces, width, cols, out)


def solution(mesh):
    in_specs = (P("pos", "pix"), P("pix", None))
    out_specs = P(None, "pix")
    run = functools.partial(body, mesh.shape["pos"], mesh.shape["pix"])
    return jax.shard_map(run, mesh=mesh, in_specs=in_specs, out_specs=out_specs, check_vma=False)
```

```python
import functools

import jax
import jax.numpy as jnp
from jax import lax
from jax.experimental import pallas as pl
from jax.experimental.pallas import tpu as pltpu
from jax.sharding import PartitionSpec as P

F32 = jnp.float32
BF16 = jnp.bfloat16
VMEM_LIMIT = 40 * 1024 * 1024
LANES = 128
CHUNKS = 2
AHEAD = 8
UNIT = 512
TILE = 256
PANEL = 4
LAST = (((1,), (1,)), ((), ()))
PLAIN = (((1,), (0,)), ((), ()))
ANYWHERE = pl.BlockSpec(memory_space=pl.ANY)
HBM = pl.BlockSpec(memory_space=pltpu.MemorySpace.HBM)
WHOLE = pl.BlockSpec(memory_space=pltpu.VMEM)
TABLE = pl.BlockSpec(memory_space=pltpu.SMEM)
PARAMS = pltpu.CompilerParams(vmem_limit_bytes=VMEM_LIMIT)


def split(x):
    head = x.astype(BF16)
    return head, (x - head.astype(F32)).astype(BF16)


def dot(a, b, dims):
    return lax.dot_general(a, b, dims, preferred_element_type=F32)


def tiles(size):
    step = min(TILE, size)
    return [slice(start, start + step) for start in range(0, size, step)]


def in_hbm(x):
    return pltpu.with_memory_space_constraint(x, pltpu.MemorySpace.HBM)


def stream(copies, use):
    for copy in copies[:AHEAD]:
        copy.start()
    for k, copy in enumerate(copies):
        copy.wait()
        if k + AHEAD < len(copies):
            copies[k + AHEAD].start()
        use(k)


def tall_kernel(x_hbm, s_hbm, out_ref, x_buf, s_buf, head_buf, rest_buf, x_sems, s_sems):
    blocks, _, unit = x_buf.shape
    rank = s_hbm.shape[0]

    def copies(k):
        where = pl.ds(k * unit, unit)
        return (
            pltpu.make_async_copy(s_hbm.at[:, where], s_buf.at[k], s_sems.at[k]),
            pltpu.make_async_copy(x_hbm.at[:, where], x_buf.at[k], x_sems.at[k]),
        )

    for k in range(blocks):
        for copy in copies(k):
            copy.start()
    for k in range(blocks):
        for copy in copies(k):
            copy.wait()
        s_head, s_rest = split(s_buf[k])
        s_both = jnp.concatenate([s_head, s_rest], axis=0)
        x_head, x_rest = split(x_buf[k])
        head_buf[k] = x_head
        rest_buf[k] = x_rest
        both = dot(s_both, x_head, LAST)
        part = both[:rank] + (both[rank:] + dot(s_head, x_rest, LAST))
        if k == 0:
            out_ref[...] = part
        else:
            out_ref[...] += part


def tall_partial(probes, sketch_t):
    rows, cols = probes.shape
    rank = sketch_t.shape[0]
    unit = min(2 * UNIT, cols)
    blocks = cols // unit
    return pl.pallas_call(
        tall_kernel,
        in_specs=[HBM, HBM],
        out_specs=WHOLE,
        out_shape=jax.ShapeDtypeStruct((rank, rows), F32),
        scratch_shapes=[
            pltpu.VMEM((blocks, rows, unit), F32),
            pltpu.VMEM((blocks, rank, unit), F32),
            pltpu.VMEM((blocks, rows, unit), BF16),
            pltpu.VMEM((blocks, rows, unit), BF16),
            pltpu.SemaphoreType.DMA((blocks,)),
            pltpu.SemaphoreType.DMA((blocks,)),
        ],
        compiler_params=PARAMS,
        cost_estimate=pl.CostEstimate(
            flops=6 * rows * cols * rank, bytes_accessed=4 * rows * cols, transcendentals=0
        ),
        name="tall_partial",
    )(in_hbm(probes), in_hbm(sketch_t))


def multiply_blocks(both_ref, which_ref, x_hbm, x_buf, sems, plan, outs):
    rank = outs[0].shape[0]
    unit = x_buf.shape[2]
    copies = [
        pltpu.make_async_copy(
            x_hbm.at[:, pl.ds(pl.multiple_of(which_ref[k] * unit, unit), unit)],
            x_buf.at[k],
            sems.at[k],
        )
        for k in range(len(plan))
    ]

    def use(k):
        out, offset = plan[k]
        for cols in tiles(unit):
            total = None
            for rows in tiles(x_buf.shape[1]):
                x_head, x_rest = split(x_buf[k, rows, cols])
                both = dot(both_ref[:, rows], x_head, PLAIN)
                part = both[:rank] + (both[rank:] + dot(both_ref[:rank, rows], x_rest, PLAIN))
                total = part if total is None else total + part
            outs[out][:, offset + cols.start : offset + cols.stop] = total

    return copies, use


def first_kernel(plan, grams, which_ref, one_ref, two_ref, x_hbm, both_ref, gram_ref, *refs):
    outs, (x_buf, sems) = refs[:-2], refs[-2:]
    copies, use = multiply_blocks(both_ref, which_ref, x_hbm, x_buf, sems, plan, outs)

    def use_first(k):
        if k == 0:
            tall = one_ref[...] + two_ref[...]
            head, rest = split(tall)
            both_ref[...] = jnp.concatenate([head, rest], axis=0)
        use(k)

    stream(copies, use_first)
    tall = one_ref[...] + two_ref[...]
    r = tall.shape[0]
    head, rest = split(tall)
    tail = (tall - head.astype(F32) - rest.astype(F32)).astype(BF16)
    three = jnp.concatenate([head, rest, tail], axis=0)
    g = dot(three, three, LAST)
    cross = g[:r, r : 2 * r] + g[r : 2 * r, :r]
    small = g[:r, 2 * r :] + g[2 * r :, :r] + g[r : 2 * r, r : 2 * r]
    gram = g[:r, :r] + (cross + small)
    gram_ref[...] = jnp.concatenate([gram, jnp.zeros((r, LANES - r), F32)], axis=1)
    for out, offset in grams:
        outs[out][:, offset : offset + LANES] = gram_ref[...]


def rest_kernel(plan, grams, which_ref, both_ref, gram_ref, x_hbm, after_ref, *refs):
    outs, (x_buf, sems) = refs[:-2], refs[-2:]
    copies, use = multiply_blocks(both_ref, which_ref, x_hbm, x_buf, sems, plan, outs)
    stream(copies, use)
    for out, offset in grams:
        outs[out][:, offset : offset + LANES] = gram_ref[...]


def layout(outputs, sub):
    unit = min(UNIT, sub)
    plan, grams, widths, which = [], [], [], []
    for out, (blocks, with_gram) in enumerate(outputs):
        extra = LANES if with_gram else 0
        for j, block in enumerate(blocks):
            for part in range(sub // unit):
                plan.append((out, j * sub + part * unit + (extra if j else 0)))
                which.append(block * (sub // unit) + part)
        if with_gram:
            grams.append((out, sub))
        widths.append(len(blocks) * sub + extra)
    return unit, plan, grams, widths, jnp.stack(which)


def products(kernel, inputs, in_specs, made, probes, outputs, sub, name):
    rows = probes.shape[0]
    rank = inputs[1].shape[0]
    unit, plan, grams, widths, which = layout(outputs, sub)
    shapes = [*made, *[jax.ShapeDtypeStruct((rank, width), F32) for width in widths]]
    return pl.pallas_call(
        functools.partial(kernel, plan, grams),
        in_specs=[TABLE, *in_specs],
        out_specs=[WHOLE] * len(shapes),
        out_shape=shapes,
        scratch_shapes=[
            pltpu.VMEM((len(plan), rows, unit), F32),
            pltpu.SemaphoreType.DMA((len(plan),)),
        ],
        compiler_params=PARAMS,
        cost_estimate=pl.CostEstimate(
            flops=6 * rows * rank * unit * len(plan),
            bytes_accessed=4 * rows * unit * len(plan),
            transcendentals=0,
        ),
        name=name,
    )(which, *inputs)


def first_products(one, two, probes, outputs, sub):
    rank, rows = one.shape
    made = [
        jax.ShapeDtypeStruct((2 * rank, rows), BF16),
        jax.ShapeDtypeStruct((rank, LANES), F32),
    ]
    both, gram, *outs = products(
        first_kernel,
        [one, two, in_hbm(probes)],
        [WHOLE, WHOLE, HBM],
        made,
        probes,
        outputs,
        sub,
        "first_products",
    )
    return both, gram, outs


def rest_products(both, gram, probes, outputs, sub, after):
    return products(
        rest_kernel,
        [both, gram, in_hbm(probes), after],
        [WHOLE, WHOLE, HBM, ANYWHERE],
        [],
        probes,
        outputs,
        sub,
        "rest_products",
    )


def inverse_kernel(gram_ref, out_ref):
    rank = out_ref.shape[0]
    rows = lax.broadcasted_iota(jnp.int32, (rank, LANES), 0)
    cols = lax.broadcasted_iota(jnp.int32, (rank, LANES), 1)
    work = jnp.where(cols < rank, gram_ref[...], (cols == rows + rank).astype(F32))
    scale = jnp.ones((rank, LANES), F32)
    for start in range(0, rank, PANEL):
        panel = [
            jnp.broadcast_to(work[:, k : k + 1], (rank, LANES))
            for k in range(start, start + PANEL)
        ]
        for j in range(PANEL):
            k = start + j
            over = 1.0 / panel[j][k : k + 1, :]
            scale = jnp.where(rows == k, over, scale)
            factor = jnp.where(rows > k, panel[j] * over, 0.0)
            work = work - factor * work[k : k + 1, :]
            for later in range(j + 1, PANEL):
                panel[later] = panel[later] - factor * panel[later][k : k + 1, :]
    out_ref[...] = (work * jnp.sqrt(scale))[:, rank : 2 * rank]


def inverse_factor(chunk, start):
    rank = chunk.shape[0]
    return pl.pallas_call(
        inverse_kernel,
        grid=(1,),
        in_specs=[pl.BlockSpec((rank, LANES), lambda i: (0, start // LANES))],
        out_specs=pl.BlockSpec((rank, rank), lambda i: (0, 0)),
        out_shape=jax.ShapeDtypeStruct((rank, rank), F32),
        compiler_params=PARAMS,
        cost_estimate=pl.CostEstimate(
            flops=20_000_000, bytes_accessed=8 * rank * LANES, transcendentals=rank
        ),
        name="inverse_factor",
    )(chunk)


def finish_kernel(plan, where_ref, inverse_ref, *refs):
    out_hbm, buf, sems = refs[-3:]
    _, rank, width = buf.shape
    head, rest = split(inverse_ref[...])
    both = jnp.concatenate([head, rest], axis=0)
    copies = []
    for k, (source, offset) in enumerate(plan):
        p_head, p_rest = split(refs[source][:, offset : offset + width])
        first = dot(both, p_head, PLAIN)
        buf[k] = first[:rank] + (first[rank:] + dot(head, p_rest, PLAIN))
        where = pl.ds(pl.multiple_of(where_ref[k] * width, width), width)
        copies.append(pltpu.make_async_copy(buf.at[k], out_hbm.at[:, where], sems.at[k]))
        copies[k].start()
    for copy in copies:
        copy.wait()


def finish(inverse, sources, pieces, width, total, before=None):
    rank = inverse.shape[0]
    count = len(pieces)
    in_specs = [TABLE, WHOLE, *[WHOLE] * len(sources)]
    args = [jnp.stack([piece[0] for piece in pieces]), inverse, *sources]
    aliases = {}
    if before is not None:
        in_specs.append(HBM)
        args.append(before)
        aliases = {len(args) - 1: 0}
    return pl.pallas_call(
        functools.partial(finish_kernel, [piece[1:] for piece in pieces]),
        in_specs=in_specs,
        out_specs=HBM,
        out_shape=jax.ShapeDtypeStruct((rank, total), F32),
        scratch_shapes=[
            pltpu.VMEM((count, rank, width), F32),
            pltpu.SemaphoreType.DMA((count,)),
        ],
        input_output_aliases=aliases,
        compiler_params=PARAMS,
        cost_estimate=pl.CostEstimate(
            flops=6 * rank * rank * width * count,
            bytes_accessed=8 * rank * width * count,
            transcendentals=0,
        ),
        name="finish",
    )(*args)


def body(n_pos, n_pix, probes, sketch):
    def swap(value, axis, size, bit):
        return lax.ppermute(value, axis, [(i, i ^ bit) for i in range(size)])

    def over(value, turn):
        pairs = [
            (i * n_pix + j, (i ^ (1 << ((turn + j + 1) % 2))) * n_pix + j)
            for i in range(n_pos)
            for j in range(n_pix)
        ]
        return lax.ppermute(value, ("pos", "pix"), pairs)

    def after(value, *others):
        return lax.optimization_barrier((value, *others))[0]

    me = lax.axis_index("pos").astype(jnp.int32)
    odd = lax.axis_index("pix").astype(jnp.int32) & 1
    first_bit, second_bit = (me >> (1 - odd)) & 1, (me >> odd) & 1
    cols = probes.shape[1]
    width = cols // (4 * CHUNKS)

    tall = tall_partial(probes, sketch.T)
    bit = 1
    while 2 * bit < n_pix:
        tall = tall + swap(tall, "pix", n_pix, bit)
        bit *= 2
    other = swap(tall, "pix", n_pix, bit)

    def block(c, p, q):
        return 4 * c + 2 * (first_bit ^ p) + (second_bit ^ q)

    def outputs(c, p):
        return [([block(c, p, 1), block(c, p, 0)], c == 0)]

    both, gram, away = first_products(tall, other, probes, outputs(0, 1), width)

    whole, total, send = [], [], None
    for c in range(CHUNKS):
        g = LANES if c == 0 else 0
        more = outputs(c + 1, 1) if c + 1 < CHUNKS else []
        ready = away[0] if c == 0 else whole[-1]
        own, *made = rest_products(both, gram, probes, outputs(c, 0) + more, width, ready)
        sent = away[0] if c == 0 else after(away[0], send)
        part, away = own + over(sent, 0), made
        send = part[:, : width + g]
        got = over(send, 1)
        added = part[:, width + g :] + got[:, :width]
        if g:
            added = jnp.concatenate([added, part[:, width : width + g] + got[:, width:]], axis=1)
        whole.append(added)
        bit = 4
        while bit < n_pos:
            added = added + swap(added, "pos", n_pos, bit)
            bit *= 2
        total.append(added)

    inverse = inverse_factor(total[0], width)
    sources, pieces = [], []
    for c in range(CHUNKS):
        mine = total[c][:, :width]
        near = over(mine, 1)
        far = over(jnp.concatenate([mine, near], axis=1), 0)
        k = len(sources)
        sources += [mine, near, far]
        pieces += [
            (block(c, 0, 0), k, 0),
            (block(c, 0, 1), k + 1, 0),
            (block(c, 1, 0), k + 2, 0),
            (block(c, 1, 1), k + 2, width),
        ]
    out = finish(inverse, sources[:-1], pieces[:-2], width, cols)
    pieces = [(where, 0, start) for where, _, start in pieces[-2:]]
    return finish(inverse, sources[-1:], pieces, width, cols, out)


def solution(mesh):
    in_specs = (P("pos", "pix"), P("pix", None))
    out_specs = P(None, "pix")
    run = functools.partial(body, mesh.shape["pos"], mesh.shape["pix"])
    return jax.shard_map(run, mesh=mesh, in_specs=in_specs, out_specs=out_specs, check_vma=False)
```

```python
import functools

import jax
import jax.numpy as jnp
from jax import lax
from jax.experimental import pallas as pl
from jax.experimental.pallas import tpu as pltpu
from jax.sharding import PartitionSpec as P

F32 = jnp.float32
BF16 = jnp.bfloat16
VMEM_LIMIT = 40 * 1024 * 1024
LANES = 128
CHUNKS = 2
AHEAD = 6
UNIT = 512
PANEL = 4
LAST = (((1,), (1,)), ((), ()))
PLAIN = (((1,), (0,)), ((), ()))
ANYWHERE = pl.BlockSpec(memory_space=pl.ANY)
HBM = pl.BlockSpec(memory_space=pltpu.MemorySpace.HBM)
WHOLE = pl.BlockSpec(memory_space=pltpu.VMEM)
TABLE = pl.BlockSpec(memory_space=pltpu.SMEM)
PARAMS = pltpu.CompilerParams(vmem_limit_bytes=VMEM_LIMIT)


def split(x):
    head = x.astype(BF16)
    return head, (x - head.astype(F32)).astype(BF16)


def dot(a, b, dims):
    return lax.dot_general(a, b, dims, preferred_element_type=F32)


def in_hbm(x):
    return pltpu.with_memory_space_constraint(x, pltpu.MemorySpace.HBM)


def stream(copies, use):
    for copy in copies[:AHEAD]:
        copy.start()
    for k, copy in enumerate(copies):
        copy.wait()
        if k + AHEAD < len(copies):
            copies[k + AHEAD].start()
        use(k)


def tall_kernel(x_hbm, s_hbm, out_ref, x_buf, s_buf, head_buf, rest_buf, acc, x_sems, s_sems):
    blocks, _, unit = x_buf.shape
    rank = s_hbm.shape[0]

    def copies(k):
        where = pl.ds(k * unit, unit)
        return (
            pltpu.make_async_copy(s_hbm.at[:, where], s_buf.at[k], s_sems.at[k]),
            pltpu.make_async_copy(x_hbm.at[:, where], x_buf.at[k], x_sems.at[k]),
        )

    for k in range(blocks):
        for copy in copies(k):
            copy.start()
    for k in range(blocks):
        for copy in copies(k):
            copy.wait()
        s_both = jnp.concatenate(split(s_buf[k]), axis=0)
        x_head, x_rest = split(x_buf[k])
        head_buf[k] = x_head
        rest_buf[k] = x_rest
        part = dot(x_head, s_both, LAST) + dot(x_rest, s_both, LAST)
        if k == 0:
            acc[...] = part
        else:
            acc[...] += part
    both = acc[...].T
    out_ref[...] = both[:rank] + both[rank:]


def tall_partial(probes, sketch_t):
    rows, cols = probes.shape
    rank = sketch_t.shape[0]
    unit = min(2 * UNIT, cols)
    blocks = cols // unit
    return pl.pallas_call(
        tall_kernel,
        in_specs=[HBM, HBM],
        out_specs=WHOLE,
        out_shape=jax.ShapeDtypeStruct((rank, rows), F32),
        scratch_shapes=[
            pltpu.VMEM((blocks, rows, unit), F32),
            pltpu.VMEM((blocks, rank, unit), F32),
            pltpu.VMEM((blocks, rows, unit), BF16),
            pltpu.VMEM((blocks, rows, unit), BF16),
            pltpu.VMEM((rows, 2 * rank), F32),
            pltpu.SemaphoreType.DMA((blocks,)),
            pltpu.SemaphoreType.DMA((blocks,)),
        ],
        compiler_params=PARAMS,
        cost_estimate=pl.CostEstimate(
            flops=6 * rows * cols * rank, bytes_accessed=4 * rows * cols, transcendentals=0
        ),
        name="tall_partial",
    )(in_hbm(probes), in_hbm(sketch_t))


def multiply_blocks(both_ref, which_ref, x_hbm, x_buf, sems, plan, outs):
    rank = outs[0].shape[0]
    unit = x_buf.shape[2]
    copies = [
        pltpu.make_async_copy(
            x_hbm.at[:, pl.ds(pl.multiple_of(which_ref[k] * unit, unit), unit)],
            x_buf.at[k],
            sems.at[k],
        )
        for k in range(len(plan))
    ]

    def use(k):
        both = both_ref[...]
        x_head, x_rest = split(x_buf[k])
        first = dot(both, x_head, PLAIN)
        second = dot(both[:rank], x_rest, PLAIN)
        out, offset = plan[k]
        outs[out][:, offset : offset + unit] = first[:rank] + (first[rank:] + second)

    return copies, use


def first_kernel(plan, grams, which_ref, one_ref, two_ref, x_hbm, both_ref, gram_ref, *refs):
    outs, (x_buf, sems) = refs[:-2], refs[-2:]
    copies, use = multiply_blocks(both_ref, which_ref, x_hbm, x_buf, sems, plan, outs)

    def use_first(k):
        if k == 0:
            tall = one_ref[...] + two_ref[...]
            head, rest = split(tall)
            both_ref[...] = jnp.concatenate([head, rest], axis=0)
        use(k)

    stream(copies, use_first)
    tall = one_ref[...] + two_ref[...]
    r = tall.shape[0]
    head, rest = split(tall)
    tail = (tall - head.astype(F32) - rest.astype(F32)).astype(BF16)
    three = jnp.concatenate([head, rest, tail], axis=0)
    g = dot(three, three, LAST)
    cross = g[:r, r : 2 * r] + g[r : 2 * r, :r]
    small = g[:r, 2 * r :] + g[2 * r :, :r] + g[r : 2 * r, r : 2 * r]
    gram = g[:r, :r] + (cross + small)
    gram_ref[...] = jnp.concatenate([gram, jnp.zeros((r, LANES - r), F32)], axis=1)
    for out, offset in grams:
        outs[out][:, offset : offset + LANES] = gram_ref[...]


def rest_kernel(plan, grams, which_ref, both_ref, gram_ref, x_hbm, after_ref, *refs):
    outs, (x_buf, sems) = refs[:-2], refs[-2:]
    copies, use = multiply_blocks(both_ref, which_ref, x_hbm, x_buf, sems, plan, outs)
    stream(copies, use)
    for out, offset in grams:
        outs[out][:, offset : offset + LANES] = gram_ref[...]


def layout(outputs, sub):
    unit = min(UNIT, sub)
    plan, grams, widths, which = [], [], [], []
    for out, (blocks, with_gram) in enumerate(outputs):
        extra = LANES if with_gram else 0
        for j, block in enumerate(blocks):
            for part in range(sub // unit):
                plan.append((out, j * sub + part * unit + (extra if j else 0)))
                which.append(block * (sub // unit) + part)
        if with_gram:
            grams.append((out, sub))
        widths.append(len(blocks) * sub + extra)
    return unit, plan, grams, widths, jnp.stack(which)


def products(kernel, inputs, in_specs, made, probes, outputs, sub, name):
    rows = probes.shape[0]
    rank = inputs[1].shape[0]
    unit, plan, grams, widths, which = layout(outputs, sub)
    shapes = [*made, *[jax.ShapeDtypeStruct((rank, width), F32) for width in widths]]
    return pl.pallas_call(
        functools.partial(kernel, plan, grams),
        in_specs=[TABLE, *in_specs],
        out_specs=[WHOLE] * len(shapes),
        out_shape=shapes,
        scratch_shapes=[
            pltpu.VMEM((len(plan), rows, unit), F32),
            pltpu.SemaphoreType.DMA((len(plan),)),
        ],
        compiler_params=PARAMS,
        cost_estimate=pl.CostEstimate(
            flops=6 * rows * rank * unit * len(plan),
            bytes_accessed=4 * rows * unit * len(plan),
            transcendentals=0,
        ),
        name=name,
    )(which, *inputs)


def first_products(one, two, probes, outputs, sub):
    rank, rows = one.shape
    made = [
        jax.ShapeDtypeStruct((2 * rank, rows), BF16),
        jax.ShapeDtypeStruct((rank, LANES), F32),
    ]
    both, gram, *outs = products(
        first_kernel,
        [one, two, in_hbm(probes)],
        [WHOLE, WHOLE, HBM],
        made,
        probes,
        outputs,
        sub,
        "first_products",
    )
    return both, gram, outs


def rest_products(both, gram, probes, outputs, sub, after):
    return products(
        rest_kernel,
        [both, gram, in_hbm(probes), after],
        [WHOLE, WHOLE, HBM, ANYWHERE],
        [],
        probes,
        outputs,
        sub,
        "rest_products",
    )


def inverse_kernel(gram_ref, out_ref):
    rank = out_ref.shape[0]
    rows = lax.broadcasted_iota(jnp.int32, (rank, LANES), 0)
    cols = lax.broadcasted_iota(jnp.int32, (rank, LANES), 1)
    work = jnp.where(cols < rank, gram_ref[...], (cols == rows + rank).astype(F32))
    scale = jnp.ones((rank, LANES), F32)
    for start in range(0, rank, PANEL):
        panel = [
            jnp.broadcast_to(work[:, k : k + 1], (rank, LANES))
            for k in range(start, start + PANEL)
        ]
        for j in range(PANEL):
            k = start + j
            over = 1.0 / panel[j][k : k + 1, :]
            scale = jnp.where(rows == k, over, scale)
            factor = jnp.where(rows > k, panel[j] * over, 0.0)
            work = work - factor * work[k : k + 1, :]
            for later in range(j + 1, PANEL):
                panel[later] = panel[later] - factor * panel[later][k : k + 1, :]
    out_ref[...] = (work * jnp.sqrt(scale))[:, rank : 2 * rank]


def inverse_factor(chunk, start):
    rank = chunk.shape[0]
    return pl.pallas_call(
        inverse_kernel,
        grid=(1,),
        in_specs=[pl.BlockSpec((rank, LANES), lambda i: (0, start // LANES))],
        out_specs=pl.BlockSpec((rank, rank), lambda i: (0, 0)),
        out_shape=jax.ShapeDtypeStruct((rank, rank), F32),
        compiler_params=PARAMS,
        cost_estimate=pl.CostEstimate(
            flops=20_000_000, bytes_accessed=8 * rank * LANES, transcendentals=rank
        ),
        name="inverse_factor",
    )(chunk)


def finish_kernel(plan, where_ref, inverse_ref, *refs):
    out_hbm, buf, sems = refs[-3:]
    _, rank, width = buf.shape
    head, rest = split(inverse_ref[...])
    both = jnp.concatenate([head, rest], axis=0)
    copies = []
    for k, (source, offset) in enumerate(plan):
        p_head, p_rest = split(refs[source][:, offset : offset + width])
        first = dot(both, p_head, PLAIN)
        buf[k] = first[:rank] + (first[rank:] + dot(head, p_rest, PLAIN))
        where = pl.ds(pl.multiple_of(where_ref[k] * width, width), width)
        copies.append(pltpu.make_async_copy(buf.at[k], out_hbm.at[:, where], sems.at[k]))
        copies[k].start()
    for copy in copies:
        copy.wait()


def finish(inverse, sources, pieces, width, total, before=None):
    rank = inverse.shape[0]
    count = len(pieces)
    in_specs = [TABLE, WHOLE, *[WHOLE] * len(sources)]
    args = [jnp.stack([piece[0] for piece in pieces]), inverse, *sources]
    aliases = {}
    if before is not None:
        in_specs.append(HBM)
        args.append(before)
        aliases = {len(args) - 1: 0}
    return pl.pallas_call(
        functools.partial(finish_kernel, [piece[1:] for piece in pieces]),
        in_specs=in_specs,
        out_specs=HBM,
        out_shape=jax.ShapeDtypeStruct((rank, total), F32),
        scratch_shapes=[
            pltpu.VMEM((count, rank, width), F32),
            pltpu.SemaphoreType.DMA((count,)),
        ],
        input_output_aliases=aliases,
        compiler_params=PARAMS,
        cost_estimate=pl.CostEstimate(
            flops=6 * rank * rank * width * count,
            bytes_accessed=8 * rank * width * count,
            transcendentals=0,
        ),
        name="finish",
    )(*args)


def body(n_pos, n_pix, probes, sketch):
    def swap(value, axis, size, bit):
        return lax.ppermute(value, axis, [(i, i ^ bit) for i in range(size)])

    def over(value, bit):
        if bit > 2:
            return swap(value, "pos", n_pos, bit)
        pairs = [
            (i * n_pix + j, (i ^ (bit if j % 2 else 3 - bit)) * n_pix + j)
            for i in range(n_pos)
            for j in range(n_pix)
        ]
        return lax.ppermute(value, ("pos", "pix"), pairs)

    me = lax.axis_index("pos").astype(jnp.int32)
    odd = lax.axis_index("pix").astype(jnp.int32) & 1
    near, far = (me >> (1 - odd)) & 1, (me >> odd) & 1
    cols = probes.shape[1]
    width = cols // (8 * CHUNKS)

    tall = tall_partial(probes, sketch.T)
    bit = 1
    while 2 * bit < n_pix:
        tall = tall + swap(tall, "pix", n_pix, bit)
        bit *= 2
    other = swap(tall, "pix", n_pix, bit)

    def block_a(c, p, q):
        return 8 * c + 2 * (near ^ p) + (far ^ q)

    def block_b(c, p, q):
        return 8 * c + 4 + 2 * (far ^ p) + (near ^ q)

    def outputs(c, p):
        return [
            ([block_a(c, p, 1), block_a(c, p, 0)], c == 0),
            ([block_b(c, p, 1), block_b(c, p, 0)], False),
        ]

    both, gram, away = first_products(tall, other, probes, outputs(0, 1), width)

    inverse, out, after = None, None, away[0]
    for c in range(CHUNKS):
        g = LANES if c == 0 else 0
        last = c == CHUNKS - 1
        made = rest_products(
            both, gram, probes, outputs(c, 0) + ([] if last else outputs(c + 1, 1)), width, after
        )
        away_a, away_b = away
        (own_a, own_b), away = made[:2], made[2:]
        got_a = over(away_a, 1)
        sum_a = own_a + got_a
        sum_b = own_b + over(away_b, 2)
        after = got_a
        send_a, send_b = sum_a[:, : width + g], sum_b[:, :width]
        if c > 0:
            send_a, send_b, whole = lax.optimization_barrier((send_a, send_b, whole))
        got_a = over(send_a, 2)
        got_b = over(send_b, 1)
        whole = jnp.concatenate(
            [
                sum_a[:, width + g :] + got_a[:, :width],
                sum_a[:, width : width + g] + got_a[:, width:],
                sum_b[:, width:] + got_b,
            ],
            axis=1,
        )
        total = whole
        bit = 4
        while bit < n_pos:
            total = total + over(total, bit)
            bit *= 2
        if c == 0:
            inverse = inverse_factor(total, width)
        mine_a, mine_b = total[:, :width], total[:, width + g :]
        if c > 0:
            mine_a, mine_b, inverse = lax.optimization_barrier((mine_a, mine_b, inverse))
        next_a = over(mine_a, 2)
        next_b = over(mine_b, 1)
        last_a = over(jnp.concatenate([mine_a, next_a], axis=1), 1)
        last_b = over(jnp.concatenate([mine_b, next_b], axis=1), 2)
        sources = [total, next_a, next_b]
        pieces = [
            (block_a(c, 0, 0), 0, 0),
            (block_b(c, 0, 0), 0, width + g),
            (block_a(c, 0, 1), 1, 0),
            (block_b(c, 0, 1), 2, 0),
        ]
        if last:
            out = finish(inverse, sources, pieces, width, cols, out)
            sources, pieces = [], []
        k = len(sources)
        sources += [last_a, last_b]
        pieces += [
            (block_a(c, 1, 0), k, 0),
            (block_a(c, 1, 1), k, width),
            (block_b(c, 1, 0), k + 1, 0),
            (block_b(c, 1, 1), k + 1, width),
        ]
        out = finish(inverse, sources, pieces, width, cols, out)
    return out


def solution(mesh):
    in_specs = (P("pos", "pix"), P("pix", None))
    out_specs = P(None, "pix")
    run = functools.partial(body, mesh.shape["pos"], mesh.shape["pix"])
    return jax.shard_map(run, mesh=mesh, in_specs=in_specs, out_specs=out_specs, check_vma=False)
```

```python
import functools

import jax
import jax.numpy as jnp
from jax import lax
from jax.experimental import pallas as pl
from jax.experimental.pallas import tpu as pltpu
from jax.sharding import PartitionSpec as P

F32 = jnp.float32
BF16 = jnp.bfloat16
VMEM_LIMIT = 40 * 1024 * 1024
LANES = 128
SHARES = (3, 5)
AHEAD = 6
UNIT = 512
PANEL = 4
LAST = (((1,), (1,)), ((), ()))
PLAIN = (((1,), (0,)), ((), ()))
ANYWHERE = pl.BlockSpec(memory_space=pl.ANY)
HBM = pl.BlockSpec(memory_space=pltpu.MemorySpace.HBM)
WHOLE = pl.BlockSpec(memory_space=pltpu.VMEM)
TABLE = pl.BlockSpec(memory_space=pltpu.SMEM)
PARAMS = pltpu.CompilerParams(vmem_limit_bytes=VMEM_LIMIT)


def split(x):
    head = x.astype(BF16)
    return head, (x - head.astype(F32)).astype(BF16)


def dot(a, b, dims):
    return lax.dot_general(a, b, dims, preferred_element_type=F32)


def in_hbm(x):
    return pltpu.with_memory_space_constraint(x, pltpu.MemorySpace.HBM)


def stream(copies, use):
    for copy in copies[:AHEAD]:
        copy.start()
    for k, copy in enumerate(copies):
        copy.wait()
        if k + AHEAD < len(copies):
            copies[k + AHEAD].start()
        use(k)


def tall_kernel(x_hbm, s_hbm, out_ref, x_buf, s_buf, head_buf, rest_buf, x_sems, s_sems):
    blocks, _, unit = x_buf.shape
    rank = s_hbm.shape[0]

    def copies(k):
        where = pl.ds(k * unit, unit)
        return (
            pltpu.make_async_copy(s_hbm.at[:, where], s_buf.at[k], s_sems.at[k]),
            pltpu.make_async_copy(x_hbm.at[:, where], x_buf.at[k], x_sems.at[k]),
        )

    for k in range(blocks):
        for copy in copies(k):
            copy.start()
    for k in range(blocks):
        for copy in copies(k):
            copy.wait()
        s_head, s_rest = split(s_buf[k])
        s_both = jnp.concatenate([s_head, s_rest], axis=0)
        x_head, x_rest = split(x_buf[k])
        head_buf[k] = x_head
        rest_buf[k] = x_rest
        both = dot(s_both, x_head, LAST)
        part = both[:rank] + (both[rank:] + dot(s_head, x_rest, LAST))
        if k == 0:
            out_ref[...] = part
        else:
            out_ref[...] += part


def tall_partial(probes, sketch_t):
    rows, cols = probes.shape
    rank = sketch_t.shape[0]
    unit = min(2 * UNIT, cols)
    blocks = cols // unit
    return pl.pallas_call(
        tall_kernel,
        in_specs=[HBM, HBM],
        out_specs=WHOLE,
        out_shape=jax.ShapeDtypeStruct((rank, rows), F32),
        scratch_shapes=[
            pltpu.VMEM((blocks, rows, unit), F32),
            pltpu.VMEM((blocks, rank, unit), F32),
            pltpu.VMEM((blocks, rows, unit), BF16),
            pltpu.VMEM((blocks, rows, unit), BF16),
            pltpu.SemaphoreType.DMA((blocks,)),
            pltpu.SemaphoreType.DMA((blocks,)),
        ],
        compiler_params=PARAMS,
        cost_estimate=pl.CostEstimate(
            flops=6 * rows * cols * rank, bytes_accessed=4 * rows * cols, transcendentals=0
        ),
        name="tall_partial",
    )(in_hbm(probes), in_hbm(sketch_t))


def multiply_blocks(both_ref, start_ref, x_hbm, x_buf, sems, plan, outs):
    rank = outs[0].shape[0]
    copies = [
        pltpu.make_async_copy(
            x_hbm.at[:, pl.ds(pl.multiple_of(start_ref[k] * LANES, LANES), unit)],
            x_buf.at[k, :, pl.ds(0, unit)],
            sems.at[k],
        )
        for k, (_, _, unit) in enumerate(plan)
    ]

    def use(k):
        both = both_ref[...]
        out, offset, unit = plan[k]
        x_head, x_rest = split(x_buf[k, :, :unit])
        first = dot(both, x_head, PLAIN)
        second = dot(both[:rank], x_rest, PLAIN)
        outs[out][:, offset : offset + unit] = first[:rank] + (first[rank:] + second)

    return copies, use


def first_kernel(plan, grams, which_ref, one_ref, two_ref, x_hbm, both_ref, gram_ref, *refs):
    outs, (x_buf, sems) = refs[:-2], refs[-2:]
    copies, use = multiply_blocks(both_ref, which_ref, x_hbm, x_buf, sems, plan, outs)

    def use_first(k):
        if k == 0:
            tall = one_ref[...] + two_ref[...]
            head, rest = split(tall)
            both_ref[...] = jnp.concatenate([head, rest], axis=0)
        use(k)

    stream(copies, use_first)
    tall = one_ref[...] + two_ref[...]
    r = tall.shape[0]
    head, rest = split(tall)
    tail = (tall - head.astype(F32) - rest.astype(F32)).astype(BF16)
    three = jnp.concatenate([head, rest, tail], axis=0)
    g = dot(three, three, LAST)
    cross = g[:r, r : 2 * r] + g[r : 2 * r, :r]
    small = g[:r, 2 * r :] + g[2 * r :, :r] + g[r : 2 * r, r : 2 * r]
    gram = g[:r, :r] + (cross + small)
    gram_ref[...] = jnp.concatenate([gram, jnp.zeros((r, LANES - r), F32)], axis=1)
    for out, offset in grams:
        outs[out][:, offset : offset + LANES] = gram_ref[...]


def rest_kernel(plan, grams, which_ref, both_ref, gram_ref, x_hbm, after_ref, *refs):
    outs, (x_buf, sems) = refs[:-2], refs[-2:]
    copies, use = multiply_blocks(both_ref, which_ref, x_hbm, x_buf, sems, plan, outs)
    stream(copies, use)
    for out, offset in grams:
        outs[out][:, offset : offset + LANES] = gram_ref[...]


def layout(outputs):
    plan, grams, widths, starts = [], [], [], []
    for out, (blocks, sub, with_gram) in enumerate(outputs):
        extra = LANES if with_gram else 0
        for j, block in enumerate(blocks):
            plan.append((out, j * sub + (extra if j else 0), sub))
            starts.append(block)
        if with_gram:
            grams.append((out, sub))
        widths.append(len(blocks) * sub + extra)
    return plan, grams, widths, jnp.stack(starts)


def products(kernel, inputs, in_specs, made, probes, outputs, name):
    rows = probes.shape[0]
    rank = inputs[1].shape[0]
    plan, grams, widths, starts = layout(outputs)
    unit = max(entry[2] for entry in plan)
    shapes = [*made, *[jax.ShapeDtypeStruct((rank, width), F32) for width in widths]]
    return pl.pallas_call(
        functools.partial(kernel, plan, grams),
        in_specs=[TABLE, *in_specs],
        out_specs=[WHOLE] * len(shapes),
        out_shape=shapes,
        scratch_shapes=[
            pltpu.VMEM((len(plan), rows, unit), F32),
            pltpu.SemaphoreType.DMA((len(plan),)),
        ],
        compiler_params=PARAMS,
        cost_estimate=pl.CostEstimate(
            flops=6 * rows * rank * unit * len(plan),
            bytes_accessed=4 * rows * unit * len(plan),
            transcendentals=0,
        ),
        name=name,
    )(starts, *inputs)


def first_products(one, two, probes, outputs):
    rank, rows = one.shape
    made = [
        jax.ShapeDtypeStruct((2 * rank, rows), BF16),
        jax.ShapeDtypeStruct((rank, LANES), F32),
    ]
    both, gram, *outs = products(
        first_kernel,
        [one, two, in_hbm(probes)],
        [WHOLE, WHOLE, HBM],
        made,
        probes,
        outputs,
        "first_products",
    )
    return both, gram, outs


def rest_products(both, gram, probes, outputs, after):
    return products(
        rest_kernel,
        [both, gram, in_hbm(probes), after],
        [WHOLE, WHOLE, HBM, ANYWHERE],
        [],
        probes,
        outputs,
        "rest_products",
    )


def inverse_kernel(gram_ref, out_ref):
    rank = out_ref.shape[0]
    rows = lax.broadcasted_iota(jnp.int32, (rank, LANES), 0)
    cols = lax.broadcasted_iota(jnp.int32, (rank, LANES), 1)
    work = jnp.where(cols < rank, gram_ref[...], (cols == rows + rank).astype(F32))
    scale = jnp.ones((rank, LANES), F32)
    for start in range(0, rank, PANEL):
        panel = [
            jnp.broadcast_to(work[:, k : k + 1], (rank, LANES))
            for k in range(start, start + PANEL)
        ]
        for j in range(PANEL):
            k = start + j
            over = 1.0 / panel[j][k : k + 1, :]
            scale = jnp.where(rows == k, over, scale)
            factor = jnp.where(rows > k, panel[j] * over, 0.0)
            work = work - factor * work[k : k + 1, :]
            for later in range(j + 1, PANEL):
                panel[later] = panel[later] - factor * panel[later][k : k + 1, :]
    out_ref[...] = (work * jnp.sqrt(scale))[:, rank : 2 * rank]


def inverse_factor(chunk, start):
    rank = chunk.shape[0]
    return pl.pallas_call(
        inverse_kernel,
        grid=(1,),
        in_specs=[pl.BlockSpec((rank, LANES), lambda i: (0, start // LANES))],
        out_specs=pl.BlockSpec((rank, rank), lambda i: (0, 0)),
        out_shape=jax.ShapeDtypeStruct((rank, rank), F32),
        compiler_params=PARAMS,
        cost_estimate=pl.CostEstimate(
            flops=20_000_000, bytes_accessed=8 * rank * LANES, transcendentals=rank
        ),
        name="inverse_factor",
    )(chunk)


def finish_kernel(plan, where_ref, inverse_ref, *refs):
    out_hbm, buf, sems = refs[-3:]
    rank = buf.shape[1]
    head, rest = split(inverse_ref[...])
    both = jnp.concatenate([head, rest], axis=0)
    copies = []
    for k, (source, offset, width) in enumerate(plan):
        p_head, p_rest = split(refs[source][:, offset : offset + width])
        first = dot(both, p_head, PLAIN)
        buf[k, :, :width] = first[:rank] + (first[rank:] + dot(head, p_rest, PLAIN))
        where = pl.ds(pl.multiple_of(where_ref[k] * LANES, LANES), width)
        part = buf.at[k, :, pl.ds(0, width)]
        copies.append(pltpu.make_async_copy(part, out_hbm.at[:, where], sems.at[k]))
        copies[k].start()
    for copy in copies:
        copy.wait()


def finish(inverse, sources, pieces, width, total, before=None):
    rank = inverse.shape[0]
    count = len(pieces)
    in_specs = [TABLE, WHOLE, *[WHOLE] * len(sources)]
    args = [jnp.stack([piece[0] for piece in pieces]), inverse, *sources]
    aliases = {}
    if before is not None:
        in_specs.append(HBM)
        args.append(before)
        aliases = {len(args) - 1: 0}
    return pl.pallas_call(
        functools.partial(finish_kernel, [(*piece[1:], width) for piece in pieces]),
        in_specs=in_specs,
        out_specs=HBM,
        out_shape=jax.ShapeDtypeStruct((rank, total), F32),
        scratch_shapes=[
            pltpu.VMEM((count, rank, width), F32),
            pltpu.SemaphoreType.DMA((count,)),
        ],
        input_output_aliases=aliases,
        compiler_params=PARAMS,
        cost_estimate=pl.CostEstimate(
            flops=6 * rank * rank * width * count,
            bytes_accessed=8 * rank * width * count,
            transcendentals=0,
        ),
        name="finish",
    )(*args)


def body(n_pos, n_pix, probes, sketch):
    def swap(value, axis, size, bit):
        return lax.ppermute(value, axis, [(i, i ^ bit) for i in range(size)])

    def over(value, bit):
        return swap(value, "pos", n_pos, bit)

    me = lax.axis_index("pos").astype(jnp.int32)
    near, far = me & 1, (me >> 1) & 1
    cols = probes.shape[1]
    widths = [cols // 8 * share // sum(SHARES) for share in SHARES]
    firsts = [8 * sum(widths[:c]) // LANES for c in range(len(widths))]

    tall = tall_partial(probes, sketch.T)
    bit = 1
    while 2 * bit < n_pix:
        tall = tall + swap(tall, "pix", n_pix, bit)
        bit *= 2
    other = swap(tall, "pix", n_pix, bit)

    def block_a(c, p, q):
        return firsts[c] + (2 * (near ^ p) + (far ^ q)) * (widths[c] // LANES)

    def block_b(c, p, q):
        return firsts[c] + (4 + 2 * (far ^ p) + (near ^ q)) * (widths[c] // LANES)

    def outputs(c, p):
        return [
            ([block_a(c, p, 1), block_a(c, p, 0)], widths[c], c == 0),
            ([block_b(c, p, 1), block_b(c, p, 0)], widths[c], False),
        ]

    both, gram, away = first_products(tall, other, probes, outputs(0, 1))

    inverse, out, after = None, None, away[0]
    for c, width in enumerate(widths):
        g = LANES if c == 0 else 0
        last = c == len(widths) - 1
        made = rest_products(
            both, gram, probes, outputs(c, 0) + ([] if last else outputs(c + 1, 1)), after
        )
        away_a, away_b = away
        (own_a, own_b), away = made[:2], made[2:]
        got_a = over(away_a, 1)
        sum_a = own_a + got_a
        sum_b = own_b + over(away_b, 2)
        after = got_a
        send_a, send_b = sum_a[:, : width + g], sum_b[:, :width]
        if c > 0:
            send_a, send_b, whole = lax.optimization_barrier((send_a, send_b, whole))
        got_a = over(send_a, 2)
        got_b = over(send_b, 1)
        whole = jnp.concatenate(
            [
                sum_a[:, width + g :] + got_a[:, :width],
                sum_a[:, width : width + g] + got_a[:, width:],
                sum_b[:, width:] + got_b,
            ],
            axis=1,
        )
        total = whole
        bit = 4
        while bit < n_pos:
            total = total + over(total, bit)
            bit *= 2
        mine_a, mine_b = total[:, :width], total[:, width + g :]
        if c > 0:
            mine_a, mine_b, *_ = lax.optimization_barrier((mine_a, mine_b, inverse, last_a, last_b))
        next_a = over(mine_a, 2)
        next_b = over(mine_b, 1)
        if c == 0:
            held = lax.optimization_barrier((total, next_a, next_b))[0]
            inverse = inverse_factor(held, width)
        last_a = over(jnp.concatenate([mine_a, next_a], axis=1), 1)
        last_b = over(jnp.concatenate([mine_b, next_b], axis=1), 2)
        sources = [total, next_a, next_b]
        pieces = [
            (block_a(c, 0, 0), 0, 0),
            (block_b(c, 0, 0), 0, width + g),
            (block_a(c, 0, 1), 1, 0),
            (block_b(c, 0, 1), 2, 0),
        ]
        if last:
            out = finish(inverse, sources, pieces, width, cols, out)
            sources, pieces = [], []
        k = len(sources)
        sources += [last_a, last_b]
        pieces += [
            (block_a(c, 1, 0), k, 0),
            (block_a(c, 1, 1), k, width),
            (block_b(c, 1, 0), k + 1, 0),
            (block_b(c, 1, 1), k + 1, width),
        ]
        out = finish(inverse, sources, pieces, width, cols, out)
    return out


def solution(mesh):
    in_specs = (P("pos", "pix"), P("pix", None))
    out_specs = P(None, "pix")
    run = functools.partial(body, mesh.shape["pos"], mesh.shape["pix"])
    return jax.shard_map(run, mesh=mesh, in_specs=in_specs, out_specs=out_specs, check_vma=False)
```

```python
import functools

import jax
import jax.numpy as jnp
from jax import lax
from jax.experimental import pallas as pl
from jax.experimental.pallas import tpu as pltpu
from jax.sharding import PartitionSpec as P

F32 = jnp.float32
BF16 = jnp.bfloat16
VMEM_LIMIT = 40 * 1024 * 1024
LANES = 128
CHUNKS = 2
AHEAD = 6
UNIT = 512
PANEL = 4
LAST = (((1,), (1,)), ((), ()))
PLAIN = (((1,), (0,)), ((), ()))
ANYWHERE = pl.BlockSpec(memory_space=pl.ANY)
HBM = pl.BlockSpec(memory_space=pltpu.MemorySpace.HBM)
WHOLE = pl.BlockSpec(memory_space=pltpu.VMEM)
TABLE = pl.BlockSpec(memory_space=pltpu.SMEM)
PARAMS = pltpu.CompilerParams(vmem_limit_bytes=VMEM_LIMIT)


def split(x):
    head = x.astype(BF16)
    return head, (x - head.astype(F32)).astype(BF16)


def dot(a, b, dims):
    return lax.dot_general(a, b, dims, preferred_element_type=F32)


def in_hbm(x):
    return pltpu.with_memory_space_constraint(x, pltpu.MemorySpace.HBM)


def stream(copies, use):
    for copy in copies[:AHEAD]:
        copy.start()
    for k, copy in enumerate(copies):
        copy.wait()
        if k + AHEAD < len(copies):
            copies[k + AHEAD].start()
        use(k)


def tall_kernel(x_hbm, s_hbm, out_ref, x_buf, s_buf, head_buf, rest_buf, x_sems, s_sems):
    blocks, _, unit = x_buf.shape
    rank = s_hbm.shape[0]

    def copies(k):
        where = pl.ds(k * unit, unit)
        return (
            pltpu.make_async_copy(s_hbm.at[:, where], s_buf.at[k], s_sems.at[k]),
            pltpu.make_async_copy(x_hbm.at[:, where], x_buf.at[k], x_sems.at[k]),
        )

    for k in range(blocks):
        for copy in copies(k):
            copy.start()
    for k in range(blocks):
        for copy in copies(k):
            copy.wait()
        s_head, s_rest = split(s_buf[k])
        s_both = jnp.concatenate([s_head, s_rest], axis=0)
        x_head, x_rest = split(x_buf[k])
        head_buf[k] = x_head
        rest_buf[k] = x_rest
        both = dot(s_both, x_head, LAST)
        part = both[:rank] + (both[rank:] + dot(s_head, x_rest, LAST))
        if k == 0:
            out_ref[...] = part
        else:
            out_ref[...] += part


def tall_partial(probes, sketch_t):
    rows, cols = probes.shape
    rank = sketch_t.shape[0]
    unit = min(2 * UNIT, cols)
    blocks = cols // unit
    return pl.pallas_call(
        tall_kernel,
        in_specs=[HBM, HBM],
        out_specs=WHOLE,
        out_shape=jax.ShapeDtypeStruct((rank, rows), F32),
        scratch_shapes=[
            pltpu.VMEM((blocks, rows, unit), F32),
            pltpu.VMEM((blocks, rank, unit), F32),
            pltpu.VMEM((blocks, rows, unit), BF16),
            pltpu.VMEM((blocks, rows, unit), BF16),
            pltpu.SemaphoreType.DMA((blocks,)),
            pltpu.SemaphoreType.DMA((blocks,)),
        ],
        compiler_params=PARAMS,
        cost_estimate=pl.CostEstimate(
            flops=6 * rows * cols * rank, bytes_accessed=4 * rows * cols, transcendentals=0
        ),
        name="tall_partial",
    )(in_hbm(probes), in_hbm(sketch_t))


def multiply_blocks(both_ref, which_ref, x_hbm, x_buf, sems, plan, outs):
    rank = outs[0].shape[0]
    unit = x_buf.shape[2]
    copies = [
        pltpu.make_async_copy(
            x_hbm.at[:, pl.ds(pl.multiple_of(which_ref[k] * unit, unit), unit)],
            x_buf.at[k],
            sems.at[k],
        )
        for k in range(len(plan))
    ]

    def use(k):
        both = both_ref[...]
        x_head, x_rest = split(x_buf[k])
        first = dot(both, x_head, PLAIN)
        second = dot(both[:rank], x_rest, PLAIN)
        out, offset = plan[k]
        outs[out][:, offset : offset + unit] = first[:rank] + (first[rank:] + second)

    return copies, use


def first_kernel(plan, grams, which_ref, one_ref, two_ref, x_hbm, both_ref, gram_ref, *refs):
    outs, (x_buf, sems) = refs[:-2], refs[-2:]
    copies, use = multiply_blocks(both_ref, which_ref, x_hbm, x_buf, sems, plan, outs)

    def use_first(k):
        if k == 0:
            tall = one_ref[...] + two_ref[...]
            head, rest = split(tall)
            both_ref[...] = jnp.concatenate([head, rest], axis=0)
        use(k)

    stream(copies, use_first)
    tall = one_ref[...] + two_ref[...]
    r = tall.shape[0]
    head, rest = split(tall)
    tail = (tall - head.astype(F32) - rest.astype(F32)).astype(BF16)
    three = jnp.concatenate([head, rest, tail], axis=0)
    g = dot(three, three, LAST)
    cross = g[:r, r : 2 * r] + g[r : 2 * r, :r]
    small = g[:r, 2 * r :] + g[2 * r :, :r] + g[r : 2 * r, r : 2 * r]
    gram = g[:r, :r] + (cross + small)
    gram_ref[...] = jnp.concatenate([gram, jnp.zeros((r, LANES - r), F32)], axis=1)
    for out, offset in grams:
        outs[out][:, offset : offset + LANES] = gram_ref[...]


def rest_kernel(plan, grams, which_ref, both_ref, gram_ref, x_hbm, after_ref, *refs):
    outs, (x_buf, sems) = refs[:-2], refs[-2:]
    copies, use = multiply_blocks(both_ref, which_ref, x_hbm, x_buf, sems, plan, outs)
    stream(copies, use)
    for out, offset in grams:
        outs[out][:, offset : offset + LANES] = gram_ref[...]


def layout(outputs, sub):
    unit = min(UNIT, sub)
    plan, grams, widths, which = [], [], [], []
    for out, (blocks, with_gram) in enumerate(outputs):
        extra = LANES if with_gram else 0
        for j, block in enumerate(blocks):
            for part in range(sub // unit):
                plan.append((out, j * sub + part * unit + (extra if j else 0)))
                which.append(block * (sub // unit) + part)
        if with_gram:
            grams.append((out, sub))
        widths.append(len(blocks) * sub + extra)
    return unit, plan, grams, widths, jnp.stack(which)


def products(kernel, inputs, in_specs, made, probes, outputs, sub, name):
    rows = probes.shape[0]
    rank = inputs[1].shape[0]
    unit, plan, grams, widths, which = layout(outputs, sub)
    shapes = [*made, *[jax.ShapeDtypeStruct((rank, width), F32) for width in widths]]
    return pl.pallas_call(
        functools.partial(kernel, plan, grams),
        in_specs=[TABLE, *in_specs],
        out_specs=[WHOLE] * len(shapes),
        out_shape=shapes,
        scratch_shapes=[
            pltpu.VMEM((len(plan), rows, unit), F32),
            pltpu.SemaphoreType.DMA((len(plan),)),
        ],
        compiler_params=PARAMS,
        cost_estimate=pl.CostEstimate(
            flops=6 * rows * rank * unit * len(plan),
            bytes_accessed=4 * rows * unit * len(plan),
            transcendentals=0,
        ),
        name=name,
    )(which, *inputs)


def first_products(one, two, probes, outputs, sub):
    rank, rows = one.shape
    made = [
        jax.ShapeDtypeStruct((2 * rank, rows), BF16),
        jax.ShapeDtypeStruct((rank, LANES), F32),
    ]
    both, gram, *outs = products(
        first_kernel,
        [one, two, in_hbm(probes)],
        [WHOLE, WHOLE, HBM],
        made,
        probes,
        outputs,
        sub,
        "first_products",
    )
    return both, gram, outs


def rest_products(both, gram, probes, outputs, sub, after):
    return products(
        rest_kernel,
        [both, gram, in_hbm(probes), after],
        [WHOLE, WHOLE, HBM, ANYWHERE],
        [],
        probes,
        outputs,
        sub,
        "rest_products",
    )


def hold_kernel(*refs):
    pass


def hold(arrays, after, flops):
    count = len(arrays)
    return pl.pallas_call(
        hold_kernel,
        in_specs=[ANYWHERE] * (count + 1),
        out_specs=[ANYWHERE] * count,
        out_shape=[jax.ShapeDtypeStruct(array.shape, array.dtype) for array in arrays],
        input_output_aliases={k: k for k in range(count)},
        cost_estimate=pl.CostEstimate(flops=flops, bytes_accessed=0, transcendentals=0),
        name="hold",
    )(*arrays, after)


def inverse_kernel(gram_ref, out_ref):
    rank = out_ref.shape[0]
    rows = lax.broadcasted_iota(jnp.int32, (rank, LANES), 0)
    cols = lax.broadcasted_iota(jnp.int32, (rank, LANES), 1)
    work = jnp.where(cols < rank, gram_ref[...], (cols == rows + rank).astype(F32))
    scale = jnp.ones((rank, LANES), F32)
    for start in range(0, rank, PANEL):
        panel = [
            jnp.broadcast_to(work[:, k : k + 1], (rank, LANES))
            for k in range(start, start + PANEL)
        ]
        for j in range(PANEL):
            k = start + j
            over = 1.0 / panel[j][k : k + 1, :]
            scale = jnp.where(rows == k, over, scale)
            factor = jnp.where(rows > k, panel[j] * over, 0.0)
            work = work - factor * work[k : k + 1, :]
            for later in range(j + 1, PANEL):
                panel[later] = panel[later] - factor * panel[later][k : k + 1, :]
    out_ref[...] = (work * jnp.sqrt(scale))[:, rank : 2 * rank]


def inverse_factor(chunk, start):
    rank = chunk.shape[0]
    return pl.pallas_call(
        inverse_kernel,
        grid=(1,),
        in_specs=[pl.BlockSpec((rank, LANES), lambda i: (0, start // LANES))],
        out_specs=pl.BlockSpec((rank, rank), lambda i: (0, 0)),
        out_shape=jax.ShapeDtypeStruct((rank, rank), F32),
        compiler_params=PARAMS,
        cost_estimate=pl.CostEstimate(
            flops=20_000_000, bytes_accessed=8 * rank * LANES, transcendentals=rank
        ),
        name="inverse_factor",
    )(chunk)


def finish_kernel(plan, where_ref, inverse_ref, *refs):
    out_hbm, buf, sems = refs[-3:]
    _, rank, width = buf.shape
    head, rest = split(inverse_ref[...])
    both = jnp.concatenate([head, rest], axis=0)
    copies = []
    for k, (source, offset) in enumerate(plan):
        p_head, p_rest = split(refs[source][:, offset : offset + width])
        first = dot(both, p_head, PLAIN)
        buf[k] = first[:rank] + (first[rank:] + dot(head, p_rest, PLAIN))
        where = pl.ds(pl.multiple_of(where_ref[k] * width, width), width)
        copies.append(pltpu.make_async_copy(buf.at[k], out_hbm.at[:, where], sems.at[k]))
        copies[k].start()
    for copy in copies:
        copy.wait()


def finish(inverse, sources, pieces, width, total, before=None):
    rank = inverse.shape[0]
    count = len(pieces)
    in_specs = [TABLE, WHOLE, *[WHOLE] * len(sources)]
    args = [jnp.stack([piece[0] for piece in pieces]), inverse, *sources]
    aliases = {}
    if before is not None:
        in_specs.append(HBM)
        args.append(before)
        aliases = {len(args) - 1: 0}
    return pl.pallas_call(
        functools.partial(finish_kernel, [piece[1:] for piece in pieces]),
        in_specs=in_specs,
        out_specs=HBM,
        out_shape=jax.ShapeDtypeStruct((rank, total), F32),
        scratch_shapes=[
            pltpu.VMEM((count, rank, width), F32),
            pltpu.SemaphoreType.DMA((count,)),
        ],
        input_output_aliases=aliases,
        compiler_params=PARAMS,
        cost_estimate=pl.CostEstimate(
            flops=6 * rank * rank * width * count,
            bytes_accessed=8 * rank * width * count,
            transcendentals=0,
        ),
        name="finish",
    )(*args)


def body(n_pos, n_pix, probes, sketch):
    def swap(value, axis, size, bit):
        return lax.ppermute(value, axis, [(i, i ^ bit) for i in range(size)])

    def over(value, bit):
        return swap(value, "pos", n_pos, bit)

    me = lax.axis_index("pos").astype(jnp.int32)
    near, far = me & 1, (me >> 1) & 1
    cols = probes.shape[1]
    width = cols // (8 * CHUNKS)

    tall = tall_partial(probes, sketch.T)
    bit = 1
    while 2 * bit < n_pix:
        tall = tall + swap(tall, "pix", n_pix, bit)
        bit *= 2
    other = swap(tall, "pix", n_pix, bit)

    def block_a(c, p, q):
        return 8 * c + 2 * (near ^ p) + (far ^ q)

    def block_b(c, p, q):
        return 8 * c + 4 + 2 * (far ^ p) + (near ^ q)

    def outputs(c, p):
        return [
            ([block_a(c, p, 1), block_a(c, p, 0)], c == 0),
            ([block_b(c, p, 1), block_b(c, p, 0)], False),
        ]

    both, gram, away = first_products(tall, other, probes, outputs(0, 1), width)

    plan = [(c, p) for c in range(CHUNKS) for p in (1, 0) if (c, p) != (0, 1)]
    rest = rest_products(
        both, gram, probes, [out for c, p in plan for out in outputs(c, p)], width, away[0]
    )
    made = {(0, 1): away}
    made.update({key: rest[2 * k : 2 * k + 2] for k, key in enumerate(plan)})

    inverse, out, after = None, None, None
    for c in range(CHUNKS):
        g = LANES if c == 0 else 0
        last = c == CHUNKS - 1
        away_a, away_b = made[c, 1]
        own_a, own_b = made[c, 0]
        if c > 0:
            own_a, own_b = hold([own_a, own_b], after, 6 * probes.shape[0] * width * 4 * own_a.shape[0])
        got_a = over(away_a, 1)
        sum_a = own_a + got_a
        sum_b = own_b + over(away_b, 2)
        after = got_a
        send_a, send_b = sum_a[:, : width + g], sum_b[:, :width]
        if c > 0:
            send_a, send_b, whole = lax.optimization_barrier((send_a, send_b, whole))
        got_a = over(send_a, 2)
        got_b = over(send_b, 1)
        whole = jnp.concatenate(
            [
                sum_a[:, width + g :] + got_a[:, :width],
                sum_a[:, width : width + g] + got_a[:, width:],
                sum_b[:, width:] + got_b,
            ],
            axis=1,
        )
        total = whole
        bit = 4
        while bit < n_pos:
            total = total + over(total, bit)
            bit *= 2
        if c == 0:
            inverse = inverse_factor(total, width)
        mine_a, mine_b = total[:, :width], total[:, width + g :]
        if c > 0:
            mine_a, mine_b, inverse = lax.optimization_barrier((mine_a, mine_b, inverse))
        next_a = over(mine_a, 2)
        next_b = over(mine_b, 1)
        last_a = over(jnp.concatenate([mine_a, next_a], axis=1), 1)
        last_b = over(jnp.concatenate([mine_b, next_b], axis=1), 2)
        sources = [total, next_a, next_b]
        pieces = [
            (block_a(c, 0, 0), 0, 0),
            (block_b(c, 0, 0), 0, width + g),
            (block_a(c, 0, 1), 1, 0),
            (block_b(c, 0, 1), 2, 0),
        ]
        if last:
            out = finish(inverse, sources, pieces, width, cols, out)
            sources, pieces = [], []
        k = len(sources)
        sources += [last_a, last_b]
        pieces += [
            (block_a(c, 1, 0), k, 0),
            (block_a(c, 1, 1), k, width),
            (block_b(c, 1, 0), k + 1, 0),
            (block_b(c, 1, 1), k + 1, width),
        ]
        out = finish(inverse, sources, pieces, width, cols, out)
    return out


def solution(mesh):
    in_specs = (P("pos", "pix"), P("pix", None))
    out_specs = P(None, "pix")
    run = functools.partial(body, mesh.shape["pos"], mesh.shape["pix"])
    return jax.shard_map(run, mesh=mesh, in_specs=in_specs, out_specs=out_specs, check_vma=False)
```

```python
import functools

import jax
import jax.numpy as jnp
from jax import lax
from jax.experimental import pallas as pl
from jax.experimental.pallas import tpu as pltpu
from jax.sharding import PartitionSpec as P

F32 = jnp.float32
BF16 = jnp.bfloat16
VMEM_LIMIT = 40 * 1024 * 1024
LANES = 128
CHUNKS = 2
AHEAD = 6
UNIT = 512
PANEL = 4
LAST = (((1,), (1,)), ((), ()))
PLAIN = (((1,), (0,)), ((), ()))
ANYWHERE = pl.BlockSpec(memory_space=pl.ANY)
HBM = pl.BlockSpec(memory_space=pltpu.MemorySpace.HBM)
WHOLE = pl.BlockSpec(memory_space=pltpu.VMEM)
TABLE = pl.BlockSpec(memory_space=pltpu.SMEM)
PARAMS = pltpu.CompilerParams(vmem_limit_bytes=VMEM_LIMIT)


def split(x):
    head = x.astype(BF16)
    return head, (x - head.astype(F32)).astype(BF16)


def dot(a, b, dims):
    return lax.dot_general(a, b, dims, preferred_element_type=F32)


def in_hbm(x):
    return pltpu.with_memory_space_constraint(x, pltpu.MemorySpace.HBM)


def stream(copies, use):
    for copy in copies[:AHEAD]:
        copy.start()
    for k, copy in enumerate(copies):
        copy.wait()
        if k + AHEAD < len(copies):
            copies[k + AHEAD].start()
        use(k)


def tall_kernel(x_hbm, s_hbm, out_ref, x_buf, s_buf, head_buf, rest_buf, x_sems, s_sems):
    blocks, _, unit = x_buf.shape
    rank = s_hbm.shape[0]

    def copies(k):
        where = pl.ds(k * unit, unit)
        return (
            pltpu.make_async_copy(s_hbm.at[:, where], s_buf.at[k], s_sems.at[k]),
            pltpu.make_async_copy(x_hbm.at[:, where], x_buf.at[k], x_sems.at[k]),
        )

    for k in range(blocks):
        for copy in copies(k):
            copy.start()
    for k in range(blocks):
        for copy in copies(k):
            copy.wait()
        s_head, s_rest = split(s_buf[k])
        s_both = jnp.concatenate([s_head, s_rest], axis=0)
        x_head, x_rest = split(x_buf[k])
        head_buf[k] = x_head
        rest_buf[k] = x_rest
        both = dot(s_both, x_head, LAST)
        part = both[:rank] + (both[rank:] + dot(s_head, x_rest, LAST))
        if k == 0:
            out_ref[...] = part
        else:
            out_ref[...] += part


def tall_partial(probes, sketch_t):
    rows, cols = probes.shape
    rank = sketch_t.shape[0]
    unit = min(2 * UNIT, cols)
    blocks = cols // unit
    return pl.pallas_call(
        tall_kernel,
        in_specs=[HBM, HBM],
        out_specs=WHOLE,
        out_shape=jax.ShapeDtypeStruct((rank, rows), F32),
        scratch_shapes=[
            pltpu.VMEM((blocks, rows, unit), F32),
            pltpu.VMEM((blocks, rank, unit), F32),
            pltpu.VMEM((blocks, rows, unit), BF16),
            pltpu.VMEM((blocks, rows, unit), BF16),
            pltpu.SemaphoreType.DMA((blocks,)),
            pltpu.SemaphoreType.DMA((blocks,)),
        ],
        compiler_params=PARAMS,
        cost_estimate=pl.CostEstimate(
            flops=6 * rows * cols * rank, bytes_accessed=4 * rows * cols, transcendentals=0
        ),
        name="tall_partial",
    )(in_hbm(probes), in_hbm(sketch_t))


def multiply_blocks(both_ref, which_ref, x_hbm, x_buf, sems, plan, outs):
    rank = outs[0].shape[0]
    unit = x_buf.shape[2]
    copies = [
        pltpu.make_async_copy(
            x_hbm.at[:, pl.ds(pl.multiple_of(which_ref[k] * unit, unit), unit)],
            x_buf.at[k],
            sems.at[k],
        )
        for k in range(len(plan))
    ]

    def use(k):
        both = both_ref[...]
        x_head, x_rest = split(x_buf[k])
        first = dot(both, x_head, PLAIN)
        second = dot(both[:rank], x_rest, PLAIN)
        out, offset = plan[k]
        outs[out][:, offset : offset + unit] = first[:rank] + (first[rank:] + second)

    return copies, use


def first_kernel(plan, grams, which_ref, one_ref, two_ref, x_hbm, both_ref, gram_ref, *refs):
    outs, (x_buf, sems) = refs[:-2], refs[-2:]
    copies, use = multiply_blocks(both_ref, which_ref, x_hbm, x_buf, sems, plan, outs)

    def use_first(k):
        if k == 0:
            tall = one_ref[...] + two_ref[...]
            head, rest = split(tall)
            both_ref[...] = jnp.concatenate([head, rest], axis=0)
        use(k)

    stream(copies, use_first)
    tall = one_ref[...] + two_ref[...]
    r = tall.shape[0]
    head, rest = split(tall)
    tail = (tall - head.astype(F32) - rest.astype(F32)).astype(BF16)
    three = jnp.concatenate([head, rest, tail], axis=0)
    g = dot(three, three, LAST)
    cross = g[:r, r : 2 * r] + g[r : 2 * r, :r]
    small = g[:r, 2 * r :] + g[2 * r :, :r] + g[r : 2 * r, r : 2 * r]
    gram = g[:r, :r] + (cross + small)
    gram_ref[...] = jnp.concatenate([gram, jnp.zeros((r, LANES - r), F32)], axis=1)
    for out, offset in grams:
        outs[out][:, offset : offset + LANES] = gram_ref[...]


def rest_kernel(plan, grams, which_ref, both_ref, gram_ref, x_hbm, after_ref, *refs):
    outs, (x_buf, sems) = refs[:-2], refs[-2:]
    copies, use = multiply_blocks(both_ref, which_ref, x_hbm, x_buf, sems, plan, outs)
    stream(copies, use)
    for out, offset in grams:
        outs[out][:, offset : offset + LANES] = gram_ref[...]


def layout(outputs, sub):
    unit = min(UNIT, sub)
    plan, grams, widths, which = [], [], [], []
    for out, (blocks, with_gram) in enumerate(outputs):
        extra = LANES if with_gram else 0
        for j, block in enumerate(blocks):
            for part in range(sub // unit):
                plan.append((out, j * sub + part * unit + (extra if j else 0)))
                which.append(block * (sub // unit) + part)
        if with_gram:
            grams.append((out, sub))
        widths.append(len(blocks) * sub + extra)
    return unit, plan, grams, widths, jnp.stack(which)


def products(kernel, inputs, in_specs, made, probes, outputs, sub, name):
    rows = probes.shape[0]
    rank = inputs[1].shape[0]
    unit, plan, grams, widths, which = layout(outputs, sub)
    shapes = [*made, *[jax.ShapeDtypeStruct((rank, width), F32) for width in widths]]
    return pl.pallas_call(
        functools.partial(kernel, plan, grams),
        in_specs=[TABLE, *in_specs],
        out_specs=[WHOLE] * len(shapes),
        out_shape=shapes,
        scratch_shapes=[
            pltpu.VMEM((len(plan), rows, unit), F32),
            pltpu.SemaphoreType.DMA((len(plan),)),
        ],
        compiler_params=PARAMS,
        cost_estimate=pl.CostEstimate(
            flops=6 * rows * rank * unit * len(plan),
            bytes_accessed=4 * rows * unit * len(plan),
            transcendentals=0,
        ),
        name=name,
    )(which, *inputs)


def first_products(one, two, probes, outputs, sub):
    rank, rows = one.shape
    made = [
        jax.ShapeDtypeStruct((2 * rank, rows), BF16),
        jax.ShapeDtypeStruct((rank, LANES), F32),
    ]
    both, gram, *outs = products(
        first_kernel,
        [one, two, in_hbm(probes)],
        [WHOLE, WHOLE, HBM],
        made,
        probes,
        outputs,
        sub,
        "first_products",
    )
    return both, gram, outs


def rest_products(both, gram, probes, outputs, sub, after):
    return products(
        rest_kernel,
        [both, gram, in_hbm(probes), after],
        [WHOLE, WHOLE, HBM, ANYWHERE],
        [],
        probes,
        outputs,
        sub,
        "rest_products",
    )


def hold_kernel(count, *refs):
    for k in range(count):
        refs[count + 1 + k][...] = refs[k][...]


def hold(arrays, after, flops):
    count = len(arrays)
    return pl.pallas_call(
        functools.partial(hold_kernel, count),
        in_specs=[WHOLE] * count + [ANYWHERE],
        out_specs=[WHOLE] * count,
        out_shape=[jax.ShapeDtypeStruct(array.shape, array.dtype) for array in arrays],
        compiler_params=PARAMS,
        cost_estimate=pl.CostEstimate(flops=flops, bytes_accessed=0, transcendentals=0),
        name="hold",
    )(*arrays, after)


def inverse_kernel(gram_ref, out_ref):
    rank = out_ref.shape[0]
    rows = lax.broadcasted_iota(jnp.int32, (rank, LANES), 0)
    cols = lax.broadcasted_iota(jnp.int32, (rank, LANES), 1)
    work = jnp.where(cols < rank, gram_ref[...], (cols == rows + rank).astype(F32))
    scale = jnp.ones((rank, LANES), F32)
    for start in range(0, rank, PANEL):
        panel = [
            jnp.broadcast_to(work[:, k : k + 1], (rank, LANES))
            for k in range(start, start + PANEL)
        ]
        for j in range(PANEL):
            k = start + j
            over = 1.0 / panel[j][k : k + 1, :]
            scale = jnp.where(rows == k, over, scale)
            factor = jnp.where(rows > k, panel[j] * over, 0.0)
            work = work - factor * work[k : k + 1, :]
            for later in range(j + 1, PANEL):
                panel[later] = panel[later] - factor * panel[later][k : k + 1, :]
    out_ref[...] = (work * jnp.sqrt(scale))[:, rank : 2 * rank]


def inverse_factor(chunk, start):
    rank = chunk.shape[0]
    return pl.pallas_call(
        inverse_kernel,
        grid=(1,),
        in_specs=[pl.BlockSpec((rank, LANES), lambda i: (0, start // LANES))],
        out_specs=pl.BlockSpec((rank, rank), lambda i: (0, 0)),
        out_shape=jax.ShapeDtypeStruct((rank, rank), F32),
        compiler_params=PARAMS,
        cost_estimate=pl.CostEstimate(
            flops=20_000_000, bytes_accessed=8 * rank * LANES, transcendentals=rank
        ),
        name="inverse_factor",
    )(chunk)


def finish_kernel(plan, where_ref, inverse_ref, *refs):
    out_hbm, buf, sems = refs[-3:]
    _, rank, width = buf.shape
    head, rest = split(inverse_ref[...])
    both = jnp.concatenate([head, rest], axis=0)
    copies = []
    for k, (source, offset) in enumerate(plan):
        p_head, p_rest = split(refs[source][:, offset : offset + width])
        first = dot(both, p_head, PLAIN)
        buf[k] = first[:rank] + (first[rank:] + dot(head, p_rest, PLAIN))
        where = pl.ds(pl.multiple_of(where_ref[k] * width, width), width)
        copies.append(pltpu.make_async_copy(buf.at[k], out_hbm.at[:, where], sems.at[k]))
        copies[k].start()
    for copy in copies:
        copy.wait()


def finish(inverse, sources, pieces, width, total, before=None):
    rank = inverse.shape[0]
    count = len(pieces)
    in_specs = [TABLE, WHOLE, *[WHOLE] * len(sources)]
    args = [jnp.stack([piece[0] for piece in pieces]), inverse, *sources]
    aliases = {}
    if before is not None:
        in_specs.append(HBM)
        args.append(before)
        aliases = {len(args) - 1: 0}
    return pl.pallas_call(
        functools.partial(finish_kernel, [piece[1:] for piece in pieces]),
        in_specs=in_specs,
        out_specs=HBM,
        out_shape=jax.ShapeDtypeStruct((rank, total), F32),
        scratch_shapes=[
            pltpu.VMEM((count, rank, width), F32),
            pltpu.SemaphoreType.DMA((count,)),
        ],
        input_output_aliases=aliases,
        compiler_params=PARAMS,
        cost_estimate=pl.CostEstimate(
            flops=6 * rank * rank * width * count,
            bytes_accessed=8 * rank * width * count,
            transcendentals=0,
        ),
        name="finish",
    )(*args)


def body(n_pos, n_pix, probes, sketch):
    def swap(value, axis, size, bit):
        return lax.ppermute(value, axis, [(i, i ^ bit) for i in range(size)])

    def over(value, bit):
        return swap(value, "pos", n_pos, bit)

    me = lax.axis_index("pos").astype(jnp.int32)
    near, far = me & 1, (me >> 1) & 1
    cols = probes.shape[1]
    width = cols // (8 * CHUNKS)

    tall = tall_partial(probes, sketch.T)
    bit = 1
    while 2 * bit < n_pix:
        tall = tall + swap(tall, "pix", n_pix, bit)
        bit *= 2
    other = swap(tall, "pix", n_pix, bit)

    def block_a(c, p, q):
        return 8 * c + 2 * (near ^ p) + (far ^ q)

    def block_b(c, p, q):
        return 8 * c + 4 + 2 * (far ^ p) + (near ^ q)

    def outputs(c, p):
        return [
            ([block_a(c, p, 1), block_a(c, p, 0)], c == 0),
            ([block_b(c, p, 1), block_b(c, p, 0)], False),
        ]

    both, gram, away = first_products(tall, other, probes, outputs(0, 1), width)

    plan = [(c, p) for c in range(CHUNKS) for p in (1, 0) if (c, p) != (0, 1)]
    rest = rest_products(
        both, gram, probes, [out for c, p in plan for out in outputs(c, p)], width, away[0]
    )
    made = {(0, 1): away}
    made.update({key: rest[2 * k : 2 * k + 2] for k, key in enumerate(plan)})

    inverse, out, after = None, None, None
    for c in range(CHUNKS):
        g = LANES if c == 0 else 0
        last = c == CHUNKS - 1
        away_a, away_b = made[c, 1]
        own_a, own_b = made[c, 0]
        if c > 0:
            own_a, own_b = hold([own_a, own_b], after, 6 * probes.shape[0] * width * 4 * own_a.shape[0])
        got_a = over(away_a, 1)
        sum_a = own_a + got_a
        sum_b = own_b + over(away_b, 2)
        after = got_a
        send_a, send_b = sum_a[:, : width + g], sum_b[:, :width]
        if c > 0:
            send_a, send_b, whole = lax.optimization_barrier((send_a, send_b, whole))
        got_a = over(send_a, 2)
        got_b = over(send_b, 1)
        whole = jnp.concatenate(
            [
                sum_a[:, width + g :] + got_a[:, :width],
                sum_a[:, width : width + g] + got_a[:, width:],
                sum_b[:, width:] + got_b,
            ],
            axis=1,
        )
        total = whole
        bit = 4
        while bit < n_pos:
            total = total + over(total, bit)
            bit *= 2
        if c == 0:
            inverse = inverse_factor(total, width)
        mine_a, mine_b = total[:, :width], total[:, width + g :]
        if c > 0:
            mine_a, mine_b, inverse = lax.optimization_barrier((mine_a, mine_b, inverse))
        next_a = over(mine_a, 2)
        next_b = over(mine_b, 1)
        last_a = over(jnp.concatenate([mine_a, next_a], axis=1), 1)
        last_b = over(jnp.concatenate([mine_b, next_b], axis=1), 2)
        sources = [total, next_a, next_b]
        pieces = [
            (block_a(c, 0, 0), 0, 0),
            (block_b(c, 0, 0), 0, width + g),
            (block_a(c, 0, 1), 1, 0),
            (block_b(c, 0, 1), 2, 0),
        ]
        if last:
            out = finish(inverse, sources, pieces, width, cols, out)
            sources, pieces = [], []
        k = len(sources)
        sources += [last_a, last_b]
        pieces += [
            (block_a(c, 1, 0), k, 0),
            (block_a(c, 1, 1), k, width),
            (block_b(c, 1, 0), k + 1, 0),
            (block_b(c, 1, 1), k + 1, width),
        ]
        out = finish(inverse, sources, pieces, width, cols, out)
    return out


def solution(mesh):
    in_specs = (P("pos", "pix"), P("pix", None))
    out_specs = P(None, "pix")
    run = functools.partial(body, mesh.shape["pos"], mesh.shape["pix"])
    return jax.shard_map(run, mesh=mesh, in_specs=in_specs, out_specs=out_specs, check_vma=False)
```

```python
import functools

import jax
import jax.numpy as jnp
from jax import lax
from jax.experimental import pallas as pl
from jax.experimental.pallas import tpu as pltpu
from jax.sharding import PartitionSpec as P

F32 = jnp.float32
BF16 = jnp.bfloat16
VMEM_LIMIT = 40 * 1024 * 1024
LANES = 128
CHUNKS = 2
AHEAD = 6
UNIT = 512
PANEL = 4
LAST = (((1,), (1,)), ((), ()))
PLAIN = (((1,), (0,)), ((), ()))
ANYWHERE = pl.BlockSpec(memory_space=pl.ANY)
HBM = pl.BlockSpec(memory_space=pltpu.MemorySpace.HBM)
WHOLE = pl.BlockSpec(memory_space=pltpu.VMEM)
TABLE = pl.BlockSpec(memory_space=pltpu.SMEM)
PARAMS = pltpu.CompilerParams(vmem_limit_bytes=VMEM_LIMIT)


def split(x):
    head = x.astype(BF16)
    return head, (x - head.astype(F32)).astype(BF16)


def dot(a, b, dims):
    return lax.dot_general(a, b, dims, preferred_element_type=F32)


def in_hbm(x):
    return pltpu.with_memory_space_constraint(x, pltpu.MemorySpace.HBM)


def stream(copies, use):
    for copy in copies[:AHEAD]:
        copy.start()
    for k, copy in enumerate(copies):
        copy.wait()
        if k + AHEAD < len(copies):
            copies[k + AHEAD].start()
        use(k)


def tall_kernel(x_hbm, s_hbm, out_ref, x_buf, s_buf, head_buf, rest_buf, x_sems, s_sems):
    blocks, _, unit = x_buf.shape
    rank = s_hbm.shape[0]

    def copies(k):
        where = pl.ds(k * unit, unit)
        return (
            pltpu.make_async_copy(s_hbm.at[:, where], s_buf.at[k], s_sems.at[k]),
            pltpu.make_async_copy(x_hbm.at[:, where], x_buf.at[k], x_sems.at[k]),
        )

    for k in range(blocks):
        for copy in copies(k):
            copy.start()
    for k in range(blocks):
        for copy in copies(k):
            copy.wait()
        s_head, s_rest = split(s_buf[k])
        s_both = jnp.concatenate([s_head, s_rest], axis=0)
        x_head, x_rest = split(x_buf[k])
        head_buf[k] = x_head
        rest_buf[k] = x_rest
        both = dot(s_both, x_head, LAST)
        part = both[:rank] + (both[rank:] + dot(s_head, x_rest, LAST))
        if k == 0:
            out_ref[...] = part
        else:
            out_ref[...] += part


def tall_partial(probes, sketch_t):
    rows, cols = probes.shape
    rank = sketch_t.shape[0]
    unit = min(2 * UNIT, cols)
    blocks = cols // unit
    return pl.pallas_call(
        tall_kernel,
        in_specs=[HBM, HBM],
        out_specs=WHOLE,
        out_shape=jax.ShapeDtypeStruct((rank, rows), F32),
        scratch_shapes=[
            pltpu.VMEM((blocks, rows, unit), F32),
            pltpu.VMEM((blocks, rank, unit), F32),
            pltpu.VMEM((blocks, rows, unit), BF16),
            pltpu.VMEM((blocks, rows, unit), BF16),
            pltpu.SemaphoreType.DMA((blocks,)),
            pltpu.SemaphoreType.DMA((blocks,)),
        ],
        compiler_params=PARAMS,
        cost_estimate=pl.CostEstimate(
            flops=6 * rows * cols * rank, bytes_accessed=4 * rows * cols, transcendentals=0
        ),
        name="tall_partial",
    )(in_hbm(probes), in_hbm(sketch_t))


def multiply_blocks(both_ref, which_ref, x_hbm, x_buf, sems, plan, outs):
    rank = outs[0].shape[0]
    unit = x_buf.shape[2]
    copies = [
        pltpu.make_async_copy(
            x_hbm.at[:, pl.ds(pl.multiple_of(which_ref[k] * unit, unit), unit)],
            x_buf.at[k],
            sems.at[k],
        )
        for k in range(len(plan))
    ]

    def use(k):
        both = both_ref[...]
        x_head, x_rest = split(x_buf[k])
        first = dot(both, x_head, PLAIN)
        second = dot(both[:rank], x_rest, PLAIN)
        out, offset = plan[k]
        outs[out][:, offset : offset + unit] = first[:rank] + (first[rank:] + second)

    return copies, use


def first_kernel(plan, grams, which_ref, one_ref, two_ref, x_hbm, both_ref, gram_ref, *refs):
    outs, (x_buf, sems) = refs[:-2], refs[-2:]
    copies, use = multiply_blocks(both_ref, which_ref, x_hbm, x_buf, sems, plan, outs)

    def use_first(k):
        if k == 0:
            tall = one_ref[...] + two_ref[...]
            head, rest = split(tall)
            both_ref[...] = jnp.concatenate([head, rest], axis=0)
        use(k)

    stream(copies, use_first)
    tall = one_ref[...] + two_ref[...]
    r = tall.shape[0]
    head, rest = split(tall)
    tail = (tall - head.astype(F32) - rest.astype(F32)).astype(BF16)
    three = jnp.concatenate([head, rest, tail], axis=0)
    g = dot(three, three, LAST)
    cross = g[:r, r : 2 * r] + g[r : 2 * r, :r]
    small = g[:r, 2 * r :] + g[2 * r :, :r] + g[r : 2 * r, r : 2 * r]
    gram = g[:r, :r] + (cross + small)
    gram_ref[...] = jnp.concatenate([gram, jnp.zeros((r, LANES - r), F32)], axis=1)
    for out, offset in grams:
        outs[out][:, offset : offset + LANES] = gram_ref[...]


def rest_kernel(plan, grams, which_ref, both_ref, gram_ref, x_hbm, after_ref, *refs):
    outs, (x_buf, sems) = refs[:-2], refs[-2:]
    copies, use = multiply_blocks(both_ref, which_ref, x_hbm, x_buf, sems, plan, outs)
    stream(copies, use)
    for out, offset in grams:
        outs[out][:, offset : offset + LANES] = gram_ref[...]


def layout(outputs, sub):
    unit = min(UNIT, sub)
    plan, grams, widths, which = [], [], [], []
    for out, (blocks, with_gram) in enumerate(outputs):
        extra = LANES if with_gram else 0
        for j, block in enumerate(blocks):
            for part in range(sub // unit):
                plan.append((out, j * sub + part * unit + (extra if j else 0)))
                which.append(block * (sub // unit) + part)
        if with_gram:
            grams.append((out, sub))
        widths.append(len(blocks) * sub + extra)
    return unit, plan, grams, widths, jnp.stack(which)


def products(kernel, inputs, in_specs, made, probes, outputs, sub, name):
    rows = probes.shape[0]
    rank = inputs[1].shape[0]
    unit, plan, grams, widths, which = layout(outputs, sub)
    shapes = [*made, *[jax.ShapeDtypeStruct((rank, width), F32) for width in widths]]
    return pl.pallas_call(
        functools.partial(kernel, plan, grams),
        in_specs=[TABLE, *in_specs],
        out_specs=[WHOLE] * len(shapes),
        out_shape=shapes,
        scratch_shapes=[
            pltpu.VMEM((len(plan), rows, unit), F32),
            pltpu.SemaphoreType.DMA((len(plan),)),
        ],
        compiler_params=PARAMS,
        cost_estimate=pl.CostEstimate(
            flops=6 * rows * rank * unit * len(plan),
            bytes_accessed=4 * rows * unit * len(plan),
            transcendentals=0,
        ),
        name=name,
    )(which, *inputs)


def first_products(one, two, probes, outputs, sub):
    rank, rows = one.shape
    made = [
        jax.ShapeDtypeStruct((2 * rank, rows), BF16),
        jax.ShapeDtypeStruct((rank, LANES), F32),
    ]
    both, gram, *outs = products(
        first_kernel,
        [one, two, in_hbm(probes)],
        [WHOLE, WHOLE, HBM],
        made,
        probes,
        outputs,
        sub,
        "first_products",
    )
    return both, gram, outs


def rest_products(both, gram, probes, outputs, sub, after):
    return products(
        rest_kernel,
        [both, gram, in_hbm(probes), after],
        [WHOLE, WHOLE, HBM, ANYWHERE],
        [],
        probes,
        outputs,
        sub,
        "rest_products",
    )


def inverse_kernel(gram_ref, out_ref):
    rank = out_ref.shape[0]
    rows = lax.broadcasted_iota(jnp.int32, (rank, LANES), 0)
    cols = lax.broadcasted_iota(jnp.int32, (rank, LANES), 1)
    work = jnp.where(cols < rank, gram_ref[...], (cols == rows + rank).astype(F32))
    scale = jnp.ones((rank, LANES), F32)
    for start in range(0, rank, PANEL):
        panel = [
            jnp.broadcast_to(work[:, k : k + 1], (rank, LANES))
            for k in range(start, start + PANEL)
        ]
        for j in range(PANEL):
            k = start + j
            over = 1.0 / panel[j][k : k + 1, :]
            scale = jnp.where(rows == k, over, scale)
            factor = jnp.where(rows > k, panel[j] * over, 0.0)
            work = work - factor * work[k : k + 1, :]
            for later in range(j + 1, PANEL):
                panel[later] = panel[later] - factor * panel[later][k : k + 1, :]
    out_ref[...] = (work * jnp.sqrt(scale))[:, rank : 2 * rank]


def inverse_factor(chunk, start):
    rank = chunk.shape[0]
    return pl.pallas_call(
        inverse_kernel,
        grid=(1,),
        in_specs=[pl.BlockSpec((rank, LANES), lambda i: (0, start // LANES))],
        out_specs=pl.BlockSpec((rank, rank), lambda i: (0, 0)),
        out_shape=jax.ShapeDtypeStruct((rank, rank), F32),
        compiler_params=PARAMS,
        cost_estimate=pl.CostEstimate(
            flops=20_000_000, bytes_accessed=8 * rank * LANES, transcendentals=rank
        ),
        name="inverse_factor",
    )(chunk)


def finish_kernel(plan, where_ref, inverse_ref, *refs):
    out_hbm, buf, sems = refs[-3:]
    _, rank, width = buf.shape
    head, rest = split(inverse_ref[...])
    both = jnp.concatenate([head, rest], axis=0)
    copies = []
    for k, (source, offset) in enumerate(plan):
        p_head, p_rest = split(refs[source][:, offset : offset + width])
        first = dot(both, p_head, PLAIN)
        buf[k] = first[:rank] + (first[rank:] + dot(head, p_rest, PLAIN))
        where = pl.ds(pl.multiple_of(where_ref[k] * width, width), width)
        copies.append(pltpu.make_async_copy(buf.at[k], out_hbm.at[:, where], sems.at[k]))
        copies[k].start()
    for copy in copies:
        copy.wait()


def finish(inverse, sources, pieces, width, total, before=None):
    rank = inverse.shape[0]
    count = len(pieces)
    in_specs = [TABLE, WHOLE, *[WHOLE] * len(sources)]
    args = [jnp.stack([piece[0] for piece in pieces]), inverse, *sources]
    aliases = {}
    if before is not None:
        in_specs.append(HBM)
        args.append(before)
        aliases = {len(args) - 1: 0}
    return pl.pallas_call(
        functools.partial(finish_kernel, [piece[1:] for piece in pieces]),
        in_specs=in_specs,
        out_specs=HBM,
        out_shape=jax.ShapeDtypeStruct((rank, total), F32),
        scratch_shapes=[
            pltpu.VMEM((count, rank, width), F32),
            pltpu.SemaphoreType.DMA((count,)),
        ],
        input_output_aliases=aliases,
        compiler_params=PARAMS,
        cost_estimate=pl.CostEstimate(
            flops=6 * rank * rank * width * count,
            bytes_accessed=8 * rank * width * count,
            transcendentals=0,
        ),
        name="finish",
    )(*args)


def body(n_pos, n_pix, probes, sketch):
    def swap(value, axis, size, bit):
        return lax.ppermute(value, axis, [(i, i ^ bit) for i in range(size)])

    def over(value, bit):
        return swap(value, "pos", n_pos, bit)

    me = lax.axis_index("pos").astype(jnp.int32)
    near, far = me & 1, (me >> 1) & 1
    cols = probes.shape[1]
    width = cols // (8 * CHUNKS)

    tall = tall_partial(probes, sketch.T)
    bit = 1
    while 2 * bit < n_pix:
        tall = tall + swap(tall, "pix", n_pix, bit)
        bit *= 2
    other = swap(tall, "pix", n_pix, bit)

    def block_a(c, p, q):
        return 8 * c + 2 * (near ^ p) + (far ^ q)

    def block_b(c, p, q):
        return 8 * c + 4 + 2 * (far ^ p) + (near ^ q)

    def outputs(c, p):
        return [
            ([block_a(c, p, 1), block_a(c, p, 0)], c == 0),
            ([block_b(c, p, 1), block_b(c, p, 0)], False),
        ]

    both, gram, away = first_products(tall, other, probes, outputs(0, 1), width)

    aways = [away] + [
        rest_products(both, gram, probes, outputs(c, 1), width, away[0]) for c in range(1, CHUNKS)
    ]
    ready = over(away[0], 1)
    owns = rest_products(
        both, gram, probes, [o for c in range(CHUNKS) for o in outputs(c, 0)], width, ready
    )

    inverse, out = None, None
    for c in range(CHUNKS):
        g = LANES if c == 0 else 0
        last = c == CHUNKS - 1
        (away_a, away_b), (own_a, own_b) = aways[c], owns[2 * c : 2 * c + 2]
        got_a = ready if c == 0 else over(away_a, 1)
        sum_a = own_a + got_a
        sum_b = own_b + over(away_b, 2)
        send_a, send_b = sum_a[:, : width + g], sum_b[:, :width]
        if c > 0:
            send_a, send_b, whole = lax.optimization_barrier((send_a, send_b, whole))
        got_a = over(send_a, 2)
        got_b = over(send_b, 1)
        whole = jnp.concatenate(
            [
                sum_a[:, width + g :] + got_a[:, :width],
                sum_a[:, width : width + g] + got_a[:, width:],
                sum_b[:, width:] + got_b,
            ],
            axis=1,
        )
        total = whole
        bit = 4
        while bit < n_pos:
            total = total + over(total, bit)
            bit *= 2
        if c == 0:
            inverse = inverse_factor(total, width)
        mine_a, mine_b = total[:, :width], total[:, width + g :]
        if c > 0:
            mine_a, mine_b, inverse = lax.optimization_barrier((mine_a, mine_b, inverse))
        next_a = over(mine_a, 2)
        next_b = over(mine_b, 1)
        last_a = over(jnp.concatenate([mine_a, next_a], axis=1), 1)
        last_b = over(jnp.concatenate([mine_b, next_b], axis=1), 2)
        sources = [total, next_a, next_b]
        pieces = [
            (block_a(c, 0, 0), 0, 0),
            (block_b(c, 0, 0), 0, width + g),
            (block_a(c, 0, 1), 1, 0),
            (block_b(c, 0, 1), 2, 0),
        ]
        if last:
            out = finish(inverse, sources, pieces, width, cols, out)
            sources, pieces = [], []
        k = len(sources)
        sources += [last_a, last_b]
        pieces += [
            (block_a(c, 1, 0), k, 0),
            (block_a(c, 1, 1), k, width),
            (block_b(c, 1, 0), k + 1, 0),
            (block_b(c, 1, 1), k + 1, width),
        ]
        out = finish(inverse, sources, pieces, width, cols, out)
    return out


def solution(mesh):
    in_specs = (P("pos", "pix"), P("pix", None))
    out_specs = P(None, "pix")
    run = functools.partial(body, mesh.shape["pos"], mesh.shape["pix"])
    return jax.shard_map(run, mesh=mesh, in_specs=in_specs, out_specs=out_specs, check_vma=False)
```

```python
import functools

import jax
import jax.numpy as jnp
from jax import lax
from jax.experimental import pallas as pl
from jax.experimental.pallas import tpu as pltpu
from jax.sharding import PartitionSpec as P

F32 = jnp.float32
BF16 = jnp.bfloat16
VMEM_LIMIT = 40 * 1024 * 1024
LANES = 128
CHUNKS = 2
AHEAD = 8
UNIT = 512
TILE = 256
PANEL = 4
LAST = (((1,), (1,)), ((), ()))
PLAIN = (((1,), (0,)), ((), ()))
ANYWHERE = pl.BlockSpec(memory_space=pl.ANY)
HBM = pl.BlockSpec(memory_space=pltpu.MemorySpace.HBM)
WHOLE = pl.BlockSpec(memory_space=pltpu.VMEM)
TABLE = pl.BlockSpec(memory_space=pltpu.SMEM)
PARAMS = pltpu.CompilerParams(vmem_limit_bytes=VMEM_LIMIT)


def split(x):
    head = x.astype(BF16)
    return head, (x - head.astype(F32)).astype(BF16)


def dot(a, b, dims):
    return lax.dot_general(a, b, dims, preferred_element_type=F32)


def tiles(size):
    step = min(TILE, size)
    return [slice(start, start + step) for start in range(0, size, step)]


def in_hbm(x):
    return pltpu.with_memory_space_constraint(x, pltpu.MemorySpace.HBM)


def stream(copies, use):
    for copy in copies[:AHEAD]:
        copy.start()
    for k, copy in enumerate(copies):
        copy.wait()
        if k + AHEAD < len(copies):
            copies[k + AHEAD].start()
        use(k)


def tall_kernel(x_hbm, s_hbm, out_ref, x_buf, s_buf, head_buf, rest_buf, x_sems, s_sems):
    blocks, _, unit = x_buf.shape
    rank = s_hbm.shape[0]

    def copies(k):
        where = pl.ds(k * unit, unit)
        return (
            pltpu.make_async_copy(s_hbm.at[:, where], s_buf.at[k], s_sems.at[k]),
            pltpu.make_async_copy(x_hbm.at[:, where], x_buf.at[k], x_sems.at[k]),
        )

    for k in range(blocks):
        for copy in copies(k):
            copy.start()
    for k in range(blocks):
        for copy in copies(k):
            copy.wait()
        s_head, s_rest = split(s_buf[k])
        s_both = jnp.concatenate([s_head, s_rest], axis=0)
        x_head, x_rest = split(x_buf[k])
        head_buf[k] = x_head
        rest_buf[k] = x_rest
        both = dot(s_both, x_head, LAST)
        part = both[:rank] + (both[rank:] + dot(s_head, x_rest, LAST))
        if k == 0:
            out_ref[...] = part
        else:
            out_ref[...] += part


def tall_partial(probes, sketch_t):
    rows, cols = probes.shape
    rank = sketch_t.shape[0]
    unit = min(2 * UNIT, cols)
    blocks = cols // unit
    return pl.pallas_call(
        tall_kernel,
        in_specs=[HBM, HBM],
        out_specs=WHOLE,
        out_shape=jax.ShapeDtypeStruct((rank, rows), F32),
        scratch_shapes=[
            pltpu.VMEM((blocks, rows, unit), F32),
            pltpu.VMEM((blocks, rank, unit), F32),
            pltpu.VMEM((blocks, rows, unit), BF16),
            pltpu.VMEM((blocks, rows, unit), BF16),
            pltpu.SemaphoreType.DMA((blocks,)),
            pltpu.SemaphoreType.DMA((blocks,)),
        ],
        compiler_params=PARAMS,
        cost_estimate=pl.CostEstimate(
            flops=6 * rows * cols * rank, bytes_accessed=4 * rows * cols, transcendentals=0
        ),
        name="tall_partial",
    )(in_hbm(probes), in_hbm(sketch_t))


def multiply_blocks(both_ref, which_ref, x_hbm, x_buf, sems, plan, outs):
    rank = outs[0].shape[0]
    unit = x_buf.shape[2]
    copies = [
        pltpu.make_async_copy(
            x_hbm.at[:, pl.ds(pl.multiple_of(which_ref[k] * unit, unit), unit)],
            x_buf.at[k],
            sems.at[k],
        )
        for k in range(len(plan))
    ]

    def use(k):
        out, offset = plan[k]
        for cols in tiles(unit):
            total = None
            for rows in tiles(x_buf.shape[1]):
                x_head, x_rest = split(x_buf[k, rows, cols])
                both = dot(both_ref[:, rows], x_head, PLAIN)
                part = both[:rank] + (both[rank:] + dot(both_ref[:rank, rows], x_rest, PLAIN))
                total = part if total is None else total + part
            outs[out][:, offset + cols.start : offset + cols.stop] = total

    return copies, use


def first_kernel(plan, grams, which_ref, one_ref, two_ref, x_hbm, both_ref, gram_ref, *refs):
    outs, (x_buf, sems) = refs[:-2], refs[-2:]
    copies, use = multiply_blocks(both_ref, which_ref, x_hbm, x_buf, sems, plan, outs)

    def use_first(k):
        if k == 0:
            tall = one_ref[...] + two_ref[...]
            head, rest = split(tall)
            both_ref[...] = jnp.concatenate([head, rest], axis=0)
        use(k)

    stream(copies, use_first)
    tall = one_ref[...] + two_ref[...]
    r = tall.shape[0]
    head, rest = split(tall)
    tail = (tall - head.astype(F32) - rest.astype(F32)).astype(BF16)
    three = jnp.concatenate([head, rest, tail], axis=0)
    g = dot(three, three, LAST)
    cross = g[:r, r : 2 * r] + g[r : 2 * r, :r]
    small = g[:r, 2 * r :] + g[2 * r :, :r] + g[r : 2 * r, r : 2 * r]
    gram = g[:r, :r] + (cross + small)
    gram_ref[...] = jnp.concatenate([gram, jnp.zeros((r, LANES - r), F32)], axis=1)
    for out, offset in grams:
        outs[out][:, offset : offset + LANES] = gram_ref[...]


def rest_kernel(plan, grams, which_ref, both_ref, gram_ref, x_hbm, after_ref, *refs):
    outs, (x_buf, sems) = refs[:-2], refs[-2:]
    copies, use = multiply_blocks(both_ref, which_ref, x_hbm, x_buf, sems, plan, outs)
    stream(copies, use)
    for out, offset in grams:
        outs[out][:, offset : offset + LANES] = gram_ref[...]


def layout(outputs, sub):
    unit = min(UNIT, sub)
    plan, grams, widths, which = [], [], [], []
    for out, (blocks, with_gram) in enumerate(outputs):
        extra = LANES if with_gram else 0
        for j, block in enumerate(blocks):
            for part in range(sub // unit):
                plan.append((out, j * sub + part * unit + (extra if j else 0)))
                which.append(block * (sub // unit) + part)
        if with_gram:
            grams.append((out, sub))
        widths.append(len(blocks) * sub + extra)
    return unit, plan, grams, widths, jnp.stack(which)


def products(kernel, inputs, in_specs, made, probes, outputs, sub, name):
    rows = probes.shape[0]
    rank = inputs[1].shape[0]
    unit, plan, grams, widths, which = layout(outputs, sub)
    shapes = [*made, *[jax.ShapeDtypeStruct((rank, width), F32) for width in widths]]
    return pl.pallas_call(
        functools.partial(kernel, plan, grams),
        in_specs=[TABLE, *in_specs],
        out_specs=[WHOLE] * len(shapes),
        out_shape=shapes,
        scratch_shapes=[
            pltpu.VMEM((len(plan), rows, unit), F32),
            pltpu.SemaphoreType.DMA((len(plan),)),
        ],
        compiler_params=PARAMS,
        cost_estimate=pl.CostEstimate(
            flops=6 * rows * rank * unit * len(plan),
            bytes_accessed=4 * rows * unit * len(plan),
            transcendentals=0,
        ),
        name=name,
    )(which, *inputs)


def first_products(one, two, probes, outputs, sub):
    rank, rows = one.shape
    made = [
        jax.ShapeDtypeStruct((2 * rank, rows), BF16),
        jax.ShapeDtypeStruct((rank, LANES), F32),
    ]
    both, gram, *outs = products(
        first_kernel,
        [one, two, in_hbm(probes)],
        [WHOLE, WHOLE, HBM],
        made,
        probes,
        outputs,
        sub,
        "first_products",
    )
    return both, gram, outs


def rest_products(both, gram, probes, outputs, sub, after):
    return products(
        rest_kernel,
        [both, gram, in_hbm(probes), after],
        [WHOLE, WHOLE, HBM, ANYWHERE],
        [],
        probes,
        outputs,
        sub,
        "rest_products",
    )


def inverse_kernel(gram_ref, out_ref):
    rank = out_ref.shape[0]
    rows = lax.broadcasted_iota(jnp.int32, (rank, LANES), 0)
    cols = lax.broadcasted_iota(jnp.int32, (rank, LANES), 1)
    work = jnp.where(cols < rank, gram_ref[...], (cols == rows + rank).astype(F32))
    scale = jnp.ones((rank, LANES), F32)
    for start in range(0, rank, PANEL):
        panel = [
            jnp.broadcast_to(work[:, k : k + 1], (rank, LANES))
            for k in range(start, start + PANEL)
        ]
        for j in range(PANEL):
            k = start + j
            over = 1.0 / panel[j][k : k + 1, :]
            scale = jnp.where(rows == k, over, scale)
            factor = jnp.where(rows > k, panel[j] * over, 0.0)
            work = work - factor * work[k : k + 1, :]
            for later in range(j + 1, PANEL):
                panel[later] = panel[later] - factor * panel[later][k : k + 1, :]
    out_ref[...] = (work * jnp.sqrt(scale))[:, rank : 2 * rank]


def inverse_factor(chunk, start):
    rank = chunk.shape[0]
    return pl.pallas_call(
        inverse_kernel,
        grid=(1,),
        in_specs=[pl.BlockSpec((rank, LANES), lambda i: (0, start // LANES))],
        out_specs=pl.BlockSpec((rank, rank), lambda i: (0, 0)),
        out_shape=jax.ShapeDtypeStruct((rank, rank), F32),
        compiler_params=PARAMS,
        cost_estimate=pl.CostEstimate(
            flops=20_000_000, bytes_accessed=8 * rank * LANES, transcendentals=rank
        ),
        name="inverse_factor",
    )(chunk)


def finish_kernel(plan, where_ref, inverse_ref, *refs):
    out_hbm, buf, sems = refs[-3:]
    _, rank, width = buf.shape
    head, rest = split(inverse_ref[...])
    both = jnp.concatenate([head, rest], axis=0)
    copies = []
    for k, (source, offset) in enumerate(plan):
        p_head, p_rest = split(refs[source][:, offset : offset + width])
        first = dot(both, p_head, PLAIN)
        buf[k] = first[:rank] + (first[rank:] + dot(head, p_rest, PLAIN))
        where = pl.ds(pl.multiple_of(where_ref[k] * width, width), width)
        copies.append(pltpu.make_async_copy(buf.at[k], out_hbm.at[:, where], sems.at[k]))
        copies[k].start()
    for copy in copies:
        copy.wait()


def finish(inverse, sources, pieces, width, total, before=None):
    rank = inverse.shape[0]
    count = len(pieces)
    in_specs = [TABLE, WHOLE, *[WHOLE] * len(sources)]
    args = [jnp.stack([piece[0] for piece in pieces]), inverse, *sources]
    aliases = {}
    if before is not None:
        in_specs.append(HBM)
        args.append(before)
        aliases = {len(args) - 1: 0}
    return pl.pallas_call(
        functools.partial(finish_kernel, [piece[1:] for piece in pieces]),
        in_specs=in_specs,
        out_specs=HBM,
        out_shape=jax.ShapeDtypeStruct((rank, total), F32),
        scratch_shapes=[
            pltpu.VMEM((count, rank, width), F32),
            pltpu.SemaphoreType.DMA((count,)),
        ],
        input_output_aliases=aliases,
        compiler_params=PARAMS,
        cost_estimate=pl.CostEstimate(
            flops=6 * rank * rank * width * count,
            bytes_accessed=8 * rank * width * count,
            transcendentals=0,
        ),
        name="finish",
    )(*args)


def body(n_pos, n_pix, probes, sketch):
    def swap(value, axis, size, bit):
        return lax.ppermute(value, axis, [(i, i ^ bit) for i in range(size)])

    def over(value, bit):
        return swap(value, "pos", n_pos, bit)

    me = lax.axis_index("pos").astype(jnp.int32)
    near, far = me & 1, (me >> 1) & 1
    cols = probes.shape[1]
    width = cols // (8 * CHUNKS)

    tall = tall_partial(probes, sketch.T)
    bit = 1
    while 2 * bit < n_pix:
        tall = tall + swap(tall, "pix", n_pix, bit)
        bit *= 2
    other = swap(tall, "pix", n_pix, bit)

    def block_a(c, p, q):
        return 8 * c + 2 * (near ^ p) + (far ^ q)

    def block_b(c, p, q):
        return 8 * c + 4 + 2 * (far ^ p) + (near ^ q)

    def outputs(c, p):
        return [
            ([block_a(c, p, 1), block_a(c, p, 0)], c == 0),
            ([block_b(c, p, 1), block_b(c, p, 0)], False),
        ]

    both, gram, away = first_products(tall, other, probes, outputs(0, 1), width)

    inverse, after = None, away[0]
    sources, pieces = [], []
    for c in range(CHUNKS):
        g = LANES if c == 0 else 0
        last = c == CHUNKS - 1
        made = rest_products(
            both, gram, probes, outputs(c, 0) + ([] if last else outputs(c + 1, 1)), width, after
        )
        away_a, away_b = away
        (own_a, own_b), away = made[:2], made[2:]
        got_a = over(away_a, 1)
        sum_a = own_a + got_a
        sum_b = own_b + over(away_b, 2)
        after = got_a
        send_a, send_b = sum_a[:, : width + g], sum_b[:, :width]
        if c > 0:
            send_a, send_b, whole = lax.optimization_barrier((send_a, send_b, whole))
        got_a = over(send_a, 2)
        got_b = over(send_b, 1)
        whole = jnp.concatenate(
            [
                sum_a[:, width + g :] + got_a[:, :width],
                sum_a[:, width : width + g] + got_a[:, width:],
                sum_b[:, width:] + got_b,
            ],
            axis=1,
        )
        total = whole
        bit = 4
        while bit < n_pos:
            total = total + over(total, bit)
            bit *= 2
        if c == 0:
            inverse = inverse_factor(total, width)
        mine_a, mine_b = total[:, :width], total[:, width + g :]
        if c > 0:
            mine_a, mine_b, inverse = lax.optimization_barrier((mine_a, mine_b, inverse))
        next_a = over(mine_a, 2)
        next_b = over(mine_b, 1)
        last_a = over(jnp.concatenate([mine_a, next_a], axis=1), 1)
        last_b = over(jnp.concatenate([mine_b, next_b], axis=1), 2)
        k = len(sources)
        sources += [total, next_a, next_b, last_a, last_b]
        pieces += [
            (block_a(c, 0, 0), k, 0),
            (block_b(c, 0, 0), k, width + g),
            (block_a(c, 0, 1), k + 1, 0),
            (block_b(c, 0, 1), k + 2, 0),
            (block_a(c, 1, 0), k + 3, 0),
            (block_a(c, 1, 1), k + 3, width),
            (block_b(c, 1, 0), k + 4, 0),
            (block_b(c, 1, 1), k + 4, width),
        ]
    out = finish(inverse, sources[:-2], pieces[:-4], width, cols)
    pieces = [(where, source - k - 3, start) for where, source, start in pieces[-4:]]
    return finish(inverse, sources[-2:], pieces, width, cols, out)


def solution(mesh):
    in_specs = (P("pos", "pix"), P("pix", None))
    out_specs = P(None, "pix")
    run = functools.partial(body, mesh.shape["pos"], mesh.shape["pix"])
    return jax.shard_map(run, mesh=mesh, in_specs=in_specs, out_specs=out_specs, check_vma=False)
```

```python
import functools

import jax
import jax.numpy as jnp
from jax import lax
from jax.experimental import pallas as pl
from jax.experimental.pallas import tpu as pltpu
from jax.sharding import PartitionSpec as P

F32 = jnp.float32
BF16 = jnp.bfloat16
VMEM_LIMIT = 40 * 1024 * 1024
LANES = 128
CHUNKS = 2
AHEAD = 8
UNIT = 512
TILE = 256
PANEL = 4
LAST = (((1,), (1,)), ((), ()))
PLAIN = (((1,), (0,)), ((), ()))
ANYWHERE = pl.BlockSpec(memory_space=pl.ANY)
HBM = pl.BlockSpec(memory_space=pltpu.MemorySpace.HBM)
WHOLE = pl.BlockSpec(memory_space=pltpu.VMEM)
TABLE = pl.BlockSpec(memory_space=pltpu.SMEM)
PARAMS = pltpu.CompilerParams(vmem_limit_bytes=VMEM_LIMIT)


def split(x):
    head = x.astype(BF16)
    return head, (x - head.astype(F32)).astype(BF16)


def dot(a, b, dims):
    return lax.dot_general(a, b, dims, preferred_element_type=F32)


def tiles(size):
    step = min(TILE, size)
    return [slice(start, start + step) for start in range(0, size, step)]


def in_hbm(x):
    return pltpu.with_memory_space_constraint(x, pltpu.MemorySpace.HBM)


def stream(copies, use):
    for copy in copies[:AHEAD]:
        copy.start()
    for k, copy in enumerate(copies):
        copy.wait()
        if k + AHEAD < len(copies):
            copies[k + AHEAD].start()
        use(k)


def tall_kernel(x_hbm, s_hbm, out_ref, x_buf, s_buf, head_buf, rest_buf, x_sems, s_sems):
    blocks, _, unit = x_buf.shape
    rank = s_hbm.shape[0]

    def copies(k):
        where = pl.ds(k * unit, unit)
        return (
            pltpu.make_async_copy(s_hbm.at[:, where], s_buf.at[k], s_sems.at[k]),
            pltpu.make_async_copy(x_hbm.at[:, where], x_buf.at[k], x_sems.at[k]),
        )

    for k in range(blocks):
        for copy in copies(k):
            copy.start()
    for k in range(blocks):
        for copy in copies(k):
            copy.wait()
        s_head, s_rest = split(s_buf[k])
        s_both = jnp.concatenate([s_head, s_rest], axis=0)
        x_head, x_rest = split(x_buf[k])
        head_buf[k] = x_head
        rest_buf[k] = x_rest
        both = dot(s_both, x_head, LAST)
        part = both[:rank] + (both[rank:] + dot(s_head, x_rest, LAST))
        if k == 0:
            out_ref[...] = part
        else:
            out_ref[...] += part


def tall_partial(probes, sketch_t):
    rows, cols = probes.shape
    rank = sketch_t.shape[0]
    unit = min(UNIT, cols)
    blocks = cols // unit
    return pl.pallas_call(
        tall_kernel,
        in_specs=[HBM, HBM],
        out_specs=WHOLE,
        out_shape=jax.ShapeDtypeStruct((rank, rows), F32),
        scratch_shapes=[
            pltpu.VMEM((blocks, rows, unit), F32),
            pltpu.VMEM((blocks, rank, unit), F32),
            pltpu.VMEM((blocks, rows, unit), BF16),
            pltpu.VMEM((blocks, rows, unit), BF16),
            pltpu.SemaphoreType.DMA((blocks,)),
            pltpu.SemaphoreType.DMA((blocks,)),
        ],
        compiler_params=PARAMS,
        cost_estimate=pl.CostEstimate(
            flops=6 * rows * cols * rank, bytes_accessed=4 * rows * cols, transcendentals=0
        ),
        name="tall_partial",
    )(in_hbm(probes), in_hbm(sketch_t))


def multiply_blocks(both_ref, which_ref, x_hbm, x_buf, sems, plan, outs):
    rank = outs[0].shape[0]
    unit = x_buf.shape[2]
    copies = [
        pltpu.make_async_copy(
            x_hbm.at[:, pl.ds(pl.multiple_of(which_ref[k] * unit, unit), unit)],
            x_buf.at[k],
            sems.at[k],
        )
        for k in range(len(plan))
    ]

    def use(k):
        out, offset = plan[k]
        for cols in tiles(unit):
            total = None
            for rows in tiles(x_buf.shape[1]):
                x_head, x_rest = split(x_buf[k, rows, cols])
                both = dot(both_ref[:, rows], x_head, PLAIN)
                part = both[:rank] + (both[rank:] + dot(both_ref[:rank, rows], x_rest, PLAIN))
                total = part if total is None else total + part
            outs[out][:, offset + cols.start : offset + cols.stop] = total

    return copies, use


def first_kernel(plan, grams, which_ref, one_ref, two_ref, x_hbm, both_ref, gram_ref, *refs):
    outs, (x_buf, sems) = refs[:-2], refs[-2:]
    copies, use = multiply_blocks(both_ref, which_ref, x_hbm, x_buf, sems, plan, outs)

    def use_first(k):
        if k == 0:
            tall = one_ref[...] + two_ref[...]
            head, rest = split(tall)
            both_ref[...] = jnp.concatenate([head, rest], axis=0)
        use(k)

    stream(copies, use_first)
    tall = one_ref[...] + two_ref[...]
    r = tall.shape[0]
    head, rest = split(tall)
    tail = (tall - head.astype(F32) - rest.astype(F32)).astype(BF16)
    three = jnp.concatenate([head, rest, tail], axis=0)
    g = dot(three, three, LAST)
    cross = g[:r, r : 2 * r] + g[r : 2 * r, :r]
    small = g[:r, 2 * r :] + g[2 * r :, :r] + g[r : 2 * r, r : 2 * r]
    gram = g[:r, :r] + (cross + small)
    gram_ref[...] = jnp.concatenate([gram, jnp.zeros((r, LANES - r), F32)], axis=1)
    for out, offset in grams:
        outs[out][:, offset : offset + LANES] = gram_ref[...]


def rest_kernel(plan, grams, which_ref, both_ref, gram_ref, x_hbm, after_ref, *refs):
    outs, (x_buf, sems) = refs[:-2], refs[-2:]
    copies, use = multiply_blocks(both_ref, which_ref, x_hbm, x_buf, sems, plan, outs)
    stream(copies, use)
    for out, offset in grams:
        outs[out][:, offset : offset + LANES] = gram_ref[...]


def layout(outputs, sub):
    unit = min(UNIT, sub)
    plan, grams, widths, which = [], [], [], []
    for out, (blocks, with_gram) in enumerate(outputs):
        extra = LANES if with_gram else 0
        for j, block in enumerate(blocks):
            for part in range(sub // unit):
                plan.append((out, j * sub + part * unit + (extra if j else 0)))
                which.append(block * (sub // unit) + part)
        if with_gram:
            grams.append((out, sub))
        widths.append(len(blocks) * sub + extra)
    return unit, plan, grams, widths, jnp.stack(which)


def products(kernel, inputs, in_specs, made, probes, outputs, sub, name):
    rows = probes.shape[0]
    rank = inputs[1].shape[0]
    unit, plan, grams, widths, which = layout(outputs, sub)
    shapes = [*made, *[jax.ShapeDtypeStruct((rank, width), F32) for width in widths]]
    return pl.pallas_call(
        functools.partial(kernel, plan, grams),
        in_specs=[TABLE, *in_specs],
        out_specs=[WHOLE] * len(shapes),
        out_shape=shapes,
        scratch_shapes=[
            pltpu.VMEM((len(plan), rows, unit), F32),
            pltpu.SemaphoreType.DMA((len(plan),)),
        ],
        compiler_params=PARAMS,
        cost_estimate=pl.CostEstimate(
            flops=6 * rows * rank * unit * len(plan),
            bytes_accessed=4 * rows * unit * len(plan),
            transcendentals=0,
        ),
        name=name,
    )(which, *inputs)


def first_products(one, two, probes, outputs, sub):
    rank, rows = one.shape
    made = [
        jax.ShapeDtypeStruct((2 * rank, rows), BF16),
        jax.ShapeDtypeStruct((rank, LANES), F32),
    ]
    both, gram, *outs = products(
        first_kernel,
        [one, two, in_hbm(probes)],
        [WHOLE, WHOLE, HBM],
        made,
        probes,
        outputs,
        sub,
        "first_products",
    )
    return both, gram, outs


def rest_products(both, gram, probes, outputs, sub, after):
    return products(
        rest_kernel,
        [both, gram, in_hbm(probes), after],
        [WHOLE, WHOLE, HBM, ANYWHERE],
        [],
        probes,
        outputs,
        sub,
        "rest_products",
    )


def inverse_kernel(gram_ref, out_ref):
    rank = out_ref.shape[0]
    rows = lax.broadcasted_iota(jnp.int32, (rank, LANES), 0)
    cols = lax.broadcasted_iota(jnp.int32, (rank, LANES), 1)
    work = jnp.where(cols < rank, gram_ref[...], (cols == rows + rank).astype(F32))
    scale = jnp.ones((rank, LANES), F32)
    for start in range(0, rank, PANEL):
        panel = [
            jnp.broadcast_to(work[:, k : k + 1], (rank, LANES))
            for k in range(start, start + PANEL)
        ]
        for j in range(PANEL):
            k = start + j
            over = 1.0 / panel[j][k : k + 1, :]
            scale = jnp.where(rows == k, over, scale)
            factor = jnp.where(rows > k, panel[j] * over, 0.0)
            work = work - factor * work[k : k + 1, :]
            for later in range(j + 1, PANEL):
                panel[later] = panel[later] - factor * panel[later][k : k + 1, :]
    out_ref[...] = (work * jnp.sqrt(scale))[:, rank : 2 * rank]


def inverse_factor(chunk, start):
    rank = chunk.shape[0]
    return pl.pallas_call(
        inverse_kernel,
        grid=(1,),
        in_specs=[pl.BlockSpec((rank, LANES), lambda i: (0, start // LANES))],
        out_specs=pl.BlockSpec((rank, rank), lambda i: (0, 0)),
        out_shape=jax.ShapeDtypeStruct((rank, rank), F32),
        compiler_params=PARAMS,
        cost_estimate=pl.CostEstimate(
            flops=20_000_000, bytes_accessed=8 * rank * LANES, transcendentals=rank
        ),
        name="inverse_factor",
    )(chunk)


def finish_kernel(plan, where_ref, inverse_ref, *refs):
    out_hbm, buf, sems = refs[-3:]
    _, rank, width = buf.shape
    head, rest = split(inverse_ref[...])
    both = jnp.concatenate([head, rest], axis=0)
    copies = []
    for k, (source, offset) in enumerate(plan):
        p_head, p_rest = split(refs[source][:, offset : offset + width])
        first = dot(both, p_head, PLAIN)
        buf[k] = first[:rank] + (first[rank:] + dot(head, p_rest, PLAIN))
        where = pl.ds(pl.multiple_of(where_ref[k] * width, width), width)
        copies.append(pltpu.make_async_copy(buf.at[k], out_hbm.at[:, where], sems.at[k]))
        copies[k].start()
    for copy in copies:
        copy.wait()


def finish(inverse, sources, pieces, width, total, before=None):
    rank = inverse.shape[0]
    count = len(pieces)
    in_specs = [TABLE, WHOLE, *[WHOLE] * len(sources)]
    args = [jnp.stack([piece[0] for piece in pieces]), inverse, *sources]
    aliases = {}
    if before is not None:
        in_specs.append(HBM)
        args.append(before)
        aliases = {len(args) - 1: 0}
    return pl.pallas_call(
        functools.partial(finish_kernel, [piece[1:] for piece in pieces]),
        in_specs=in_specs,
        out_specs=HBM,
        out_shape=jax.ShapeDtypeStruct((rank, total), F32),
        scratch_shapes=[
            pltpu.VMEM((count, rank, width), F32),
            pltpu.SemaphoreType.DMA((count,)),
        ],
        input_output_aliases=aliases,
        compiler_params=PARAMS,
        cost_estimate=pl.CostEstimate(
            flops=6 * rank * rank * width * count,
            bytes_accessed=8 * rank * width * count,
            transcendentals=0,
        ),
        name="finish",
    )(*args)


def body(n_pos, n_pix, probes, sketch):
    def swap(value, axis, size, bit):
        return lax.ppermute(value, axis, [(i, i ^ bit) for i in range(size)])

    def over(value, bit):
        return swap(value, "pos", n_pos, bit)

    me = lax.axis_index("pos").astype(jnp.int32)
    near, far = me & 1, (me >> 1) & 1
    cols = probes.shape[1]
    width = cols // (8 * CHUNKS)

    tall = tall_partial(probes, sketch.T)
    bit = 1
    while 2 * bit < n_pix:
        tall = tall + swap(tall, "pix", n_pix, bit)
        bit *= 2
    other = swap(tall, "pix", n_pix, bit)

    def block_a(c, p, q):
        return 8 * c + 2 * (near ^ p) + (far ^ q)

    def block_b(c, p, q):
        return 8 * c + 4 + 2 * (far ^ p) + (near ^ q)

    def outputs(c, p):
        return [
            ([block_a(c, p, 1), block_a(c, p, 0)], c == 0),
            ([block_b(c, p, 1), block_b(c, p, 0)], False),
        ]

    both, gram, away = first_products(tall, other, probes, outputs(0, 1), width)

    inverse, after = None, away[0]
    sources, pieces = [], []
    for c in range(CHUNKS):
        g = LANES if c == 0 else 0
        last = c == CHUNKS - 1
        made = rest_products(
            both, gram, probes, outputs(c, 0) + ([] if last else outputs(c + 1, 1)), width, after
        )
        away_a, away_b = away
        (own_a, own_b), away = made[:2], made[2:]
        got_a = over(away_a, 1)
        sum_a = own_a + got_a
        sum_b = own_b + over(away_b, 2)
        after = got_a
        send_a, send_b = sum_a[:, : width + g], sum_b[:, :width]
        if c > 0:
            send_a, send_b, whole = lax.optimization_barrier((send_a, send_b, whole))
        got_a = over(send_a, 2)
        got_b = over(send_b, 1)
        whole = jnp.concatenate(
            [
                sum_a[:, width + g :] + got_a[:, :width],
                sum_a[:, width : width + g] + got_a[:, width:],
                sum_b[:, width:] + got_b,
            ],
            axis=1,
        )
        total = whole
        bit = 4
        while bit < n_pos:
            total = total + over(total, bit)
            bit *= 2
        if c == 0:
            inverse = inverse_factor(total, width)
        mine_a, mine_b = total[:, :width], total[:, width + g :]
        if c > 0:
            mine_a, mine_b, inverse = lax.optimization_barrier((mine_a, mine_b, inverse))
        next_a = over(mine_a, 2)
        next_b = over(mine_b, 1)
        last_a = over(jnp.concatenate([mine_a, next_a], axis=1), 1)
        last_b = over(jnp.concatenate([mine_b, next_b], axis=1), 2)
        k = len(sources)
        sources += [total, next_a, next_b, last_a, last_b]
        pieces += [
            (block_a(c, 0, 0), k, 0),
            (block_b(c, 0, 0), k, width + g),
            (block_a(c, 0, 1), k + 1, 0),
            (block_b(c, 0, 1), k + 2, 0),
            (block_a(c, 1, 0), k + 3, 0),
            (block_a(c, 1, 1), k + 3, width),
            (block_b(c, 1, 0), k + 4, 0),
            (block_b(c, 1, 1), k + 4, width),
        ]
    out = finish(inverse, sources[:-2], pieces[:-4], width, cols)
    pieces = [(where, source - k - 3, start) for where, source, start in pieces[-4:]]
    return finish(inverse, sources[-2:], pieces, width, cols, out)


def solution(mesh):
    in_specs = (P("pos", "pix"), P("pix", None))
    out_specs = P(None, "pix")
    run = functools.partial(body, mesh.shape["pos"], mesh.shape["pix"])
    return jax.shard_map(run, mesh=mesh, in_specs=in_specs, out_specs=out_specs, check_vma=False)
```
